32 devices in a mesh: row: 8 (over y, x, core), col: 4 (over z).
Axes of the slice: x: 2, y: 2, z: 4, core: 2. Of those that a mesh axis runs over, the one named last changes fastest.
Arguments:
- homolog_activations: bfloat16 [128, 352, 256], P('row', 'col'), may hold values from -8 to 8
- coupling_activations: bfloat16 [352, 352, 128], P('row', 'col'), may hold values from -6 to 6
- homolog_existence_marks: int32 [128, 352], P('row', 'col'), may hold values from 0 to 1, as said below
- observed_peptide_marks: int32 [352], replicated, may hold values 0 or 1
- peptide_ordinals: int32 [352], replicated, may hold values from 1 to 1056, as said below
- strand_membership: int32 [352], replicated, may hold values from 0 to 7, never falling along the last dimension, each value on 1 to 88 neighbouring positions
- distance_ordinal_vectors: bfloat16 [66, 128], replicated, may hold values from -6 to 6
- coupling_score_mapping: bfloat16 [128, 8], replicated, may hold values from -0.5 to 0.5
- question_mapping_weights: bfloat16 [256, 256], replicated, may hold values from -4 to 4
- address_payload_mapping: bfloat16 [256, 512], replicated, may hold values from -4 to 4
- logistic_valve_mapping: bfloat16 [256, 256], replicated, may hold values from -0.375 to 0.375
- mixture_exit_mapping: bfloat16 [256, 256], replicated, may hold values from -0.375 to 0.375
- twofold_covariance_mapping: bfloat16 [256, 64], replicated, may hold values from -0.375 to 0.375
- covariance_exit_mapping: bfloat16 [1024, 128], replicated, may hold values from -0.1875 to 0.1875
- triad_opening_mappings: bfloat16 [128, 512], replicated, may hold values from -0.5 to 0.5
- triad_valve_mapping: bfloat16 [128, 128], replicated, may hold values from -0.5 to 0.5
- triad_exit_mapping: bfloat16 [128, 128], replicated, may hold values from -0.5 to 0.5
Outputs:
- homologs_after: bfloat16 [128, 352, 256], P('row', 'col')
- couplings_after: bfloat16 [352, 352, 128], P('row', 'col')
The draws below stay inside these ranges and needn't reach their ends.
Inputs may be any that keep to these rules, and one draw needn't show every extreme that they name: Row 0 and column 0 of homolog_existence_marks are all ones. `peptide_ordinals`: strictly increasing along the residues.
All inputs are finite; a program needn't handle non-finite values.
Results may differ from the reference program's by a relative error of at most 0.008.
Values may be sent and summed in bfloat16 or wider, within the bound.
No kernel may reach another device: no remote copies, remote signals or barrier semaphores. Data moves between devices by JAX's collectives and lax.ppermute only.
A program may use at most 192 MiB of HBM per device.

```python
import math
import jax
import jax.numpy as jnp
import numpy as np
from jax import lax

ALIGNMENT_WIDTH = 256
PAIR_W = 128
ATTENTION_HEADS = 8
HEAD_CHANNELS = 32
OUTER_CHANNELS = 32
TRI_W = 128
REL_MAX = 32
RT = 44
SEQUENCE_COUNT = 128
RESIDUE_COUNT = 352
N_ROW = 8


def attention_tables(key):
    random_base_key = jax.random.fold_in(key, 202)
    matrix_shape = (ALIGNMENT_WIDTH, ATTENTION_HEADS, HEAD_CHANNELS)
    query_base = jax.random.normal(jax.random.fold_in(random_base_key, 1), matrix_shape, jnp.float32)
    key_extra = jax.random.normal(jax.random.fold_in(random_base_key, 2), matrix_shape, jnp.float32)
    value_base = jax.random.normal(jax.random.fold_in(random_base_key, 3), matrix_shape, jnp.float32)
    query_matrix = query_base
    key_matrix = key_extra
    scale_for_norm = 1.0 / math.sqrt(ALIGNMENT_WIDTH)
    return (query_matrix * scale_for_norm, key_matrix * scale_for_norm, value_base * scale_for_norm)


def draw_question_mapping_weights(key, part):
    query_matrix, key_matrix, value_matrix = attention_tables(key)
    return jnp.clip(query_matrix.reshape(ALIGNMENT_WIDTH, ATTENTION_HEADS * HEAD_CHANNELS), -4.0, 4.0).astype(jnp.bfloat16)


def draw_address_payload_mapping(key, part):
    query_matrix, key_matrix, value_matrix = attention_tables(key)
    joined_parts = jnp.concatenate([key_matrix.reshape(ALIGNMENT_WIDTH, ATTENTION_HEADS * HEAD_CHANNELS), value_matrix.reshape(ALIGNMENT_WIDTH, ATTENTION_HEADS * HEAD_CHANNELS)], axis=1)
    return jnp.clip(joined_parts, -4.0, 4.0).astype(jnp.bfloat16)


def draw_homolog_activations(key, part):
    random_base_key = jax.random.fold_in(key, 101)
    shared_values = jax.random.normal(jax.random.fold_in(random_base_key, 1), (RESIDUE_COUNT, ALIGNMENT_WIDTH), jnp.float32)
    random_offsets = jax.random.normal(jax.random.fold_in(random_base_key, 2), (SEQUENCE_COUNT, RESIDUE_COUNT, ALIGNMENT_WIDTH), jnp.float32)
    field = 0.7 * shared_values[None] + 0.7 * random_offsets
    return jnp.clip(field, -8.0, 8.0).astype(jnp.bfloat16)


def draw_homolog_existence_marks(key, part):
    rolls = jax.random.randint(jax.random.fold_in(key, 303), (SEQUENCE_COUNT, RESIDUE_COUNT), 0, 10 * SEQUENCE_COUNT)
    limit = 3 * SEQUENCE_COUNT + 6 * jnp.arange(SEQUENCE_COUNT, dtype=jnp.int32)[:, None]
    presence = (rolls < limit).astype(jnp.int32)
    presence = presence.at[0, :].set(1)
    presence = presence.at[:, 0].set(1)
    return presence


def draw_peptide_ordinals(key, part):
    gaps = jax.random.randint(jax.random.fold_in(key, 404), (RESIDUE_COUNT,), 1, 4)
    gaps = gaps.at[0].set(1)
    numbers = jnp.cumsum(gaps).astype(jnp.int32)
    numbers = numbers.at[RESIDUE_COUNT - 1].set(3 * RESIDUE_COUNT)
    return numbers.astype(jnp.int32)


def touch_ends(values, own_key, least, high):
    dims = values.shape
    place = [jax.random.randint(jax.random.fold_in(own_key, axis), (), 0, dims[axis]) for axis in range(len(dims))]
    values = values.at[tuple(place)].set(least)
    longest = dims.index(max(dims))
    place[longest] = (place[longest] + 1) % dims[longest]
    return values.at[tuple(place)].set(high)


def block_levels(key, dims, split, low, top_value):
    def one(dim, blocks):
        draws = jax.random.uniform(jax.random.fold_in(jax.random.fold_in(key, 6), dim), (blocks,), jnp.float32, low / len(split), top_value / len(split))
        return jnp.repeat(jnp.exp(draws), dims[dim] // blocks).reshape((-1,) + (1,) * (len(dims) - dim - 1))

    gain = one(*split[0])
    for cut in split[1:]:
        gain = gain * one(*cut)
    return gain


def length_profile(amount, total, bound, skew):
    weights = [(1 << 20) // math.isqrt(standing ** skew) + 1 for standing in range(2, amount + 1)]
    spare, given = total - bound - (amount - 1), [1] * (amount - 1)
    while spare > 0:
        movable = [i for i in range(amount - 1) if given[i] < bound]
        whole, budget = sum([weights[i] for i in movable]), spare
        for i in movable:
            extra = min(bound - given[i], max(1, budget * weights[i] // whole), spare)
            given[i] = given[i] + extra
            spare = spare - extra
    return np.array([bound] + given)


def uneven_parts(key, number_of, total, most, skew):
    if number_of == 2:
        one = jax.random.randint(key, (), max(1, total - most), min(most, total - 1) + 1)
        return jnp.stack([one, total - one])
    sizes = jnp.asarray(length_profile(number_of, total, most, skew), jnp.int32)
    twos = (number_of - 1) // 2
    source_of, receiver = sizes[1:1 + 2 * twos:2], sizes[2:2 + 2 * twos:2]
    room = jnp.minimum(source_of - 1, most - receiver)
    passed = jax.random.randint(jax.random.fold_in(key, 1), (twos,), 0, 1 << 20) % (room + 1)
    sizes = sizes.at[1:1 + 2 * twos:2].set(source_of - passed).at[2:2 + 2 * twos:2].set(receiver + passed)
    return sizes[jax.random.permutation(jax.random.fold_in(key, 2), number_of)]


def bell_draw(stream_key, extent, width, most, split=(), kind=jnp.bfloat16):
    gain = block_levels(stream_key, extent, split, -0.22, 0.18) if split else 1.0
    drawn = jax.random.normal(stream_key, extent, jnp.float32) * width * gain
    return jnp.minimum(jnp.maximum(drawn, -most), most).astype(kind)


def setup_inputs(seed: int = 0) -> dict:
    key_of = jax.random.split(jax.random.key(seed), 18)
    homolog_activations = draw_homolog_activations(jax.random.fold_in(key_of[17], 71), 0)
    coupling_activations = bell_draw(key_of[1], (RESIDUE_COUNT, RESIDUE_COUNT, PAIR_W), 1.0, 6.0, ((0, 8), (1, 4)))
    homolog_existence_marks = draw_homolog_existence_marks(jax.random.fold_in(key_of[17], 71), 0)
    observed_peptide_marks = touch_ends((jax.random.randint(key_of[3], (RESIDUE_COUNT,), 0, 4) < 3).astype(jnp.int32), jax.random.fold_in(key_of[3], 1), 0, 1)
    peptide_ordinals = draw_peptide_ordinals(jax.random.fold_in(key_of[17], 71), 0)
    strand_membership = jnp.searchsorted(jnp.cumsum(uneven_parts(key_of[5], 8, RESIDUE_COUNT, RESIDUE_COUNT // 4, 0)), jnp.arange(RESIDUE_COUNT), side="right").astype(jnp.int32)
    distance_ordinal_vectors = bell_draw(key_of[6], (2 * REL_MAX + 2, PAIR_W), 1.0, 6.0)
    coupling_score_mapping = bell_draw(key_of[7], (PAIR_W, ATTENTION_HEADS), PAIR_W ** -0.5, 0.5)
    question_mapping_weights = draw_question_mapping_weights(jax.random.fold_in(key_of[17], 71), 0)
    address_payload_mapping = draw_address_payload_mapping(jax.random.fold_in(key_of[17], 71), 0)
    logistic_valve_mapping = bell_draw(key_of[10], (ALIGNMENT_WIDTH, ATTENTION_HEADS * HEAD_CHANNELS), ALIGNMENT_WIDTH ** -0.5, 0.375)
    mixture_exit_mapping = bell_draw(key_of[11], (ATTENTION_HEADS * HEAD_CHANNELS, ALIGNMENT_WIDTH), (ATTENTION_HEADS * HEAD_CHANNELS) ** -0.5, 0.375)
    twofold_covariance_mapping = bell_draw(key_of[12], (ALIGNMENT_WIDTH, 2 * OUTER_CHANNELS), ALIGNMENT_WIDTH ** -0.5, 0.375)
    covariance_exit_mapping = bell_draw(key_of[13], (OUTER_CHANNELS * OUTER_CHANNELS, PAIR_W), (OUTER_CHANNELS * OUTER_CHANNELS) ** -0.5, 0.1875)
    triad_opening_mappings = bell_draw(key_of[14], (PAIR_W, 4 * TRI_W), PAIR_W ** -0.5, 0.5)
    triad_valve_mapping = bell_draw(key_of[15], (PAIR_W, PAIR_W), PAIR_W ** -0.5, 0.5)
    triad_exit_mapping = bell_draw(key_of[16], (TRI_W, PAIR_W), TRI_W ** -0.5, 0.5)
    return dict(homolog_activations=homolog_activations, coupling_activations=coupling_activations, homolog_existence_marks=homolog_existence_marks, observed_peptide_marks=observed_peptide_marks, peptide_ordinals=peptide_ordinals, strand_membership=strand_membership, distance_ordinal_vectors=distance_ordinal_vectors, coupling_score_mapping=coupling_score_mapping, question_mapping_weights=question_mapping_weights, address_payload_mapping=address_payload_mapping, logistic_valve_mapping=logistic_valve_mapping, mixture_exit_mapping=mixture_exit_mapping, twofold_covariance_mapping=twofold_covariance_mapping, covariance_exit_mapping=covariance_exit_mapping, triad_opening_mappings=triad_opening_mappings, triad_valve_mapping=triad_valve_mapping, triad_exit_mapping=triad_exit_mapping)


norm_eps = 1e-05
count_eps = 0.001
masked_score = -1000000000.0

def zscore_transform(inputs):
    inputs = inputs.astype(jnp.float32)
    centred = inputs - lax.optimization_barrier(jnp.mean(inputs, axis=-1, keepdims=True))
    spread = lax.optimization_barrier(jnp.mean(centred * centred, axis=-1, keepdims=True))
    return centred * lax.rsqrt(spread + norm_eps)

def regrouped_covariance(operand, weights):
    batch_shape = operand.shape[:-1]
    result = jnp.dot(operand.reshape(-1, operand.shape[-1]), weights, preferred_element_type=jnp.float32)
    return result.reshape(batch_shape + (weights.shape[-1],))

def quantized_numbers(tensor):
    return lax.optimization_barrier(tensor.astype(jnp.bfloat16)).astype(jnp.float32)

def position_bins(index_rows, index_cols, chain_rows, chain_cols):
    offset = jnp.clip(index_rows[:, None] - index_cols[None, :] + REL_MAX, 0, 2 * REL_MAX)
    return jnp.where(chain_rows[:, None] == chain_cols[None, :], offset, 2 * REL_MAX + 1).astype(jnp.int32)

def reference(homolog_activations, coupling_activations, homolog_existence_marks, observed_peptide_marks, peptide_ordinals, strand_membership, distance_ordinal_vectors, coupling_score_mapping, question_mapping_weights, address_payload_mapping, logistic_valve_mapping, mixture_exit_mapping, twofold_covariance_mapping, covariance_exit_mapping, triad_opening_mappings, triad_valve_mapping, triad_exit_mapping):
    similarity_breadth = ATTENTION_HEADS * HEAD_CHANNELS
    zscored_homologs = zscore_transform(homolog_activations).astype(jnp.bfloat16)
    existing_homolog_marks = homolog_existence_marks.astype(jnp.float32)
    covariance_source = quantized_numbers(regrouped_covariance(zscored_homologs, twofold_covariance_mapping) * existing_homolog_marks[:, :, None])
    left_all = covariance_source[:, :, :OUTER_CHANNELS]
    right_all = covariance_source[:, :, OUTER_CHANNELS:]
    counts = jnp.dot(existing_homolog_marks.T, existing_homolog_marks, precision=lax.Precision.HIGHEST)

    def opm_block(block_start):
        row_block = lax.dynamic_slice_in_dim(left_all, block_start, RT, 1)
        outer_prod = quantized_numbers(jnp.einsum('sic,sje->ijce', row_block, right_all))
        mixed_opm = jnp.dot(outer_prod.reshape(RT * RESIDUE_COUNT, OUTER_CHANNELS * OUTER_CHANNELS), covariance_exit_mapping.astype(jnp.float32))
        mixed_opm = mixed_opm.reshape(RT, RESIDUE_COUNT, PAIR_W)
        number = lax.dynamic_slice_in_dim(counts, block_start, RT, 0)
        return mixed_opm / (count_eps + number[:, :, None])
    starts = jnp.arange(N_ROW, dtype=jnp.int32) * RT
    outer_update = lax.map(opm_block, starts).reshape(RESIDUE_COUNT, RESIDUE_COUNT, PAIR_W)
    bucket = position_bins(peptide_ordinals, peptide_ordinals, strand_membership, strand_membership)
    z_one = coupling_activations.astype(jnp.float32) + distance_ordinal_vectors.astype(jnp.float32)[bucket] + outer_update
    ln_pair = zscore_transform(z_one)
    pair_bias = jnp.einsum('ijc,ch->hij', ln_pair, coupling_score_mapping.astype(jnp.float32), precision=lax.Precision.HIGHEST)
    bias_full = quantized_numbers(pair_bias)
    score_scale = 1.0 / math.sqrt(HEAD_CHANNELS)

    def homolog_softmax_mixing(row_inputs):
        normed, existing_lookup_marks = row_inputs
        queries = quantized_numbers(regrouped_covariance(normed, question_mapping_weights)).reshape(RESIDUE_COUNT, ATTENTION_HEADS, HEAD_CHANNELS)
        key_vals = quantized_numbers(regrouped_covariance(normed, address_payload_mapping))
        key_part = key_vals[:, :similarity_breadth].reshape(RESIDUE_COUNT, ATTENTION_HEADS, HEAD_CHANNELS)
        value_part = key_vals[:, similarity_breadth:].reshape(RESIDUE_COUNT, ATTENTION_HEADS, HEAD_CHANNELS)
        gate_activation = jax.nn.sigmoid(regrouped_covariance(normed, logistic_valve_mapping))
        scores = jnp.einsum('ihd,jhd->hij', queries, key_part) * score_scale + bias_full
        scores = jnp.where(existing_lookup_marks[None, None, :] > 0, scores, masked_score)
        maximal_precision = lax.optimization_barrier(jnp.max(scores, axis=-1, keepdims=True))
        exp_terms = jnp.exp(scores - maximal_precision)
        coefficient_accumulation = lax.optimization_barrier(jnp.sum(exp_terms, axis=-1))
        prob_terms = quantized_numbers(exp_terms)
        softmax_mixture = jnp.einsum('hij,jhd->ihd', prob_terms, value_part) / coefficient_accumulation.T[:, :, None]
        filtered_attended_result = (gate_activation * softmax_mixture.reshape(RESIDUE_COUNT, similarity_breadth)).astype(jnp.bfloat16)
        return jnp.dot(filtered_attended_result, mixture_exit_mapping, preferred_element_type=jnp.float32)
    additive_change = lax.map(homolog_softmax_mixing, (zscored_homologs, existing_homolog_marks))
    homologs_after = (homolog_activations.astype(jnp.float32) + additive_change).astype(jnp.bfloat16)
    ln_tri = ln_pair.astype(jnp.bfloat16)
    pair_live = (observed_peptide_marks[:, None] * observed_peptide_marks[None, :]).astype(jnp.float32)[:, :, None]
    side_left = regrouped_covariance(ln_tri, triad_opening_mappings[:, :2 * TRI_W])
    tri_left = quantized_numbers(jax.nn.sigmoid(side_left[:, :, TRI_W:]) * side_left[:, :, :TRI_W] * pair_live)
    side_right = regrouped_covariance(ln_tri, triad_opening_mappings[:, 2 * TRI_W:])
    tri_right = quantized_numbers(jax.nn.sigmoid(side_right[:, :, TRI_W:]) * side_right[:, :, :TRI_W] * pair_live)
    crossed = jnp.einsum('ikc,jkc->ijc', tri_left, tri_right)
    normed_cross = zscore_transform(crossed).astype(jnp.bfloat16)
    tri_proj = regrouped_covariance(normed_cross, triad_exit_mapping)
    tri_gate = jax.nn.sigmoid(regrouped_covariance(ln_tri, triad_valve_mapping))
    couplings_after = (z_one + tri_gate * tri_proj).astype(jnp.bfloat16)
    return (homologs_after, couplings_after)
```

```python
import math

import jax
import jax.numpy as jnp
from jax import lax
from jax.sharding import PartitionSpec as P

REL_MAX = 32


norm_eps = 1e-05
count_eps = 0.001
masked_score = -1000000000.0


def swap(pieces, axis):
    total = len(pieces)
    return [pieces[0]] + [
        lax.ppermute(pieces[k], axis, [(i, i ^ k) for i in range(total)]) for k in range(1, total)
    ]


def collect(block, axis):
    return swap([block] * lax.axis_size(axis), axis)


def exchange(pieces, axis):
    me = lax.axis_index(axis)
    total = lax.axis_size(axis)
    return swap(
        [lax.dynamic_index_in_dim(pieces, me ^ k, 0, keepdims=False) for k in range(total)], axis
    )


def in_order(slots, axis):
    me = lax.axis_index(axis)
    stacked = jnp.stack(slots)
    return jnp.stack(
        [
            lax.dynamic_index_in_dim(stacked, me ^ k, 0, keepdims=False)
            for k in range(len(slots))
        ]
    )


def zscore_transform(inputs):
    inputs = inputs.astype(jnp.float32)
    centred = inputs - jnp.mean(inputs, axis=-1, keepdims=True)
    spread = jnp.mean(centred * centred, axis=-1, keepdims=True)
    return centred * lax.rsqrt(spread + norm_eps)


def regrouped_covariance(operand, weights):
    batch_shape = operand.shape[:-1]
    result = jnp.dot(
        operand.reshape(-1, operand.shape[-1]), weights, preferred_element_type=jnp.float32
    )
    return result.reshape(batch_shape + (weights.shape[-1],))


def position_bins(index_rows, index_cols, chain_rows, chain_cols):
    offset = jnp.clip(index_rows[:, None] - index_cols[None, :] + REL_MAX, 0, 2 * REL_MAX)
    return jnp.where(chain_rows[:, None] == chain_cols[None, :], offset, 2 * REL_MAX + 1)


def shards(
    homolog_activations,
    coupling_activations,
    homolog_existence_marks,
    observed_peptide_marks,
    peptide_ordinals,
    strand_membership,
    distance_ordinal_vectors,
    coupling_score_mapping,
    question_mapping_weights,
    address_payload_mapping,
    logistic_valve_mapping,
    mixture_exit_mapping,
    twofold_covariance_mapping,
    covariance_exit_mapping,
    triad_opening_mappings,
    triad_valve_mapping,
    triad_exit_mapping,
):
    row_total = lax.axis_size("row")
    col_total = lax.axis_size("col")
    group_ratio = row_total // col_total
    devices = row_total * col_total
    row_place = lax.axis_index("row")
    col_place = lax.axis_index("col")
    tile_rows = coupling_activations.shape[0]
    block_columns = coupling_activations.shape[1]
    number_of_homologs = homolog_activations.shape[0]
    residues = row_total * tile_rows
    heads = coupling_score_mapping.shape[1]
    breadth = question_mapping_weights.shape[1]
    head_breadth = breadth // heads
    opm = twofold_covariance_mapping.shape[1] // 2
    tri_width = triad_exit_mapping.shape[0]
    pair_width = coupling_activations.shape[2]
    own_seqs = number_of_homologs // col_total
    share = tri_width // devices
    row_first = row_place * tile_rows
    col_first = col_place * block_columns
    bf16 = jnp.bfloat16

    zscored = zscore_transform(homolog_activations).astype(bf16)
    marks = homolog_existence_marks.astype(jnp.float32)
    source = (regrouped_covariance(zscored, twofold_covariance_mapping) * marks[:, :, None]).astype(bf16)
    flat_left = source[:, :, :opm].reshape(number_of_homologs, block_columns * opm)
    left_payload = jnp.concatenate([flat_left, marks.astype(bf16)], axis=1)
    left_all = in_order(collect(left_payload, "col"), "col")
    left_all, mark_all = left_all[:, :, : block_columns * opm], left_all[:, :, block_columns * opm :]
    left_all = left_all.reshape(col_total, number_of_homologs, group_ratio, tile_rows * opm)
    mark_all = mark_all.reshape(col_total, number_of_homologs, group_ratio, tile_rows)
    left_all = jnp.swapaxes(jnp.concatenate([left_all, mark_all], axis=3), 1, 2)
    left_all = left_all.reshape(row_total, number_of_homologs, tile_rows * (opm + 1))
    right = jnp.swapaxes(source[:, :, opm:], 1, 2).reshape(number_of_homologs, opm * block_columns)
    right_payload = jnp.concatenate([right, marks.astype(bf16)], axis=1)
    both = jnp.concatenate(
        [left_all, jnp.broadcast_to(right_payload[None], (row_total,) + right_payload.shape)], axis=2
    )
    both = jnp.concatenate(exchange(both, "row"), axis=0)
    left_rows = both[:, : tile_rows * opm].reshape(-1, tile_rows, opm)
    mark_rows = both[:, tile_rows * opm : tile_rows * (opm + 1)]
    both = both[:, tile_rows * (opm + 1) :]
    right_cols = both[:, : block_columns * opm].reshape(-1, opm, block_columns)
    mark_cols = both[:, block_columns * opm :]

    split = homolog_activations.reshape(col_total, own_seqs, block_columns, -1)
    own_raw = in_order(exchange(split, "col"), "col")
    own_raw = jnp.swapaxes(own_raw, 0, 1).reshape(own_seqs, residues, -1)
    split_marks = homolog_existence_marks.astype(bf16).reshape(col_total, own_seqs, block_columns)
    own_marks = in_order(exchange(split_marks, "col"), "col")
    own_marks = jnp.swapaxes(own_marks, 0, 1).reshape(own_seqs, residues)

    counts = jnp.dot(mark_rows.T, mark_cols, preferred_element_type=jnp.float32)
    outer_prod = jnp.einsum(
        "sic,sej->ijce", left_rows, right_cols, preferred_element_type=jnp.float32
    ).astype(bf16)
    mixed_opm = regrouped_covariance(
        outer_prod.reshape(tile_rows, block_columns, opm * opm), covariance_exit_mapping
    )
    outer_update = mixed_opm / (count_eps + counts[:, :, None])
    index_rows = lax.dynamic_slice_in_dim(peptide_ordinals, row_first, tile_rows)
    index_cols = lax.dynamic_slice_in_dim(peptide_ordinals, col_first, block_columns)
    chain_rows = lax.dynamic_slice_in_dim(strand_membership, row_first, tile_rows)
    chain_cols = lax.dynamic_slice_in_dim(strand_membership, col_first, block_columns)
    bucket = position_bins(index_rows, index_cols, chain_rows, chain_cols)
    one_hot = (
        bucket[:, :, None] == jnp.arange(distance_ordinal_vectors.shape[0], dtype=jnp.int32)
    ).astype(bf16)
    z_one = (
        coupling_activations.astype(jnp.float32)
        + regrouped_covariance(one_hot, distance_ordinal_vectors)
        + outer_update
    )
    ln_pair = zscore_transform(z_one)
    ln_tri = ln_pair.astype(bf16)
    flat_pair = ln_pair.reshape(tile_rows * block_columns, pair_width)
    flat_tri = ln_tri.reshape(tile_rows * block_columns, pair_width)
    bias_flat = lax.dot_general(
        coupling_score_mapping.astype(jnp.float32),
        flat_pair,
        (((0,), (1,)), ((), ())),
        precision=lax.Precision.HIGHEST,
    ).astype(bf16)
    live_rows = lax.dynamic_slice_in_dim(observed_peptide_marks, row_first, tile_rows)
    live_cols = lax.dynamic_slice_in_dim(observed_peptide_marks, col_first, block_columns)
    pair_live = (live_rows[:, None] * live_cols[None, :]).astype(jnp.float32).reshape(1, 1, -1)
    opened = lax.dot_general(
        triad_opening_mappings, flat_tri, (((0,), (1,)), ((), ())), preferred_element_type=jnp.float32
    ).reshape(4, tri_width, -1)
    sides = (jax.nn.sigmoid(opened[1::2]) * opened[0::2] * pair_live).astype(bf16)
    sides = sides.reshape(2, row_total, col_total, share, -1).transpose(2, 1, 0, 3, 4)

    bias_slots = in_order(collect(bias_flat, "col"), "col")
    bias_slots = in_order(collect(bias_slots, "row"), "row")
    bias_all = bias_slots.reshape(row_total, col_total, heads, tile_rows, block_columns)
    bias_all = bias_all.transpose(2, 0, 3, 1, 4).reshape(heads, residues, residues)

    side_slots = in_order(exchange(sides, "col"), "col")
    side_slots = in_order(exchange(jnp.swapaxes(side_slots, 0, 1), "row"), "row")
    side_all = side_slots.reshape(row_total, col_total, 2, share, tile_rows, block_columns)
    side_all = side_all.transpose(2, 3, 0, 4, 1, 5).reshape(2, share, residues, residues)

    own = zscore_transform(own_raw).astype(bf16)
    queries = regrouped_covariance(own, question_mapping_weights).astype(bf16)
    queries = queries.reshape(own_seqs, residues, heads, head_breadth)
    key_vals = regrouped_covariance(own, address_payload_mapping).astype(bf16)
    gate = jax.nn.sigmoid(regrouped_covariance(own, logistic_valve_mapping))
    keys = key_vals[:, :, :breadth].reshape(own_seqs, residues, heads, head_breadth)
    values = key_vals[:, :, breadth:].reshape(own_seqs, residues, heads, head_breadth)
    scores = jnp.einsum("sihd,sjhd->shij", queries, keys, preferred_element_type=jnp.float32)
    scores = scores * (1.0 / math.sqrt(head_breadth)) + bias_all[None].astype(jnp.float32)
    scores = jnp.where(own_marks[:, None, None, :] > 0, scores, masked_score)
    exp_terms = jnp.exp(scores - jnp.max(scores, axis=-1, keepdims=True))
    weight_sum = jnp.sum(exp_terms, axis=-1)
    attended = jnp.einsum(
        "shij,sjhd->shid", exp_terms.astype(bf16), values, preferred_element_type=jnp.float32
    )
    attended = attended / weight_sum[..., None]
    attended = attended.transpose(0, 2, 1, 3).reshape(own_seqs, residues, breadth)
    gated = (gate * attended).astype(bf16)
    own_after = (
        own_raw.astype(jnp.float32) + regrouped_covariance(gated, mixture_exit_mapping)
    ).astype(bf16)
    own_after = own_after.reshape(own_seqs, col_total, block_columns, -1)
    homologs_after = in_order(exchange(jnp.swapaxes(own_after, 0, 1), "col"), "col")
    homologs_after = homologs_after.reshape(number_of_homologs, block_columns, -1)

    crossed = jnp.einsum(
        "cik,cjk->cij", side_all[0], side_all[1], preferred_element_type=jnp.float32
    ).astype(bf16)
    crossed = crossed.reshape(share, row_total, tile_rows, col_total, block_columns)
    crossed = crossed.transpose(3, 1, 0, 2, 4).reshape(
        col_total, row_total, share, tile_rows * block_columns
    )
    back = in_order(exchange(crossed, "col"), "col")
    back = in_order(exchange(jnp.swapaxes(back, 0, 1), "row"), "row")
    crossed = back.reshape(tri_width, tile_rows * block_columns).astype(jnp.float32)
    centred = crossed - jnp.mean(crossed, axis=0, keepdims=True)
    spread = jnp.mean(centred * centred, axis=0, keepdims=True)
    normed = (centred * lax.rsqrt(spread + norm_eps)).astype(bf16)
    tri_proj = lax.dot_general(
        normed, triad_exit_mapping, (((0,), (0,)), ((), ())), preferred_element_type=jnp.float32
    ).reshape(tile_rows, block_columns, pair_width)
    tri_gate = jax.nn.sigmoid(regrouped_covariance(ln_tri, triad_valve_mapping))
    couplings_after = (z_one + tri_gate * tri_proj).astype(bf16)
    return (homologs_after, couplings_after)


def solution(mesh):
    placed = (
        P("row", "col", None),
        P("row", "col", None),
        P("row", "col"),
        P(),
        P(),
        P(),
        P(),
        P(),
        P(),
        P(),
        P(),
        P(),
        P(),
        P(),
        P(),
        P(),
        P(),
    )
    return jax.shard_map(
        shards,
        mesh=mesh,
        in_specs=placed,
        out_specs=(P("row", "col", None), P("row", "col", None)),
        check_vma=False,
    )
```

```python
import functools
import math

import jax
import jax.numpy as jnp
from jax import lax
from jax.experimental import pallas as pl
from jax.experimental.pallas import tpu as pltpu
from jax.sharding import PartitionSpec as P

REL_MAX = 32


norm_eps = 1e-05
count_eps = 0.001
masked_score = -1000000000.0


def swap(pieces, axis):
    total = len(pieces)
    return [pieces[0]] + [
        lax.ppermute(pieces[k], axis, [(i, i ^ k) for i in range(total)]) for k in range(1, total)
    ]


def collect(block, axis):
    return swap([block] * lax.axis_size(axis), axis)


def exchange(pieces, axis):
    me = lax.axis_index(axis)
    total = lax.axis_size(axis)
    return swap(
        [lax.dynamic_index_in_dim(pieces, me ^ k, 0, keepdims=False) for k in range(total)], axis
    )


def in_order(slots, axis):
    me = lax.axis_index(axis)
    stacked = jnp.stack(slots)
    return jnp.stack(
        [
            lax.dynamic_index_in_dim(stacked, me ^ k, 0, keepdims=False)
            for k in range(len(slots))
        ]
    )


def zscore_transform(inputs):
    inputs = inputs.astype(jnp.float32)
    centred = inputs - jnp.mean(inputs, axis=-1, keepdims=True)
    spread = jnp.mean(centred * centred, axis=-1, keepdims=True)
    return centred * lax.rsqrt(spread + norm_eps)


def regrouped_covariance(operand, weights):
    batch_shape = operand.shape[:-1]
    result = jnp.dot(
        operand.reshape(-1, operand.shape[-1]), weights, preferred_element_type=jnp.float32
    )
    return result.reshape(batch_shape + (weights.shape[-1],))


def position_bins(index_rows, index_cols, chain_rows, chain_cols):
    offset = jnp.clip(index_rows[:, None] - index_cols[None, :] + REL_MAX, 0, 2 * REL_MAX)
    return jnp.where(chain_rows[:, None] == chain_cols[None, :], offset, 2 * REL_MAX + 1)


def operand_kernel(x_ref, marks_ref, spread_ref, wl_ref, wr_ref, left_ref, right_ref, ln, side, acc):
    seqs, places, width = x_ref.shape
    groups = left_ref.shape[0] - 1
    rights = right_ref.shape[0] - 1
    lanes = left_ref.shape[2]
    per = places // groups
    for s in range(seqs):
        own = zscore_transform(x_ref[s])
        for h in range(width // 128):
            ln[h, s * places : (s + 1) * places, :] = own[:, h * 128 : (h + 1) * 128]
    marks = marks_ref[...]
    for s in range(seqs):
        own = jnp.concatenate(
            [ln[h, s * places : (s + 1) * places, :] for h in range(width // 128)], axis=1
        )
        got = lax.dot_general(
            wr_ref[...], own.astype(jnp.bfloat16), (((1,), (1,)), ((), ())),
            preferred_element_type=jnp.float32,
        )
        got = got * marks[s : s + 1, :]
        side[pl.ds(s, rights, stride=seqs), :] = jnp.concatenate(
            [got, jnp.zeros((rights, lanes - places), jnp.float32)], axis=1
        )
    right_ref[:rights] = side[...].reshape(rights, seqs, lanes).astype(jnp.bfloat16)
    for q in range(per):
        for g in range(groups):
            for h in range(width // 128):
                acc[g * seqs : (g + 1) * seqs, h * 128 : (h + 1) * 128] = ln[
                    h, pl.ds(g * per + q, seqs, stride=places), :
                ]
        part = jnp.dot(
            acc[...].astype(jnp.bfloat16), wl_ref[q], preferred_element_type=jnp.float32
        )
        total = part if q == 0 else total + part
    spread = jnp.dot(
        marks.astype(jnp.bfloat16), spread_ref[...], preferred_element_type=jnp.float32
    )
    for g in range(groups):
        left_ref[g] = (
            total[g * seqs : (g + 1) * seqs] * spread[:, g * lanes : (g + 1) * lanes]
        ).astype(jnp.bfloat16)
    block = jnp.zeros((seqs, lanes), jnp.float32)
    side[:seqs, :] = block
    side[:seqs, :places] = marks
    left_ref[groups] = side[:seqs, :].astype(jnp.bfloat16)
    right_ref[rights] = side[:seqs, :].astype(jnp.bfloat16)


def opm_operands(x, marks, mapping):
    seqs, places, width = x.shape
    opm = mapping.shape[1] // 2
    lanes = 128
    per = lanes // opm
    groups = places // per
    wl = jnp.stack(
        [
            jnp.pad(mapping[:, :opm], ((0, 0), (q * opm, lanes - (q + 1) * opm)))
            for q in range(per)
        ]
    )
    wr = mapping[:, opm:].T
    spread = jnp.repeat(jnp.eye(places, dtype=jnp.bfloat16), opm, axis=1)
    return pl.pallas_call(
        operand_kernel,
        out_shape=(
            jax.ShapeDtypeStruct((groups + 1, seqs, lanes), jnp.bfloat16),
            jax.ShapeDtypeStruct((opm + 1, seqs, lanes), jnp.bfloat16),
        ),
        scratch_shapes=[
            pltpu.VMEM((width // 128, seqs * places, 128), jnp.float32),
            pltpu.VMEM((opm * seqs, lanes), jnp.float32),
            pltpu.VMEM((groups * seqs, width), jnp.float32),
        ],
        compiler_params=pltpu.CompilerParams(vmem_limit_bytes=40 << 20),
        name="outer_operands",
    )(x, marks, spread, wl, wr)


def pair_kernel(total_rows, total_cols, *refs):
    spots = refs[0]
    rows_in = refs[1 : 1 + total_rows]
    cols_in = refs[1 + total_rows : 1 + 2 * total_rows]
    (
        pair_ref, place_ref, exit_ref, near_ref, open_ref, score_ref, live_ref,
    ) = refs[1 + 2 * total_rows : 8 + 2 * total_rows]
    outs = refs[8 + 2 * total_rows :]
    z_ref, high_ref, bias_ref = outs[:3]
    side_refs = outs[3 : 3 + total_cols]
    left, right, prod, counts, low = outs[3 + total_cols :]
    step = pl.program_id(0)
    group, places, width = pair_ref.shape
    seqs = rows_in[0].shape[1]
    lanes = 128
    opm = cols_in[0].shape[0] - 1
    blocks = rows_in[0].shape[0] - 1
    bf16 = jnp.bfloat16

    @pl.when(step == 0)
    def _():
        mark_rows, mark_cols = [], []
        for k in range(total_rows):
            for g in range(blocks):
                left[g, k * seqs : (k + 1) * seqs, :] = rows_in[k][g]
            for e in range(opm):
                right[k * seqs : (k + 1) * seqs, e * lanes : (e + 1) * lanes] = cols_in[k][e]
            mark_rows.append(rows_in[k][blocks])
            mark_cols.append(cols_in[k][opm])
        mark_rows = jnp.concatenate(mark_rows, axis=0)
        mark_cols = jnp.concatenate(mark_cols, axis=0)
        counts[...] = lax.dot_general(
            mark_rows, mark_cols, (((0,), (0,)), ((), ())), preferred_element_type=jnp.float32
        )

    grid_left = left[step]
    half = opm // 2
    for part in range(2):
        got = lax.dot_general(
            grid_left, right[:, part * half * lanes : (part + 1) * half * lanes],
            (((0,), (0,)), ((), ())), preferred_element_type=jnp.float32,
        ).astype(bf16)
        for e in range(half):
            for i in range(group):
                prod[
                    (part * half + e) * opm : (part * half + e + 1) * opm,
                    i * lanes : (i + 1) * lanes,
                ] = got[i * opm : (i + 1) * opm, e * lanes : (e + 1) * lanes]
    mixed = jnp.dot(exit_ref[...], prod[...], preferred_element_type=jnp.float32)
    pos_cols = place_ref[0:1, :]
    chain_cols = place_ref[1:2, :]
    bins, amount = [], []
    for i in range(group):
        here = step * group + i
        offset = jnp.clip(spots[0, here] - pos_cols + REL_MAX, 0, 2 * REL_MAX)
        bins.append(jnp.where(chain_cols == spots[1, here], offset, 2 * REL_MAX + 1))
        amount.append(counts[pl.ds(spots[2, 0] + here, 1), :])
    bins = jnp.concatenate(bins, axis=1)
    amount = jnp.concatenate(amount, axis=1)
    one_hot = (
        lax.broadcasted_iota(jnp.int32, (near_ref.shape[1], group * lanes), 0) == bins
    )
    one_hot = jnp.where(one_hot, 1.0, 0.0).astype(bf16)
    near = jnp.dot(near_ref[...], one_hot, preferred_element_type=jnp.float32)
    update = jnp.transpose(mixed / (count_eps + amount) + near)
    z = jnp.concatenate(
        [
            pair_ref[i].astype(jnp.float32) + update[i * lanes : i * lanes + places]
            for i in range(group)
        ],
        axis=0,
    )
    z_ref[...] = z
    ln = zscore_transform(z)
    high = ln.astype(bf16)
    start = pl.multiple_of(step * (group * places), 16)
    high_ref[pl.ds(start, group * places), :] = high
    low[pl.ds(start, group * places), :] = (ln - high.astype(jnp.float32)).astype(bf16)

    @pl.when(step == pl.num_programs(0) - 1)
    def _():
        pairs = high_ref.shape[0]
        chunk = 512
        transposed = (((1,), (1,)), ((), ()))
        half_rows = open_ref.shape[0] // 2
        each = half_rows // total_cols
        for first in range(0, pairs, chunk):
            last = min(first + chunk, pairs)
            ours = high_ref[first:last, :]
            bias = lax.dot_general(
                score_ref[...], ours, transposed, preferred_element_type=jnp.float32
            ) + lax.dot_general(
                score_ref[...], low[first:last, :], transposed, preferred_element_type=jnp.float32
            )
            bias_ref[:, first:last] = bias[: bias_ref.shape[0]].astype(bf16)
            opened = lax.dot_general(
                open_ref[...], ours, transposed, preferred_element_type=jnp.float32
            )
            sides = (
                jax.nn.sigmoid(opened[half_rows:]) * opened[:half_rows] * live_ref[:, first:last]
            ).astype(bf16)
            for m in range(total_cols):
                side_refs[m][:, first:last] = sides[m * each : (m + 1) * each]


def pair_stage(rows_in, cols_in, pair, spots, place, exit_t, near_t, open_t, score_t, live, total_cols):
    total_rows = len(rows_in)
    tile_rows, places, width = pair.shape
    blocks, seqs, lanes = rows_in[0].shape
    blocks -= 1
    group = tile_rows // blocks
    opm = cols_in[0].shape[0] - 1
    pairs = tile_rows * places
    heads = 8
    each = open_t.shape[0] // 2 // total_cols
    every = total_rows * seqs

    def whole(a):
        return pl.BlockSpec(a.shape, lambda g, n=a.ndim: (0,) * n)

    def whole_out(shape):
        return pl.BlockSpec(shape, lambda g, n=len(shape): (0,) * n)

    ins = list(rows_in) + list(cols_in)
    rest = [place, exit_t, near_t, open_t, score_t, live]
    bf16 = jnp.bfloat16
    outs = [
        jax.ShapeDtypeStruct((pairs, width), jnp.float32),
        jax.ShapeDtypeStruct((pairs, width), bf16),
        jax.ShapeDtypeStruct((score_t.shape[0], pairs), bf16),
    ] + [jax.ShapeDtypeStruct((each, pairs), bf16)] * total_cols
    return pl.pallas_call(
        functools.partial(pair_kernel, total_rows, total_cols),
        grid=(blocks,),
        in_specs=[pl.BlockSpec(memory_space=pltpu.SMEM)]
        + [whole(a) for a in ins]
        + [pl.BlockSpec((group, places, width), lambda g: (g, 0, 0))]
        + [whole(a) for a in rest],
        out_specs=[pl.BlockSpec((group * places, width), lambda g: (g, 0))]
        + [whole_out(o.shape) for o in outs[1:]],
        out_shape=outs,
        scratch_shapes=[
            pltpu.VMEM((blocks, every, lanes), bf16),
            pltpu.VMEM((every, opm * lanes), bf16),
            pltpu.VMEM((opm * opm, group * lanes), bf16),
            pltpu.VMEM((lanes, lanes), jnp.float32),
            pltpu.VMEM((pairs, width), bf16),
        ],
        compiler_params=pltpu.CompilerParams(
            vmem_limit_bytes=56 << 20, dimension_semantics=("arbitrary",)
        ),
        cost_estimate=pl.CostEstimate(
            flops=20 * 10**9, bytes_accessed=16 * 10**6, transcendentals=10**6
        ),
        name="pair_update",
    )(spots, *ins, pair, *rest)


def shards(
    homolog_activations,
    coupling_activations,
    homolog_existence_marks,
    observed_peptide_marks,
    peptide_ordinals,
    strand_membership,
    distance_ordinal_vectors,
    coupling_score_mapping,
    question_mapping_weights,
    address_payload_mapping,
    logistic_valve_mapping,
    mixture_exit_mapping,
    twofold_covariance_mapping,
    covariance_exit_mapping,
    triad_opening_mappings,
    triad_valve_mapping,
    triad_exit_mapping,
):
    row_total = lax.axis_size("row")
    col_total = lax.axis_size("col")
    group_ratio = row_total // col_total
    devices = row_total * col_total
    row_place = lax.axis_index("row")
    col_place = lax.axis_index("col")
    tile_rows = coupling_activations.shape[0]
    block_columns = coupling_activations.shape[1]
    number_of_homologs = homolog_activations.shape[0]
    residues = row_total * tile_rows
    heads = coupling_score_mapping.shape[1]
    breadth = question_mapping_weights.shape[1]
    head_breadth = breadth // heads
    opm = twofold_covariance_mapping.shape[1] // 2
    tri_width = triad_exit_mapping.shape[0]
    pair_width = coupling_activations.shape[2]
    own_seqs = number_of_homologs // col_total
    share = tri_width // devices
    row_first = row_place * tile_rows
    col_first = col_place * block_columns
    bf16 = jnp.bfloat16

    marks = homolog_existence_marks.astype(jnp.float32)
    left, right = opm_operands(homolog_activations, marks, twofold_covariance_mapping)
    right_slots = collect(right, "row")
    left_slots = jnp.stack(collect(left, "col"))
    blocks = (left.shape[0] - 1) // group_ratio
    left_pieces = []
    for k in range(row_total):
        target = row_place ^ k
        slot = (target // group_ratio) ^ col_place
        mine = lax.dynamic_index_in_dim(left_slots, slot, 0, keepdims=False)
        part = lax.dynamic_slice_in_dim(mine, target % group_ratio * blocks, blocks, 0)
        left_pieces.append(jnp.concatenate([part, mine[-1:]], axis=0))
    left_slots = swap(left_pieces, "row")

    split = homolog_activations.reshape(col_total, own_seqs, block_columns, -1)
    own_raw = in_order(exchange(split, "col"), "col")
    own_raw = jnp.swapaxes(own_raw, 0, 1).reshape(own_seqs, residues, -1)
    split_marks = homolog_existence_marks.astype(bf16).reshape(col_total, own_seqs, block_columns)
    own_marks = in_order(exchange(split_marks, "col"), "col")
    own_marks = jnp.swapaxes(own_marks, 0, 1).reshape(own_seqs, residues)

    lanes = 128
    spots = jnp.stack(
        [
            lax.dynamic_slice_in_dim(peptide_ordinals, row_first, tile_rows),
            lax.dynamic_slice_in_dim(strand_membership, row_first, tile_rows),
            jnp.full((tile_rows,), row_place % group_ratio * tile_rows, jnp.int32),
        ]
    )
    place = jnp.pad(
        jnp.stack(
            [
                lax.dynamic_slice_in_dim(peptide_ordinals, col_first, block_columns),
                lax.dynamic_slice_in_dim(strand_membership, col_first, block_columns),
            ]
        ),
        ((0, 6), (0, lanes - block_columns)),
    )
    exit_t = covariance_exit_mapping.reshape(opm, opm, pair_width).transpose(2, 1, 0)
    exit_t = exit_t.reshape(pair_width, opm * opm)
    near_t = jnp.pad(
        distance_ordinal_vectors, ((0, lanes - distance_ordinal_vectors.shape[0]), (0, 0))
    ).T
    open_t = triad_opening_mappings.reshape(pair_width, 2, 2, row_total, col_total, share)
    open_t = open_t.transpose(2, 4, 3, 1, 5, 0)
    open_t = jnp.concatenate(
        [
            lax.dynamic_slice_in_dim(open_t, col_place ^ m, 1, 1)
            for m in range(col_total)
        ],
        axis=1,
    ).reshape(4 * tri_width, pair_width)
    score_t = coupling_score_mapping.T
    live_rows = lax.dynamic_slice_in_dim(observed_peptide_marks, row_first, tile_rows)
    live_cols = lax.dynamic_slice_in_dim(observed_peptide_marks, col_first, block_columns)
    live = (live_rows[:, None] * live_cols[None, :]).astype(jnp.float32).reshape(1, -1)
    z_one, ln_tri, bias_flat, *side_pieces = pair_stage(
        left_slots, right_slots, coupling_activations, spots, place, exit_t, near_t, open_t,
        score_t, live, col_total,
    )
    z_one = z_one.reshape(tile_rows, block_columns, pair_width)
    ln_tri = ln_tri.reshape(tile_rows, block_columns, pair_width)

    bias_slots = in_order(collect(bias_flat, "col"), "col")
    bias_slots = in_order(collect(bias_slots, "row"), "row")
    bias_all = bias_slots.reshape(row_total, col_total, heads, tile_rows, block_columns)
    bias_all = bias_all.transpose(2, 0, 3, 1, 4).reshape(heads, residues, residues)

    side_slots = in_order(swap(side_pieces, "col"), "col")
    side_slots = side_slots.reshape(col_total, row_total, 2, share, -1)
    side_slots = in_order(exchange(jnp.swapaxes(side_slots, 0, 1), "row"), "row")
    side_all = side_slots.reshape(row_total, col_total, 2, share, tile_rows, block_columns)
    side_all = side_all.transpose(2, 3, 0, 4, 1, 5).reshape(2, share, residues, residues)

    own = zscore_transform(own_raw).astype(bf16)
    queries = regrouped_covariance(own, question_mapping_weights).astype(bf16)
    queries = queries.reshape(own_seqs, residues, heads, head_breadth)
    key_vals = regrouped_covariance(own, address_payload_mapping).astype(bf16)
    gate = jax.nn.sigmoid(regrouped_covariance(own, logistic_valve_mapping))
    keys = key_vals[:, :, :breadth].reshape(own_seqs, residues, heads, head_breadth)
    values = key_vals[:, :, breadth:].reshape(own_seqs, residues, heads, head_breadth)
    scores = jnp.einsum("sihd,sjhd->shij", queries, keys, preferred_element_type=jnp.float32)
    scores = scores * (1.0 / math.sqrt(head_breadth)) + bias_all[None].astype(jnp.float32)
    scores = jnp.where(own_marks[:, None, None, :] > 0, scores, masked_score)
    exp_terms = jnp.exp(scores - jnp.max(scores, axis=-1, keepdims=True))
    weight_sum = jnp.sum(exp_terms, axis=-1)
    attended = jnp.einsum(
        "shij,sjhd->shid", exp_terms.astype(bf16), values, preferred_element_type=jnp.float32
    )
    attended = attended / weight_sum[..., None]
    attended = attended.transpose(0, 2, 1, 3).reshape(own_seqs, residues, breadth)
    gated = (gate * attended).astype(bf16)
    own_after = (
        own_raw.astype(jnp.float32) + regrouped_covariance(gated, mixture_exit_mapping)
    ).astype(bf16)
    own_after = own_after.reshape(own_seqs, col_total, block_columns, -1)
    homologs_after = in_order(exchange(jnp.swapaxes(own_after, 0, 1), "col"), "col")
    homologs_after = homologs_after.reshape(number_of_homologs, block_columns, -1)

    crossed = jnp.einsum(
        "cik,cjk->cij", side_all[0], side_all[1], preferred_element_type=jnp.float32
    ).astype(bf16)
    crossed = crossed.reshape(share, row_total, tile_rows, col_total, block_columns)
    crossed = crossed.transpose(3, 1, 0, 2, 4).reshape(
        col_total, row_total, share, tile_rows * block_columns
    )
    back = in_order(exchange(crossed, "col"), "col")
    back = in_order(exchange(jnp.swapaxes(back, 0, 1), "row"), "row")
    crossed = back.reshape(tri_width, tile_rows * block_columns).astype(jnp.float32)
    centred = crossed - jnp.mean(crossed, axis=0, keepdims=True)
    spread = jnp.mean(centred * centred, axis=0, keepdims=True)
    normed = (centred * lax.rsqrt(spread + norm_eps)).astype(bf16)
    tri_proj = lax.dot_general(
        normed, triad_exit_mapping, (((0,), (0,)), ((), ())), preferred_element_type=jnp.float32
    ).reshape(tile_rows, block_columns, pair_width)
    tri_gate = jax.nn.sigmoid(regrouped_covariance(ln_tri, triad_valve_mapping))
    couplings_after = (z_one + tri_gate * tri_proj).astype(bf16)
    return (homologs_after, couplings_after)


def solution(mesh):
    placed = (
        P("row", "col", None),
        P("row", "col", None),
        P("row", "col"),
        P(),
        P(),
        P(),
        P(),
        P(),
        P(),
        P(),
        P(),
        P(),
        P(),
        P(),
        P(),
        P(),
        P(),
    )
    return jax.shard_map(
        shards,
        mesh=mesh,
        in_specs=placed,
        out_specs=(P("row", "col", None), P("row", "col", None)),
        check_vma=False,
    )
```

```python
import functools
import math

import jax
import jax.numpy as jnp
from jax import lax
from jax.experimental import pallas as pl
from jax.experimental.pallas import tpu as pltpu
from jax.sharding import PartitionSpec as P

REL_MAX = 32


norm_eps = 1e-05
count_eps = 0.001
masked_score = -1000000000.0


def swap(pieces, axis):
    total = len(pieces)
    return [pieces[0]] + [
        lax.ppermute(pieces[k], axis, [(i, i ^ k) for i in range(total)]) for k in range(1, total)
    ]


def collect(block, axis):
    return swap([block] * lax.axis_size(axis), axis)


def exchange(pieces, axis):
    me = lax.axis_index(axis)
    total = lax.axis_size(axis)
    return swap(
        [lax.dynamic_index_in_dim(pieces, me ^ k, 0, keepdims=False) for k in range(total)], axis
    )


def in_order(slots, axis):
    me = lax.axis_index(axis)
    stacked = jnp.stack(slots)
    return jnp.stack(
        [
            lax.dynamic_index_in_dim(stacked, me ^ k, 0, keepdims=False)
            for k in range(len(slots))
        ]
    )


def zscore_transform(inputs):
    inputs = inputs.astype(jnp.float32)
    centred = inputs - jnp.mean(inputs, axis=-1, keepdims=True)
    spread = jnp.mean(centred * centred, axis=-1, keepdims=True)
    return centred * lax.rsqrt(spread + norm_eps)


def regrouped_covariance(operand, weights):
    batch_shape = operand.shape[:-1]
    result = jnp.dot(
        operand.reshape(-1, operand.shape[-1]), weights, preferred_element_type=jnp.float32
    )
    return result.reshape(batch_shape + (weights.shape[-1],))


def position_bins(index_rows, index_cols, chain_rows, chain_cols):
    offset = jnp.clip(index_rows[:, None] - index_cols[None, :] + REL_MAX, 0, 2 * REL_MAX)
    return jnp.where(chain_rows[:, None] == chain_cols[None, :], offset, 2 * REL_MAX + 1)


def operand_kernel(x_ref, marks_ref, spread_ref, wl_ref, wr_ref, left_ref, right_ref, ln, side, acc):
    seqs, places, width = x_ref.shape
    groups = left_ref.shape[0] - 1
    rights = right_ref.shape[0] - 1
    lanes = left_ref.shape[2]
    per = places // groups
    for s in range(seqs):
        own = zscore_transform(x_ref[s])
        for h in range(width // 128):
            ln[h, s * places : (s + 1) * places, :] = own[:, h * 128 : (h + 1) * 128]
    marks = marks_ref[...]
    for s in range(seqs):
        own = jnp.concatenate(
            [ln[h, s * places : (s + 1) * places, :] for h in range(width // 128)], axis=1
        )
        got = lax.dot_general(
            wr_ref[...], own.astype(jnp.bfloat16), (((1,), (1,)), ((), ())),
            preferred_element_type=jnp.float32,
        )
        got = got * marks[s : s + 1, :]
        side[pl.ds(s, rights, stride=seqs), :] = jnp.concatenate(
            [got, jnp.zeros((rights, lanes - places), jnp.float32)], axis=1
        )
    right_ref[:rights] = side[...].reshape(rights, seqs, lanes).astype(jnp.bfloat16)
    for q in range(per):
        for g in range(groups):
            for h in range(width // 128):
                acc[g * seqs : (g + 1) * seqs, h * 128 : (h + 1) * 128] = ln[
                    h, pl.ds(g * per + q, seqs, stride=places), :
                ]
        part = jnp.dot(
            acc[...].astype(jnp.bfloat16), wl_ref[q], preferred_element_type=jnp.float32
        )
        total = part if q == 0 else total + part
    spread = jnp.dot(
        marks.astype(jnp.bfloat16), spread_ref[...], preferred_element_type=jnp.float32
    )
    for g in range(groups):
        left_ref[g] = (
            total[g * seqs : (g + 1) * seqs] * spread[:, g * lanes : (g + 1) * lanes]
        ).astype(jnp.bfloat16)
    block = jnp.zeros((seqs, lanes), jnp.float32)
    side[:seqs, :] = block
    side[:seqs, :places] = marks
    left_ref[groups] = side[:seqs, :].astype(jnp.bfloat16)
    right_ref[rights] = side[:seqs, :].astype(jnp.bfloat16)


def opm_operands(x, marks, mapping):
    seqs, places, width = x.shape
    opm = mapping.shape[1] // 2
    lanes = 128
    per = lanes // opm
    groups = places // per
    wl = jnp.stack(
        [
            jnp.pad(mapping[:, :opm], ((0, 0), (q * opm, lanes - (q + 1) * opm)))
            for q in range(per)
        ]
    )
    wr = mapping[:, opm:].T
    spread = jnp.repeat(jnp.eye(places, dtype=jnp.bfloat16), opm, axis=1)
    return pl.pallas_call(
        operand_kernel,
        out_shape=(
            jax.ShapeDtypeStruct((groups + 1, seqs, lanes), jnp.bfloat16),
            jax.ShapeDtypeStruct((opm + 1, seqs, lanes), jnp.bfloat16),
        ),
        scratch_shapes=[
            pltpu.VMEM((width // 128, seqs * places, 128), jnp.float32),
            pltpu.VMEM((opm * seqs, lanes), jnp.float32),
            pltpu.VMEM((groups * seqs, width), jnp.float32),
        ],
        compiler_params=pltpu.CompilerParams(vmem_limit_bytes=40 << 20),
        name="outer_operands",
    )(x, marks, spread, wl, wr)


def pair_kernel(total_rows, total_cols, *refs):
    spots = refs[0]
    rows_in = refs[1 : 1 + total_rows]
    cols_in = refs[1 + total_rows : 1 + 2 * total_rows]
    (
        pair_ref, place_ref, exit_ref, near_ref, open_ref, score_ref, live_ref,
    ) = refs[1 + 2 * total_rows : 8 + 2 * total_rows]
    outs = refs[8 + 2 * total_rows :]
    z_ref, high_ref, bias_ref = outs[:3]
    side_refs = outs[3 : 3 + total_cols]
    left, right, prod, counts, low = outs[3 + total_cols :]
    step = pl.program_id(0)
    group, places, width = pair_ref.shape
    seqs = rows_in[0].shape[1]
    lanes = 128
    opm = cols_in[0].shape[0] - 1
    blocks = rows_in[0].shape[0] - 1
    bf16 = jnp.bfloat16

    @pl.when(step == 0)
    def _():
        mark_rows, mark_cols = [], []
        for k in range(total_rows):
            for g in range(blocks):
                left[g, k * seqs : (k + 1) * seqs, :] = rows_in[k][g]
            for e in range(opm):
                right[k * seqs : (k + 1) * seqs, e * lanes : (e + 1) * lanes] = cols_in[k][e]
            mark_rows.append(rows_in[k][blocks])
            mark_cols.append(cols_in[k][opm])
        mark_rows = jnp.concatenate(mark_rows, axis=0)
        mark_cols = jnp.concatenate(mark_cols, axis=0)
        counts[...] = lax.dot_general(
            mark_rows, mark_cols, (((0,), (0,)), ((), ())), preferred_element_type=jnp.float32
        )

    grid_left = left[step]
    half = opm // 2
    for part in range(2):
        got = lax.dot_general(
            grid_left, right[:, part * half * lanes : (part + 1) * half * lanes],
            (((0,), (0,)), ((), ())), preferred_element_type=jnp.float32,
        ).astype(bf16)
        for e in range(half):
            for i in range(group):
                prod[
                    (part * half + e) * opm : (part * half + e + 1) * opm,
                    i * lanes : (i + 1) * lanes,
                ] = got[i * opm : (i + 1) * opm, e * lanes : (e + 1) * lanes]
    mixed = jnp.dot(exit_ref[...], prod[...], preferred_element_type=jnp.float32)
    pos_cols = place_ref[0:1, :]
    chain_cols = place_ref[1:2, :]
    bins, amount = [], []
    for i in range(group):
        here = step * group + i
        offset = jnp.clip(spots[0, here] - pos_cols + REL_MAX, 0, 2 * REL_MAX)
        bins.append(jnp.where(chain_cols == spots[1, here], offset, 2 * REL_MAX + 1))
        amount.append(counts[pl.ds(spots[2, 0] + here, 1), :])
    bins = jnp.concatenate(bins, axis=1)
    amount = jnp.concatenate(amount, axis=1)
    one_hot = (
        lax.broadcasted_iota(jnp.int32, (near_ref.shape[1], group * lanes), 0) == bins
    )
    one_hot = jnp.where(one_hot, 1.0, 0.0).astype(bf16)
    near = jnp.dot(near_ref[...], one_hot, preferred_element_type=jnp.float32)
    update = jnp.transpose(mixed / (count_eps + amount) + near)
    z = jnp.concatenate(
        [
            pair_ref[i].astype(jnp.float32) + update[i * lanes : i * lanes + places]
            for i in range(group)
        ],
        axis=0,
    )
    z_ref[...] = z
    ln = zscore_transform(z)
    high = ln.astype(bf16)
    start = pl.multiple_of(step * (group * places), 16)
    high_ref[pl.ds(start, group * places), :] = high
    low[pl.ds(start, group * places), :] = (ln - high.astype(jnp.float32)).astype(bf16)

    @pl.when(step == pl.num_programs(0) - 1)
    def _():
        pairs = high_ref.shape[0]
        chunk = 512
        transposed = (((1,), (1,)), ((), ()))
        half_rows = open_ref.shape[0] // 2
        each = half_rows // total_cols
        count = each // total_rows
        for first in range(0, pairs, chunk):
            last = min(first + chunk, pairs)
            ours = high_ref[first:last, :]
            bias = lax.dot_general(
                score_ref[...], ours, transposed, preferred_element_type=jnp.float32
            ) + lax.dot_general(
                score_ref[...], low[first:last, :], transposed, preferred_element_type=jnp.float32
            )
            bias_ref[:, first:last] = bias[: bias_ref.shape[0]].astype(bf16)
            opened = lax.dot_general(
                open_ref[...], ours, transposed, preferred_element_type=jnp.float32
            )
            sides = (
                jax.nn.sigmoid(opened[half_rows:]) * opened[:half_rows] * live_ref[:, first:last]
            )
            for m in range(total_cols):
                for r in range(total_rows):
                    at = m * each + r * count
                    side_refs[m][r, :, first:last] = sides[at : at + count].astype(bf16)


def pair_stage(rows_in, cols_in, pair, spots, place, exit_t, near_t, open_t, score_t, live, total_cols):
    total_rows = len(rows_in)
    tile_rows, places, width = pair.shape
    blocks, seqs, lanes = rows_in[0].shape
    blocks -= 1
    group = tile_rows // blocks
    opm = cols_in[0].shape[0] - 1
    pairs = tile_rows * places
    heads = 8
    each = open_t.shape[0] // 2 // total_cols
    every = total_rows * seqs

    def whole(a):
        return pl.BlockSpec(a.shape, lambda g, n=a.ndim: (0,) * n)

    def whole_out(shape):
        return pl.BlockSpec(shape, lambda g, n=len(shape): (0,) * n)

    ins = list(rows_in) + list(cols_in)
    rest = [place, exit_t, near_t, open_t, score_t, live]
    bf16 = jnp.bfloat16
    outs = [
        jax.ShapeDtypeStruct((pairs, width), jnp.float32),
        jax.ShapeDtypeStruct((pairs, width), bf16),
        jax.ShapeDtypeStruct((score_t.shape[0], pairs), bf16),
    ] + [jax.ShapeDtypeStruct((total_rows, each // total_rows, pairs), bf16)] * total_cols
    return pl.pallas_call(
        functools.partial(pair_kernel, total_rows, total_cols),
        grid=(blocks,),
        in_specs=[pl.BlockSpec(memory_space=pltpu.SMEM)]
        + [whole(a) for a in ins]
        + [pl.BlockSpec((group, places, width), lambda g: (g, 0, 0))]
        + [whole(a) for a in rest],
        out_specs=[pl.BlockSpec((group * places, width), lambda g: (g, 0))]
        + [whole_out(o.shape) for o in outs[1:]],
        out_shape=outs,
        scratch_shapes=[
            pltpu.VMEM((blocks, every, lanes), bf16),
            pltpu.VMEM((every, opm * lanes), bf16),
            pltpu.VMEM((opm * opm, group * lanes), bf16),
            pltpu.VMEM((lanes, lanes), jnp.float32),
            pltpu.VMEM((pairs, width), bf16),
        ],
        compiler_params=pltpu.CompilerParams(
            vmem_limit_bytes=56 << 20, dimension_semantics=("arbitrary",)
        ),
        cost_estimate=pl.CostEstimate(
            flops=20 * 10**9, bytes_accessed=16 * 10**6, transcendentals=10**6
        ),
        name="pair_update",
    )(spots, *ins, pair, *rest)


def spread_slots(slots, stack, base_ref, tiles, total_cols, places):
    total = len(slots)
    pairs = slots[0].shape[1]
    count = slots[0].shape[0] // total_cols
    rows = pairs // places
    residues = rows * total
    lane = lax.broadcasted_iota(jnp.int32, (count, 128), 1)
    for k in range(total):
        stack[k, :, :pairs] = slots[k][...]

    def one(k, carry):
        base = base_ref[k]
        for i in range(rows):
            first = i * places // 128 * 128
            off = i * places - first
            window = stack[k, :, first : first + 256].astype(jnp.float32)
            made = [None] * tiles.shape[0]
            for c in range(total_cols):
                to, at = divmod(c * places, 128)
                piece = window[c * count : (c + 1) * count]
                if at != off:
                    piece = pltpu.roll(piece, (at - off) % 256, 1)
                begin = piece[:, :128]
                made[to] = begin if made[to] is None else jnp.where(lane >= at, begin, made[to])
                if at + places > 128:
                    made[to + 1] = piece[:, 128:]
            kept = residues - 128 * (len(made) - 1)
            made[-1] = jnp.where(lane < kept, made[-1], 0.0)
            for t, tile in enumerate(made):
                tiles[t, pl.ds(base + i, count, stride=residues), :] = tile
        return carry

    lax.fori_loop(0, total, one, 0)


def attention_kernel(total_rows, total_cols, *refs):
    base_ref = refs[0]
    bias_in = refs[1 : 1 + total_rows]
    x_in = refs[1 + total_rows : 1 + total_rows + total_cols]
    mark_ref, project_ref, mix_ref = refs[1 + total_rows + total_cols : 4 + total_rows + total_cols]
    outs = refs[4 + total_rows + total_cols : 4 + total_rows + 2 * total_cols]
    stack, tiles, mixed = refs[4 + total_rows + 2 * total_cols :]
    places, width = x_in[0].shape[1:]
    residues = places * total_cols
    heads = bias_in[0].shape[0] // total_cols
    each = width // heads
    group = 128 // each
    padded = tiles.shape[0] * 128
    bf16 = jnp.bfloat16
    transposed = (((1,), (1,)), ((), ()))
    chunk = 176

    @pl.when(pl.program_id(0) == 0)
    def _():
        spread_slots(bias_in, stack, base_ref, tiles, total_cols, places)

    x = jnp.concatenate([r[0].astype(jnp.float32) for r in x_in], axis=0)
    made = jnp.dot(
        zscore_transform(x).astype(bf16), project_ref[...], preferred_element_type=jnp.float32
    )
    present = mark_ref[0] > 0.0
    lane = lax.broadcasted_iota(jnp.int32, (1, 128), 1)
    scale = 1.0 / math.sqrt(each)
    filler = jnp.zeros((padded - residues, 128), bf16)
    for h0 in range(0, heads, group):
        at = h0 * each
        queries = made[:, at : at + 128].astype(bf16)
        keys = made[:, width + at : width + at + 128].astype(bf16)
        values = made[:, 2 * width + at : 2 * width + at + 128].astype(bf16)
        keys = jnp.concatenate([keys, filler], axis=0)
        values = jnp.concatenate([values, filler], axis=0)
        for first in range(0, residues, chunk):
            total = jnp.zeros((chunk, 128), jnp.float32)
            for h in range(group):
                ours = (lane >= h * each) & (lane < (h + 1) * each)
                own_keys = jnp.where(ours, keys, jnp.zeros_like(keys))
                own_values = jnp.where(ours, values, jnp.zeros_like(values))
                scores = lax.dot_general(
                    queries[first : first + chunk], own_keys, transposed,
                    preferred_element_type=jnp.float32,
                )
                start = (h0 + h) * residues + first
                bias = jnp.concatenate(
                    [tiles[t, start : start + chunk, :] for t in range(tiles.shape[0])], axis=1
                )
                scores = jnp.where(present, scores * scale + bias, masked_score)
                terms = jnp.exp(scores - jnp.max(scores, axis=1, keepdims=True))
                weight = jnp.sum(terms, axis=1, keepdims=True)
                got = jnp.dot(terms.astype(bf16), own_values, preferred_element_type=jnp.float32)
                total = total + got / weight
            gate = jax.nn.sigmoid(made[first : first + chunk, 3 * width + at : 3 * width + at + 128])
            mixed[first : first + chunk, at : at + 128] = (gate * total).astype(bf16)
    after = x + jnp.dot(mixed[...], mix_ref[...], preferred_element_type=jnp.float32)
    for m in range(total_cols):
        outs[m][0] = after[m * places : (m + 1) * places].astype(bf16)


def attend(base, bias_slots, x_slots, marks, project, mix):
    total_rows, total_cols = len(bias_slots), len(x_slots)
    seqs, places, width = x_slots[0].shape
    residues = places * total_cols
    padded = -(-residues // 128) * 128
    rows, pairs = bias_slots[0].shape
    heads = rows // total_cols
    wide = -(-pairs // 128) * 128 + 128

    def whole(a):
        return pl.BlockSpec(a.shape, lambda s, n=a.ndim: (0,) * n)

    per_seq = pl.BlockSpec((1, places, width), lambda s: (s, 0, 0))
    bf16 = jnp.bfloat16
    return pl.pallas_call(
        functools.partial(attention_kernel, total_rows, total_cols),
        grid=(seqs,),
        in_specs=[pl.BlockSpec(memory_space=pltpu.SMEM)]
        + [whole(a) for a in bias_slots]
        + [per_seq] * total_cols
        + [pl.BlockSpec((1, 1, padded), lambda s: (s, 0, 0)), whole(project), whole(mix)],
        out_specs=[per_seq] * total_cols,
        out_shape=[jax.ShapeDtypeStruct((seqs, places, width), bf16)] * total_cols,
        scratch_shapes=[
            pltpu.VMEM((total_rows, rows, wide), bf16),
            pltpu.VMEM((padded // 128, heads * residues, 128), jnp.float32),
            pltpu.VMEM((residues, width), bf16),
        ],
        compiler_params=pltpu.CompilerParams(
            vmem_limit_bytes=56 << 20, dimension_semantics=("arbitrary",)
        ),
        cost_estimate=pl.CostEstimate(
            flops=40 * 10**9, bytes_accessed=30 * 10**6, transcendentals=4 * 10**6
        ),
        name="row_attention",
    )(base, *bias_slots, *x_slots, marks, project, mix)


def regroup_kernel(ahead, lead_ref, *refs):
    total_in = len(refs) - ahead
    for k in range(ahead):
        lead = lead_ref[k]
        parts = [refs[m][lead].astype(jnp.float32) for m in range(total_in)]
        refs[total_in + k][...] = jnp.concatenate(parts, axis=0).astype(jnp.bfloat16)


def regroup(lead, slots):
    total_out, count, pairs = slots[0].shape
    return pl.pallas_call(
        functools.partial(regroup_kernel, total_out),
        in_specs=[pl.BlockSpec(memory_space=pltpu.SMEM)]
        + [pl.BlockSpec(memory_space=pltpu.VMEM)] * len(slots),
        out_specs=[pl.BlockSpec(memory_space=pltpu.VMEM)] * total_out,
        out_shape=[jax.ShapeDtypeStruct((len(slots) * count, pairs), jnp.bfloat16)] * total_out,
        compiler_params=pltpu.CompilerParams(vmem_limit_bytes=40 << 20),
        name="regroup",
    )(lead, *slots)


def triangle_kernel(total_rows, total_cols, *refs):
    base_ref = refs[0]
    slots = refs[1 : 1 + total_rows]
    outs = refs[1 + total_rows : 1 + total_rows + total_cols]
    stack, tiles, crossed = refs[1 + total_rows + total_cols :]
    pairs = outs[0].shape[2]
    share = outs[0].shape[1]
    residues = tiles.shape[1] // (2 * share)
    rows = residues // total_rows
    places = residues // total_cols
    bf16 = jnp.bfloat16
    spread_slots(slots, stack, base_ref, tiles, total_cols, places)
    for c in range(share):
        sides = []
        for side in range(2):
            start = (side * share + c) * residues
            sides.append(
                jnp.concatenate(
                    [tiles[t, start : start + residues, :] for t in range(tiles.shape[0])], axis=1
                ).astype(bf16)
            )
        got = lax.dot_general(
            sides[0], sides[1], (((1,), (1,)), ((), ())), preferred_element_type=jnp.float32
        )
        for t in range(tiles.shape[0]):
            last = min(128, residues - t * 128)
            crossed[t, c * residues : (c + 1) * residues, :last] = got[:, t * 128 : t * 128 + last]
    lane = lax.broadcasted_iota(jnp.int32, (share, 128), 1)

    def one(k, carry):
        base = base_ref[k]
        made = [dict() for _ in range(total_cols)]
        for i in range(rows):
            row = [
                crossed[t, pl.ds(base + i, share, stride=residues), :]
                for t in range(tiles.shape[0])
            ]
            for m in range(total_cols):
                come, off = divmod(m * places, 128)
                after = row[come + 1] if come + 1 < len(row) else row[come]
                piece = jnp.concatenate([row[come], after], axis=1)
                to, at = divmod(i * places, 128)
                if at != off:
                    piece = pltpu.roll(piece, (at - off) % 256, 1)
                begin = piece[:, :128]
                if to in made[m]:
                    begin = jnp.where(lane >= at, begin, made[m][to])
                made[m][to] = begin
                if at + places > 128:
                    made[m][to + 1] = piece[:, 128:]
                if at + places >= 128 or i == rows - 1:
                    size = min(128, pairs - to * 128)
                    outs[m][k, :, to * 128 : to * 128 + size] = made[m].pop(to)[:, :size].astype(bf16)
                    if i == rows - 1 and to + 1 in made[m]:
                        size = pairs - (to + 1) * 128
                        outs[m][k, :, (to + 1) * 128 : pairs] = made[m].pop(to + 1)[:, :size].astype(bf16)
        return carry

    lax.fori_loop(0, total_rows, one, 0)


def triangle(base, slots, share, total_cols, residues):
    total_rows = len(slots)
    rows, pairs = slots[0].shape
    padded = -(-residues // 128)
    wide = -(-pairs // 128) * 128 + 128
    bf16 = jnp.bfloat16
    return pl.pallas_call(
        functools.partial(triangle_kernel, total_rows, total_cols),
        in_specs=[pl.BlockSpec(memory_space=pltpu.SMEM)]
        + [pl.BlockSpec(memory_space=pltpu.VMEM)] * total_rows,
        out_specs=[pl.BlockSpec(memory_space=pltpu.VMEM)] * total_cols,
        out_shape=[jax.ShapeDtypeStruct((total_rows, share, pairs), bf16)] * total_cols,
        scratch_shapes=[
            pltpu.VMEM((total_rows, rows, wide), bf16),
            pltpu.VMEM((padded, 2 * share * residues, 128), jnp.float32),
            pltpu.VMEM((padded, share * residues, 128), jnp.float32),
        ],
        compiler_params=pltpu.CompilerParams(vmem_limit_bytes=56 << 20),
        cost_estimate=pl.CostEstimate(
            flops=10 * 10**9, bytes_accessed=8 * 10**6, transcendentals=0
        ),
        name="triangle",
    )(base, *slots)


def finish_kernel(total_rows, *refs):
    slots = refs[:total_rows]
    high_ref, z_ref, valve_ref, exit_ref, out_ref = refs[total_rows:]
    pairs = out_ref.shape[0]
    chunk = 512
    for first in range(0, pairs, chunk):
        last = min(first + chunk, pairs)
        crossed = jnp.concatenate(
            [s[:, first:last].astype(jnp.float32) for s in slots], axis=0
        )
        centred = crossed - jnp.mean(crossed, axis=0, keepdims=True)
        spread = jnp.mean(centred * centred, axis=0, keepdims=True)
        normed = (centred * lax.rsqrt(spread + norm_eps)).astype(jnp.bfloat16)
        projected = lax.dot_general(
            normed, exit_ref[...], (((0,), (0,)), ((), ())), preferred_element_type=jnp.float32
        )
        gate = jax.nn.sigmoid(
            jnp.dot(high_ref[first:last, :], valve_ref[...], preferred_element_type=jnp.float32)
        )
        out_ref[first:last, :] = (z_ref[first:last, :] + gate * projected).astype(jnp.bfloat16)


def finish(slots, high, z_one, valve, exit_w):
    return pl.pallas_call(
        functools.partial(finish_kernel, len(slots)),
        out_shape=jax.ShapeDtypeStruct(high.shape, jnp.bfloat16),
        compiler_params=pltpu.CompilerParams(vmem_limit_bytes=40 << 20),
        name="pair_finish",
    )(*slots, high, z_one, valve, exit_w)


def place_kernel(start_ref, *refs):
    out = refs[-1]
    for m, slot in enumerate(refs[:-1]):
        out[pl.ds(start_ref[m], slot.shape[0])] = slot[...]


def place_slots(starts, slots):
    total = len(slots)
    shape = (total * slots[0].shape[0],) + slots[0].shape[1:]
    return pl.pallas_call(
        place_kernel,
        in_specs=[pl.BlockSpec(memory_space=pltpu.SMEM)]
        + [pl.BlockSpec(memory_space=pltpu.VMEM)] * total,
        out_specs=pl.BlockSpec(memory_space=pltpu.VMEM),
        out_shape=jax.ShapeDtypeStruct(shape, slots[0].dtype),
        compiler_params=pltpu.CompilerParams(vmem_limit_bytes=40 << 20),
        name="place_sequences",
    )(starts, *slots)


def shards(
    homolog_activations,
    coupling_activations,
    homolog_existence_marks,
    observed_peptide_marks,
    peptide_ordinals,
    strand_membership,
    distance_ordinal_vectors,
    coupling_score_mapping,
    question_mapping_weights,
    address_payload_mapping,
    logistic_valve_mapping,
    mixture_exit_mapping,
    twofold_covariance_mapping,
    covariance_exit_mapping,
    triad_opening_mappings,
    triad_valve_mapping,
    triad_exit_mapping,
):
    row_total = lax.axis_size("row")
    col_total = lax.axis_size("col")
    group_ratio = row_total // col_total
    devices = row_total * col_total
    row_place = lax.axis_index("row")
    col_place = lax.axis_index("col")
    tile_rows = coupling_activations.shape[0]
    block_columns = coupling_activations.shape[1]
    number_of_homologs = homolog_activations.shape[0]
    residues = row_total * tile_rows
    heads = coupling_score_mapping.shape[1]
    breadth = question_mapping_weights.shape[1]
    head_breadth = breadth // heads
    opm = twofold_covariance_mapping.shape[1] // 2
    tri_width = triad_exit_mapping.shape[0]
    pair_width = coupling_activations.shape[2]
    own_seqs = number_of_homologs // col_total
    share = tri_width // devices
    row_first = row_place * tile_rows
    col_first = col_place * block_columns
    bf16 = jnp.bfloat16

    marks = homolog_existence_marks.astype(jnp.float32)
    left, right = opm_operands(homolog_activations, marks, twofold_covariance_mapping)
    right_slots = collect(right, "row")
    left_slots_z = jnp.stack(collect(left, "col"))
    blocks = (left.shape[0] - 1) // group_ratio
    left_pieces = []
    for k in range(row_total):
        target = row_place ^ k
        slot = (target // group_ratio) ^ col_place
        mine = lax.dynamic_index_in_dim(left_slots_z, slot, 0, keepdims=False)
        part = lax.dynamic_slice_in_dim(mine, target % group_ratio * blocks, blocks, 0)
        left_pieces.append(jnp.concatenate([part, mine[-1:]], axis=0))
    left_slots = swap(left_pieces, "row")

    x_slots = exchange(
        homolog_activations.reshape(col_total, own_seqs, block_columns, -1), "col"
    )
    own_marks = lax.dynamic_slice_in_dim(left_slots_z[:, -1], col_place * own_seqs, own_seqs, 1)
    own_marks = jnp.swapaxes(own_marks[:, :, :block_columns], 0, 1).reshape(own_seqs, 1, residues)
    padded = -(-residues // 128) * 128
    own_marks = jnp.pad(own_marks.astype(jnp.float32), ((0, 0), (0, 0), (0, padded - residues)))

    lanes = 128
    spots = jnp.stack(
        [
            lax.dynamic_slice_in_dim(peptide_ordinals, row_first, tile_rows),
            lax.dynamic_slice_in_dim(strand_membership, row_first, tile_rows),
            jnp.full((tile_rows,), row_place % group_ratio * tile_rows, jnp.int32),
        ]
    )
    place = jnp.pad(
        jnp.stack(
            [
                lax.dynamic_slice_in_dim(peptide_ordinals, col_first, block_columns),
                lax.dynamic_slice_in_dim(strand_membership, col_first, block_columns),
            ]
        ),
        ((0, 6), (0, lanes - block_columns)),
    )
    exit_t = covariance_exit_mapping.reshape(opm, opm, pair_width).transpose(2, 1, 0)
    exit_t = exit_t.reshape(pair_width, opm * opm)
    near_t = jnp.pad(
        distance_ordinal_vectors, ((0, lanes - distance_ordinal_vectors.shape[0]), (0, 0))
    ).T
    open_t = triad_opening_mappings.reshape(pair_width, 2, 2, row_total, col_total, share)
    open_t = open_t.transpose(2, 4, 3, 1, 5, 0)
    open_t = jnp.concatenate(
        [
            lax.dynamic_slice_in_dim(open_t, col_place ^ m, 1, 1)
            for m in range(col_total)
        ],
        axis=1,
    ).reshape(4 * tri_width, pair_width)
    score_t = coupling_score_mapping.T
    live_rows = lax.dynamic_slice_in_dim(observed_peptide_marks, row_first, tile_rows)
    live_cols = lax.dynamic_slice_in_dim(observed_peptide_marks, col_first, block_columns)
    live = (live_rows[:, None] * live_cols[None, :]).astype(jnp.float32).reshape(1, -1)
    z_one, ln_tri, bias_flat, *side_pieces = pair_stage(
        left_slots, right_slots, coupling_activations, spots, place, exit_t, near_t, open_t,
        score_t, live, col_total,
    )

    row_ids = row_place ^ jnp.arange(row_total, dtype=jnp.int32)
    col_ids = col_place ^ jnp.arange(col_total, dtype=jnp.int32)
    base = (row_ids // group_ratio ^ col_place) * block_columns + row_ids % group_ratio * tile_rows
    bias_part = jnp.concatenate(collect(bias_flat, "col"), axis=0)
    side_slots = swap(side_pieces, "col")
    bias_slots = collect(bias_part, "row")
    side_slots = swap(regroup(row_ids, side_slots), "row")

    project = jnp.concatenate(
        [question_mapping_weights, address_payload_mapping, logistic_valve_mapping], axis=1
    )
    own_after = attend(base, bias_slots, x_slots, own_marks, project, mixture_exit_mapping)
    after_slots = swap(own_after, "col")
    homologs_after = place_slots(col_ids * own_seqs, after_slots)

    crossed = triangle(base, side_slots, share, col_total, residues)
    crossed = swap(crossed, "col")
    crossed = swap(regroup(jnp.arange(row_total, dtype=jnp.int32), crossed), "row")
    exit_w = triad_exit_mapping.reshape(row_total, col_total, share, pair_width)
    exit_w = exit_w[row_ids][:, col_ids].reshape(tri_width, pair_width)
    couplings_after = finish(crossed, ln_tri, z_one, triad_valve_mapping, exit_w)
    return (homologs_after, couplings_after.reshape(coupling_activations.shape))


def solution(mesh):
    placed = (
        P("row", "col", None),
        P("row", "col", None),
        P("row", "col"),
        P(),
        P(),
        P(),
        P(),
        P(),
        P(),
        P(),
        P(),
        P(),
        P(),
        P(),
        P(),
        P(),
        P(),
    )
    return jax.shard_map(
        shards,
        mesh=mesh,
        in_specs=placed,
        out_specs=(P("row", "col", None), P("row", "col", None)),
        check_vma=False,
    )
```

```python
import functools
import math

import jax
import jax.numpy as jnp
from jax import lax
from jax.experimental import pallas as pl
from jax.experimental.pallas import tpu as pltpu
from jax.sharding import PartitionSpec as P

REL_MAX = 32


norm_eps = 1e-05
count_eps = 0.001
masked_score = -1000000000.0


def swap(pieces, axis):
    total = len(pieces)
    return [pieces[0]] + [
        lax.ppermute(pieces[k], axis, [(i, i ^ k) for i in range(total)]) for k in range(1, total)
    ]


def collect(block, axis):
    return swap([block] * lax.axis_size(axis), axis)


def exchange(pieces, axis):
    me = lax.axis_index(axis)
    total = lax.axis_size(axis)
    return swap(
        [lax.dynamic_index_in_dim(pieces, me ^ k, 0, keepdims=False) for k in range(total)], axis
    )


def in_order(slots, axis):
    me = lax.axis_index(axis)
    stacked = jnp.stack(slots)
    return jnp.stack(
        [
            lax.dynamic_index_in_dim(stacked, me ^ k, 0, keepdims=False)
            for k in range(len(slots))
        ]
    )


def zscore_transform(inputs):
    inputs = inputs.astype(jnp.float32)
    centred = inputs - jnp.mean(inputs, axis=-1, keepdims=True)
    spread = jnp.mean(centred * centred, axis=-1, keepdims=True)
    return centred * lax.rsqrt(spread + norm_eps)


def regrouped_covariance(operand, weights):
    batch_shape = operand.shape[:-1]
    result = jnp.dot(
        operand.reshape(-1, operand.shape[-1]), weights, preferred_element_type=jnp.float32
    )
    return result.reshape(batch_shape + (weights.shape[-1],))


def position_bins(index_rows, index_cols, chain_rows, chain_cols):
    offset = jnp.clip(index_rows[:, None] - index_cols[None, :] + REL_MAX, 0, 2 * REL_MAX)
    return jnp.where(chain_rows[:, None] == chain_cols[None, :], offset, 2 * REL_MAX + 1)


def operand_kernel(x_ref, marks_ref, spread_ref, wl_ref, wr_ref, left_ref, right_ref, ln, side, acc):
    seqs, places, width = x_ref.shape
    groups = left_ref.shape[0] - 1
    rights = right_ref.shape[0] - 1
    lanes = left_ref.shape[2]
    per = places // groups
    for s in range(seqs):
        own = zscore_transform(x_ref[s])
        for h in range(width // 128):
            ln[h, s * places : (s + 1) * places, :] = own[:, h * 128 : (h + 1) * 128]
    marks = marks_ref[...]
    for s in range(seqs):
        own = jnp.concatenate(
            [ln[h, s * places : (s + 1) * places, :] for h in range(width // 128)], axis=1
        )
        got = lax.dot_general(
            wr_ref[...], own.astype(jnp.bfloat16), (((1,), (1,)), ((), ())),
            preferred_element_type=jnp.float32,
        )
        got = got * marks[s : s + 1, :]
        side[pl.ds(s, rights, stride=seqs), :] = jnp.concatenate(
            [got, jnp.zeros((rights, lanes - places), jnp.float32)], axis=1
        )
    right_ref[:rights] = side[...].reshape(rights, seqs, lanes).astype(jnp.bfloat16)
    for q in range(per):
        for g in range(groups):
            for h in range(width // 128):
                acc[g * seqs : (g + 1) * seqs, h * 128 : (h + 1) * 128] = ln[
                    h, pl.ds(g * per + q, seqs, stride=places), :
                ]
        part = jnp.dot(
            acc[...].astype(jnp.bfloat16), wl_ref[q], preferred_element_type=jnp.float32
        )
        total = part if q == 0 else total + part
    spread = jnp.dot(
        marks.astype(jnp.bfloat16), spread_ref[...], preferred_element_type=jnp.float32
    )
    for g in range(groups):
        left_ref[g] = (
            total[g * seqs : (g + 1) * seqs] * spread[:, g * lanes : (g + 1) * lanes]
        ).astype(jnp.bfloat16)
    block = jnp.zeros((seqs, lanes), jnp.float32)
    side[:seqs, :] = block
    side[:seqs, :places] = marks
    left_ref[groups] = side[:seqs, :].astype(jnp.bfloat16)
    right_ref[rights] = side[:seqs, :].astype(jnp.bfloat16)


def opm_operands(x, marks, mapping):
    seqs, places, width = x.shape
    opm = mapping.shape[1] // 2
    lanes = 128
    per = lanes // opm
    groups = places // per
    wl = jnp.stack(
        [
            jnp.pad(mapping[:, :opm], ((0, 0), (q * opm, lanes - (q + 1) * opm)))
            for q in range(per)
        ]
    )
    wr = mapping[:, opm:].T
    spread = jnp.repeat(jnp.eye(places, dtype=jnp.bfloat16), opm, axis=1)
    return pl.pallas_call(
        operand_kernel,
        out_shape=(
            jax.ShapeDtypeStruct((groups + 1, seqs, lanes), jnp.bfloat16),
            jax.ShapeDtypeStruct((opm + 1, seqs, lanes), jnp.bfloat16),
        ),
        scratch_shapes=[
            pltpu.VMEM((width // 128, seqs * places, 128), jnp.float32),
            pltpu.VMEM((opm * seqs, lanes), jnp.float32),
            pltpu.VMEM((groups * seqs, width), jnp.float32),
        ],
        compiler_params=pltpu.CompilerParams(vmem_limit_bytes=40 << 20),
        name="outer_operands",
    )(x, marks, spread, wl, wr)


def pair_kernel(total_rows, total_cols, *refs):
    spots = refs[0]
    rows_in = refs[1:3]
    cols_in = refs[3:5]
    pair_ref, place_ref, exit_ref, near_ref, open_ref, score_ref, live_ref = refs[5:12]
    outs = refs[12:]
    z_ref, high_ref, bias_ref = outs[:3]
    side_refs = outs[3 : 3 + total_cols]
    given_ref = outs[3 + total_cols]
    left, right, prod, counts, low = outs[4 + total_cols :]
    step = pl.program_id(0)
    group, places, width = pair_ref.shape
    seqs = rows_in[0].shape[1]
    lanes = 128
    chips = total_rows // 2
    opm = cols_in[0].shape[0] // chips - 1
    sent = rows_in[0].shape[0] // chips
    blocks = left.shape[0]
    bf16 = jnp.bfloat16

    @pl.when(step == 0)
    def _():
        mark_rows, mark_cols = [], []
        for k in range(total_rows):
            half, chip = k % 2, k // 2
            for g in range(blocks):
                left[g, k * seqs : (k + 1) * seqs, :] = rows_in[half][
                    chip * sent + spots[3, 0] * blocks + g
                ]
            for e in range(opm):
                right[k * seqs : (k + 1) * seqs, e * lanes : (e + 1) * lanes] = cols_in[half][
                    chip * (opm + 1) + e
                ]
            mark_rows.append(rows_in[half][chip * sent + sent - 1])
            mark_cols.append(cols_in[half][chip * (opm + 1) + opm])
        mark_rows = jnp.concatenate(mark_rows, axis=0)
        mark_cols = jnp.concatenate(mark_cols, axis=0)
        counts[...] = lax.dot_general(
            mark_rows, mark_cols, (((0,), (0,)), ((), ())), preferred_element_type=jnp.float32
        )

    grid_left = left[step]
    half = opm // 2
    for part in range(2):
        got = lax.dot_general(
            grid_left, right[:, part * half * lanes : (part + 1) * half * lanes],
            (((0,), (0,)), ((), ())), preferred_element_type=jnp.float32,
        ).astype(bf16)
        for e in range(half):
            for i in range(group):
                prod[
                    (part * half + e) * opm : (part * half + e + 1) * opm,
                    i * lanes : (i + 1) * lanes,
                ] = got[i * opm : (i + 1) * opm, e * lanes : (e + 1) * lanes]
    mixed = jnp.dot(exit_ref[...], prod[...], preferred_element_type=jnp.float32)
    pos_cols = place_ref[0:1, :]
    chain_cols = place_ref[1:2, :]
    bins, amount = [], []
    for i in range(group):
        here = step * group + i
        offset = jnp.clip(spots[0, here] - pos_cols + REL_MAX, 0, 2 * REL_MAX)
        bins.append(jnp.where(chain_cols == spots[1, here], offset, 2 * REL_MAX + 1))
        amount.append(counts[pl.ds(spots[2, 0] + here, 1), :])
    bins = jnp.concatenate(bins, axis=1)
    amount = jnp.concatenate(amount, axis=1)
    one_hot = (
        lax.broadcasted_iota(jnp.int32, (near_ref.shape[1], group * lanes), 0) == bins
    )
    one_hot = jnp.where(one_hot, 1.0, 0.0).astype(bf16)
    near = jnp.dot(near_ref[...], one_hot, preferred_element_type=jnp.float32)
    update = jnp.transpose(mixed / (count_eps + amount) + near)
    z = jnp.concatenate(
        [
            pair_ref[i].astype(jnp.float32) + update[i * lanes : i * lanes + places]
            for i in range(group)
        ],
        axis=0,
    )
    z_ref[...] = z
    ln = zscore_transform(z)
    high = ln.astype(bf16)
    start = pl.multiple_of(step * (group * places), 16)
    high_ref[pl.ds(start, group * places), :] = high
    low[pl.ds(start, group * places), :] = (ln - high.astype(jnp.float32)).astype(bf16)

    @pl.when(step == pl.num_programs(0) - 1)
    def _():
        pairs = high_ref.shape[0]
        chunk = 512
        transposed = (((1,), (1,)), ((), ()))
        half_rows = open_ref.shape[0] // 2
        each = half_rows // total_cols // 2
        count = each // chips
        for first in range(0, pairs, chunk):
            last = min(first + chunk, pairs)
            ours = high_ref[first:last, :]
            bias = lax.dot_general(
                score_ref[...], ours, transposed, preferred_element_type=jnp.float32
            ) + lax.dot_general(
                score_ref[...], low[first:last, :], transposed, preferred_element_type=jnp.float32
            )
            bias_ref[:, first:last] = bias[: bias_ref.shape[0]].astype(bf16)
            opened = lax.dot_general(
                open_ref[...], ours, transposed, preferred_element_type=jnp.float32
            )
            sides = (
                jax.nn.sigmoid(opened[half_rows:]) * opened[:half_rows] * live_ref[:, first:last]
            )
            for m in range(total_cols):
                for r in range(chips):
                    at = m * each + r * count
                    side_refs[m][r, :, first:last] = sides[at : at + count].astype(bf16)
                    at = (total_cols + m) * each + r * count
                    given_ref[m, r, :, first:last] = sides[at : at + count].astype(bf16)


def pair_stage(rows_in, cols_in, pair, spots, place, exit_t, near_t, open_t, score_t, live, total_rows, total_cols):
    tile_rows, places, width = pair.shape
    sent, seqs, lanes = rows_in[0].shape
    chips = total_rows // 2
    blocks = (sent // chips - 1) // 2
    group = tile_rows // blocks
    opm = cols_in[0].shape[0] // chips - 1
    pairs = tile_rows * places
    count = open_t.shape[0] // 2 // total_cols // total_rows
    every = total_rows * seqs

    def whole(a):
        return pl.BlockSpec(a.shape, lambda g, n=a.ndim: (0,) * n)

    def whole_out(shape):
        return pl.BlockSpec(shape, lambda g, n=len(shape): (0,) * n)

    ins = list(rows_in) + list(cols_in)
    rest = [place, exit_t, near_t, open_t, score_t, live]
    bf16 = jnp.bfloat16
    outs = [
        jax.ShapeDtypeStruct((pairs, width), jnp.float32),
        jax.ShapeDtypeStruct((pairs, width), bf16),
        jax.ShapeDtypeStruct((score_t.shape[0], pairs), bf16),
    ] + [jax.ShapeDtypeStruct((chips, count, pairs), bf16)] * total_cols
    outs.append(jax.ShapeDtypeStruct((total_cols, chips, count, pairs), bf16))
    return pl.pallas_call(
        functools.partial(pair_kernel, total_rows, total_cols),
        grid=(blocks,),
        in_specs=[pl.BlockSpec(memory_space=pltpu.SMEM)]
        + [whole(a) for a in ins]
        + [pl.BlockSpec((group, places, width), lambda g: (g, 0, 0))]
        + [whole(a) for a in rest],
        out_specs=[pl.BlockSpec((group * places, width), lambda g: (g, 0))]
        + [whole_out(o.shape) for o in outs[1:]],
        out_shape=outs,
        scratch_shapes=[
            pltpu.VMEM((blocks, every, lanes), bf16),
            pltpu.VMEM((every, opm * lanes), bf16),
            pltpu.VMEM((opm * opm, group * lanes), bf16),
            pltpu.VMEM((lanes, lanes), jnp.float32),
            pltpu.VMEM((pairs, width), bf16),
        ],
        compiler_params=pltpu.CompilerParams(
            vmem_limit_bytes=56 << 20, dimension_semantics=("arbitrary",)
        ),
        cost_estimate=pl.CostEstimate(
            flops=20 * 10**9, bytes_accessed=16 * 10**6, transcendentals=10**6
        ),
        name="pair_update",
    )(spots, *ins, pair, *rest)


def spread_slots(slots, stack, base_ref, tiles, total_cols, places):
    total, high, wide = stack.shape
    pairs = slots[0].shape[1]
    count = high // total_cols
    rows = pairs // places
    residues = rows * total
    lane = lax.broadcasted_iota(jnp.int32, (count, 128), 1)
    for k in range(total):
        slot, at = k % len(slots), k // len(slots) * high
        stack[k, :, :pairs] = slots[slot][at : at + high]

    def one(k, carry):
        base = base_ref[k]
        for i in range(rows):
            first = i * places // 128 * 128
            off = i * places - first
            window = stack[k, :, first : first + 256].astype(jnp.float32)
            made = [None] * tiles.shape[0]
            for c in range(total_cols):
                to, at = divmod(c * places, 128)
                piece = window[c * count : (c + 1) * count]
                if at != off:
                    piece = pltpu.roll(piece, (at - off) % 256, 1)
                begin = piece[:, :128]
                made[to] = begin if made[to] is None else jnp.where(lane >= at, begin, made[to])
                if at + places > 128:
                    made[to + 1] = piece[:, 128:]
            kept = residues - 128 * (len(made) - 1)
            made[-1] = jnp.where(lane < kept, made[-1], 0.0)
            for t, tile in enumerate(made):
                tiles[t, pl.ds(base + i, count, stride=residues), :] = tile
        return carry

    lax.fori_loop(0, total, one, 0)


def attention_kernel(halves, total_cols, *refs):
    base_ref = refs[0]
    bias_in = refs[1 : 1 + halves]
    x_in = refs[1 + halves : 1 + halves + total_cols]
    mark_ref, project_ref, mix_ref = refs[1 + halves + total_cols : 4 + halves + total_cols]
    outs = refs[4 + halves + total_cols : 4 + halves + 2 * total_cols]
    stack, tiles, mixed = refs[4 + halves + 2 * total_cols :]
    places, width = x_in[0].shape[1:]
    residues = places * total_cols
    heads = stack.shape[1] // total_cols
    each = width // heads
    group = 128 // each
    padded = tiles.shape[0] * 128
    bf16 = jnp.bfloat16
    transposed = (((1,), (1,)), ((), ()))
    chunk = 176

    @pl.when(pl.program_id(0) == 0)
    def _():
        spread_slots(bias_in, stack, base_ref, tiles, total_cols, places)

    x = jnp.concatenate([r[0].astype(jnp.float32) for r in x_in], axis=0)
    made = jnp.dot(
        zscore_transform(x).astype(bf16), project_ref[...], preferred_element_type=jnp.float32
    )
    present = mark_ref[0] > 0.0
    lane = lax.broadcasted_iota(jnp.int32, (1, 128), 1)
    scale = 1.0 / math.sqrt(each)
    filler = jnp.zeros((padded - residues, 128), bf16)
    for h0 in range(0, heads, group):
        at = h0 * each
        queries = made[:, at : at + 128].astype(bf16)
        keys = made[:, width + at : width + at + 128].astype(bf16)
        values = made[:, 2 * width + at : 2 * width + at + 128].astype(bf16)
        keys = jnp.concatenate([keys, filler], axis=0)
        values = jnp.concatenate([values, filler], axis=0)
        for first in range(0, residues, chunk):
            total = jnp.zeros((chunk, 128), jnp.float32)
            for h in range(group):
                ours = (lane >= h * each) & (lane < (h + 1) * each)
                own_keys = jnp.where(ours, keys, jnp.zeros_like(keys))
                own_values = jnp.where(ours, values, jnp.zeros_like(values))
                scores = lax.dot_general(
                    queries[first : first + chunk], own_keys, transposed,
                    preferred_element_type=jnp.float32,
                )
                start = (h0 + h) * residues + first
                bias = jnp.concatenate(
                    [tiles[t, start : start + chunk, :] for t in range(tiles.shape[0])], axis=1
                )
                scores = jnp.where(present, scores * scale + bias, masked_score)
                terms = jnp.exp(scores - jnp.max(scores, axis=1, keepdims=True))
                weight = jnp.sum(terms, axis=1, keepdims=True)
                got = jnp.dot(terms.astype(bf16), own_values, preferred_element_type=jnp.float32)
                total = total + got / weight
            gate = jax.nn.sigmoid(made[first : first + chunk, 3 * width + at : 3 * width + at + 128])
            mixed[first : first + chunk, at : at + 128] = (gate * total).astype(bf16)
    after = x + jnp.dot(mixed[...], mix_ref[...], preferred_element_type=jnp.float32)
    for m in range(total_cols):
        outs[m][0] = after[m * places : (m + 1) * places].astype(bf16)


def attend(base, bias_slots, x_slots, marks, project, mix):
    total_rows, total_cols = base.shape[0], len(x_slots)
    seqs, places, width = x_slots[0].shape
    residues = places * total_cols
    padded = -(-residues // 128) * 128
    rows, pairs = bias_slots[0].shape
    rows = rows * len(bias_slots) // total_rows
    heads = rows // total_cols
    wide = -(-pairs // 128) * 128 + 128

    def whole(a):
        return pl.BlockSpec(a.shape, lambda s, n=a.ndim: (0,) * n)

    per_seq = pl.BlockSpec((1, places, width), lambda s: (s, 0, 0))
    bf16 = jnp.bfloat16
    return pl.pallas_call(
        functools.partial(attention_kernel, len(bias_slots), total_cols),
        grid=(seqs,),
        in_specs=[pl.BlockSpec(memory_space=pltpu.SMEM)]
        + [whole(a) for a in bias_slots]
        + [per_seq] * total_cols
        + [pl.BlockSpec((1, 1, padded), lambda s: (s, 0, 0)), whole(project), whole(mix)],
        out_specs=[per_seq] * total_cols,
        out_shape=[jax.ShapeDtypeStruct((seqs, places, width), bf16)] * total_cols,
        scratch_shapes=[
            pltpu.VMEM((total_rows, rows, wide), bf16),
            pltpu.VMEM((padded // 128, heads * residues, 128), jnp.float32),
            pltpu.VMEM((residues, width), bf16),
        ],
        compiler_params=pltpu.CompilerParams(
            vmem_limit_bytes=56 << 20, dimension_semantics=("arbitrary",)
        ),
        cost_estimate=pl.CostEstimate(
            flops=40 * 10**9, bytes_accessed=30 * 10**6, transcendentals=4 * 10**6
        ),
        name="row_attention",
    )(base, *bias_slots, *x_slots, marks, project, mix)


def regroup_kernel(ahead, lead_ref, *refs):
    total_in = len(refs) - ahead
    for k in range(ahead):
        lead = lead_ref[k]
        parts = [refs[m][lead].astype(jnp.float32) for m in range(total_in)]
        refs[total_in + k][...] = jnp.concatenate(parts, axis=0).astype(jnp.bfloat16)


def regroup(lead, slots):
    total_out, count, pairs = slots[0].shape
    return pl.pallas_call(
        functools.partial(regroup_kernel, total_out),
        in_specs=[pl.BlockSpec(memory_space=pltpu.SMEM)]
        + [pl.BlockSpec(memory_space=pltpu.VMEM)] * len(slots),
        out_specs=[pl.BlockSpec(memory_space=pltpu.VMEM)] * total_out,
        out_shape=[jax.ShapeDtypeStruct((len(slots) * count, pairs), jnp.bfloat16)] * total_out,
        compiler_params=pltpu.CompilerParams(vmem_limit_bytes=40 << 20),
        name="regroup",
    )(lead, *slots)


def stack_kernel(*refs):
    count = refs[0].shape[0]
    for n, ref in enumerate(refs[:-1]):
        refs[-1][n * count : (n + 1) * count] = ref[...]


def stack_blocks(blocks):
    shape = (len(blocks) * blocks[0].shape[0],) + blocks[0].shape[1:]
    return pl.pallas_call(
        stack_kernel,
        out_shape=jax.ShapeDtypeStruct(shape, blocks[0].dtype),
        compiler_params=pltpu.CompilerParams(vmem_limit_bytes=40 << 20),
        name="stack_blocks",
    )(*blocks)


def triangle_kernel(total_rows, total_cols, *refs):
    base_ref = refs[0]
    slots = refs[1 : 1 + total_rows]
    outs = refs[1 + total_rows : 1 + total_rows + total_cols]
    stack, tiles, crossed = refs[1 + total_rows + total_cols :]
    pairs = outs[0].shape[2]
    share = outs[0].shape[1]
    residues = tiles.shape[1] // (2 * share)
    rows = residues // total_rows
    places = residues // total_cols
    bf16 = jnp.bfloat16
    spread_slots(slots, stack, base_ref, tiles, total_cols, places)
    for c in range(share):
        sides = []
        for side in range(2):
            start = (side * share + c) * residues
            sides.append(
                jnp.concatenate(
                    [tiles[t, start : start + residues, :] for t in range(tiles.shape[0])], axis=1
                ).astype(bf16)
            )
        got = lax.dot_general(
            sides[0], sides[1], (((1,), (1,)), ((), ())), preferred_element_type=jnp.float32
        )
        for t in range(tiles.shape[0]):
            last = min(128, residues - t * 128)
            crossed[t, c * residues : (c + 1) * residues, :last] = got[:, t * 128 : t * 128 + last]
    lane = lax.broadcasted_iota(jnp.int32, (share, 128), 1)

    def one(k, carry):
        base = base_ref[k]
        made = [dict() for _ in range(total_cols)]
        for i in range(rows):
            row = [
                crossed[t, pl.ds(base + i, share, stride=residues), :]
                for t in range(tiles.shape[0])
            ]
            for m in range(total_cols):
                come, off = divmod(m * places, 128)
                after = row[come + 1] if come + 1 < len(row) else row[come]
                piece = jnp.concatenate([row[come], after], axis=1)
                to, at = divmod(i * places, 128)
                if at != off:
                    piece = pltpu.roll(piece, (at - off) % 256, 1)
                begin = piece[:, :128]
                if to in made[m]:
                    begin = jnp.where(lane >= at, begin, made[m][to])
                made[m][to] = begin
                if at + places > 128:
                    made[m][to + 1] = piece[:, 128:]
                if at + places >= 128 or i == rows - 1:
                    size = min(128, pairs - to * 128)
                    outs[m][k, :, to * 128 : to * 128 + size] = made[m].pop(to)[:, :size].astype(bf16)
                    if i == rows - 1 and to + 1 in made[m]:
                        size = pairs - (to + 1) * 128
                        outs[m][k, :, (to + 1) * 128 : pairs] = made[m].pop(to + 1)[:, :size].astype(bf16)
        return carry

    lax.fori_loop(0, total_rows, one, 0)


def triangle(base, slots, share, total_cols, residues):
    total_rows = len(slots)
    rows, pairs = slots[0].shape
    padded = -(-residues // 128)
    wide = -(-pairs // 128) * 128 + 128
    bf16 = jnp.bfloat16
    return pl.pallas_call(
        functools.partial(triangle_kernel, total_rows, total_cols),
        in_specs=[pl.BlockSpec(memory_space=pltpu.SMEM)]
        + [pl.BlockSpec(memory_space=pltpu.VMEM)] * total_rows,
        out_specs=[pl.BlockSpec(memory_space=pltpu.VMEM)] * total_cols,
        out_shape=[jax.ShapeDtypeStruct((total_rows, share, pairs), bf16)] * total_cols,
        scratch_shapes=[
            pltpu.VMEM((total_rows, rows, wide), bf16),
            pltpu.VMEM((padded, 2 * share * residues, 128), jnp.float32),
            pltpu.VMEM((padded, share * residues, 128), jnp.float32),
        ],
        compiler_params=pltpu.CompilerParams(vmem_limit_bytes=56 << 20),
        cost_estimate=pl.CostEstimate(
            flops=10 * 10**9, bytes_accessed=8 * 10**6, transcendentals=0
        ),
        name="triangle",
    )(base, *slots)


def finish_kernel(total_rows, *refs):
    lead_ref = refs[0]
    slots = refs[1 : 1 + total_rows]
    high_ref, z_ref, valve_ref, exit_ref, out_ref = refs[1 + total_rows :]
    pairs = out_ref.shape[0]
    chunk = 512
    exits = jnp.concatenate(
        [exit_ref[lead_ref[n]].astype(jnp.float32) for n in range(exit_ref.shape[0])], axis=0
    ).astype(jnp.bfloat16)
    for first in range(0, pairs, chunk):
        last = min(first + chunk, pairs)
        crossed = jnp.concatenate(
            [s[:, first:last].astype(jnp.float32) for s in slots], axis=0
        )
        centred = crossed - jnp.mean(crossed, axis=0, keepdims=True)
        spread = jnp.mean(centred * centred, axis=0, keepdims=True)
        normed = (centred * lax.rsqrt(spread + norm_eps)).astype(jnp.bfloat16)
        projected = lax.dot_general(
            normed, exits, (((0,), (0,)), ((), ())), preferred_element_type=jnp.float32
        )
        gate = jax.nn.sigmoid(
            jnp.dot(high_ref[first:last, :], valve_ref[...], preferred_element_type=jnp.float32)
        )
        out_ref[first:last, :] = (z_ref[first:last, :] + gate * projected).astype(jnp.bfloat16)


def finish(lead, slots, high, z_one, valve, exit_w):
    return pl.pallas_call(
        functools.partial(finish_kernel, len(slots)),
        in_specs=[pl.BlockSpec(memory_space=pltpu.SMEM)]
        + [pl.BlockSpec(memory_space=pltpu.VMEM)] * (len(slots) + 4),
        out_specs=pl.BlockSpec(memory_space=pltpu.VMEM),
        out_shape=jax.ShapeDtypeStruct(high.shape, jnp.bfloat16),
        compiler_params=pltpu.CompilerParams(vmem_limit_bytes=40 << 20),
        name="pair_finish",
    )(lead, *slots, high, z_one, valve, exit_w)


def place_kernel(start_ref, *refs):
    out = refs[-1]
    for m, slot in enumerate(refs[:-1]):
        out[pl.ds(start_ref[m], slot.shape[0])] = slot[...]


def place_slots(starts, slots):
    total = len(slots)
    shape = (total * slots[0].shape[0],) + slots[0].shape[1:]
    return pl.pallas_call(
        place_kernel,
        in_specs=[pl.BlockSpec(memory_space=pltpu.SMEM)]
        + [pl.BlockSpec(memory_space=pltpu.VMEM)] * total,
        out_specs=pl.BlockSpec(memory_space=pltpu.VMEM),
        out_shape=jax.ShapeDtypeStruct(shape, slots[0].dtype),
        compiler_params=pltpu.CompilerParams(vmem_limit_bytes=40 << 20),
        name="place_sequences",
    )(starts, *slots)


def shards(
    homolog_activations,
    coupling_activations,
    homolog_existence_marks,
    observed_peptide_marks,
    peptide_ordinals,
    strand_membership,
    distance_ordinal_vectors,
    coupling_score_mapping,
    question_mapping_weights,
    address_payload_mapping,
    logistic_valve_mapping,
    mixture_exit_mapping,
    twofold_covariance_mapping,
    covariance_exit_mapping,
    triad_opening_mappings,
    triad_valve_mapping,
    triad_exit_mapping,
):
    row_total = lax.axis_size("row")
    col_total = lax.axis_size("col")
    group_ratio = row_total // col_total
    devices = row_total * col_total
    row_place = lax.axis_index("row")
    col_place = lax.axis_index("col")
    tile_rows = coupling_activations.shape[0]
    block_columns = coupling_activations.shape[1]
    number_of_homologs = homolog_activations.shape[0]
    residues = row_total * tile_rows
    heads = coupling_score_mapping.shape[1]
    breadth = question_mapping_weights.shape[1]
    head_breadth = breadth // heads
    opm = twofold_covariance_mapping.shape[1] // 2
    tri_width = triad_exit_mapping.shape[0]
    pair_width = coupling_activations.shape[2]
    own_seqs = number_of_homologs // col_total
    share = tri_width // devices
    row_first = row_place * tile_rows
    col_first = col_place * block_columns
    bf16 = jnp.bfloat16

    marks = homolog_existence_marks.astype(jnp.float32)
    left, right = opm_operands(homolog_activations, marks, twofold_covariance_mapping)
    chips = range(0, row_total, 2)

    def over_chips(pieces):
        return [pieces[0]] + [
            lax.ppermute(piece, "row", [(i, i ^ k) for i in range(row_total)])
            for k, piece in zip(chips[1:], pieces[1:])
        ]

    def other_core(block):
        return lax.ppermute(block, "row", [(i, i ^ 1) for i in range(row_total)])

    left_z = collect(left, "col")
    left_stack = jnp.stack(left_z)
    right_even = jnp.concatenate(over_chips([right] * len(chips)), axis=0)
    right_odd = other_core(right_even)
    left_even = jnp.concatenate(
        over_chips(
            [
                lax.dynamic_index_in_dim(
                    left_stack, (row_place ^ k) // group_ratio ^ col_place, 0, keepdims=False
                )
                for k in chips
            ]
        ),
        axis=0,
    )
    left_odd = other_core(left_even)
    operands = [left_even, left_odd, right_even, right_odd]

    operands, x_own = lax.optimization_barrier((operands, homolog_activations))
    x_slots = exchange(x_own.reshape(col_total, own_seqs, block_columns, -1), "col")
    own_marks = lax.dynamic_slice_in_dim(left_stack[:, -1], col_place * own_seqs, own_seqs, 1)
    own_marks = jnp.swapaxes(own_marks[:, :, :block_columns], 0, 1).reshape(own_seqs, 1, residues)
    padded = -(-residues // 128) * 128
    own_marks = jnp.pad(own_marks.astype(jnp.float32), ((0, 0), (0, 0), (0, padded - residues)))

    lanes = 128
    spots = jnp.stack(
        [
            lax.dynamic_slice_in_dim(peptide_ordinals, row_first, tile_rows),
            lax.dynamic_slice_in_dim(strand_membership, row_first, tile_rows),
            jnp.full((tile_rows,), row_place % group_ratio * tile_rows, jnp.int32),
            jnp.full((tile_rows,), row_place % group_ratio, jnp.int32),
        ]
    )
    place = jnp.pad(
        jnp.stack(
            [
                lax.dynamic_slice_in_dim(peptide_ordinals, col_first, block_columns),
                lax.dynamic_slice_in_dim(strand_membership, col_first, block_columns),
            ]
        ),
        ((0, 6), (0, lanes - block_columns)),
    )
    exit_t = covariance_exit_mapping.reshape(opm, opm, pair_width).transpose(2, 1, 0)
    exit_t = exit_t.reshape(pair_width, opm * opm)
    near_t = jnp.pad(
        distance_ordinal_vectors, ((0, lanes - distance_ordinal_vectors.shape[0]), (0, 0))
    ).T
    open_t = triad_opening_mappings.reshape(
        pair_width, 2, 2, row_total // 2, 2, col_total, share
    )
    open_t = open_t.transpose(2, 4, 5, 3, 1, 6, 0)
    open_t = jnp.concatenate(
        [lax.dynamic_slice_in_dim(open_t, row_place % 2 ^ h, 1, 1) for h in range(2)], axis=1
    )
    open_t = jnp.concatenate(
        [lax.dynamic_slice_in_dim(open_t, col_place ^ m, 1, 2) for m in range(col_total)], axis=2
    ).reshape(4 * tri_width, pair_width)
    score_t = coupling_score_mapping.T
    live_rows = lax.dynamic_slice_in_dim(observed_peptide_marks, row_first, tile_rows)
    live_cols = lax.dynamic_slice_in_dim(observed_peptide_marks, col_first, block_columns)
    live = (live_rows[:, None] * live_cols[None, :]).astype(jnp.float32).reshape(1, -1)
    z_one, ln_tri, bias_flat, *kept, given = pair_stage(
        operands[:2], operands[2:], coupling_activations, spots, place, exit_t, near_t, open_t,
        score_t, live, row_total, col_total,
    )
    bias_flat, x_slots = lax.optimization_barrier((bias_flat, x_slots))

    row_ids = row_place ^ jnp.arange(row_total, dtype=jnp.int32)
    col_ids = col_place ^ jnp.arange(col_total, dtype=jnp.int32)
    base = (row_ids // group_ratio ^ col_place) * block_columns + row_ids % group_ratio * tile_rows
    chip_ids = row_ids[::2] // 2
    received = other_core(given)
    bias_part, kept = lax.optimization_barrier((collect(bias_flat, "col"), kept))
    bias_part = stack_blocks(bias_part)
    kept = swap(kept, "col")
    bias_even = stack_blocks(over_chips([bias_part] * len(chips)))
    bias_slots = [bias_even, other_core(bias_even)]
    kept, received = lax.optimization_barrier((kept, received))
    received = swap([received[m] for m in range(col_total)], "col")
    kept = over_chips(regroup(chip_ids, kept))

    project = jnp.concatenate(
        [question_mapping_weights, address_payload_mapping, logistic_valve_mapping], axis=1
    )
    own_after = attend(base, bias_slots, x_slots, own_marks, project, mixture_exit_mapping)

    after_slots = swap(own_after, "col")
    homologs_after = place_slots(col_ids * own_seqs, after_slots)

    received, own_after = lax.optimization_barrier((received, own_after))
    received = over_chips(regroup(chip_ids, received))
    side_slots = [slot for both in zip(kept, received) for slot in both]
    crossed = triangle(base, side_slots, share, col_total, residues)
    crossed, after_slots = lax.optimization_barrier((crossed, after_slots))
    crossed = swap(crossed, "col")
    crossed = swap(regroup(jnp.arange(row_total, dtype=jnp.int32), crossed), "row")
    exit_w = triad_exit_mapping.reshape(devices, share, pair_width)
    lead = (row_ids[:, None] * col_total + col_ids[None, :]).reshape(-1)
    couplings_after = finish(lead, crossed, ln_tri, z_one, triad_valve_mapping, exit_w)
    return (homologs_after, couplings_after.reshape(coupling_activations.shape))


def solution(mesh):
    placed = (
        P("row", "col", None),
        P("row", "col", None),
        P("row", "col"),
        P(),
        P(),
        P(),
        P(),
        P(),
        P(),
        P(),
        P(),
        P(),
        P(),
        P(),
        P(),
        P(),
        P(),
    )
    return jax.shard_map(
        shards,
        mesh=mesh,
        in_specs=placed,
        out_specs=(P("row", "col", None), P("row", "col", None)),
        check_vma=False,
    )
```

```python
import functools
import math

import jax
import jax.numpy as jnp
from jax import lax
from jax.experimental import pallas as pl
from jax.experimental.pallas import tpu as pltpu
from jax.sharding import PartitionSpec as P

REL_MAX = 32


norm_eps = 1e-05
count_eps = 0.001
masked_score = -1000000000.0


def swap(pieces, axis):
    total = len(pieces)
    return [pieces[0]] + [
        lax.ppermute(pieces[k], axis, [(i, i ^ k) for i in range(total)]) for k in range(1, total)
    ]


def collect(block, axis):
    return swap([block] * lax.axis_size(axis), axis)


def exchange(pieces, axis):
    me = lax.axis_index(axis)
    total = lax.axis_size(axis)
    return swap(
        [lax.dynamic_index_in_dim(pieces, me ^ k, 0, keepdims=False) for k in range(total)], axis
    )


def in_order(slots, axis):
    me = lax.axis_index(axis)
    stacked = jnp.stack(slots)
    return jnp.stack(
        [
            lax.dynamic_index_in_dim(stacked, me ^ k, 0, keepdims=False)
            for k in range(len(slots))
        ]
    )


def zscore_transform(inputs):
    inputs = inputs.astype(jnp.float32)
    centred = inputs - jnp.mean(inputs, axis=-1, keepdims=True)
    spread = jnp.mean(centred * centred, axis=-1, keepdims=True)
    return centred * lax.rsqrt(spread + norm_eps)


def regrouped_covariance(operand, weights):
    batch_shape = operand.shape[:-1]
    result = jnp.dot(
        operand.reshape(-1, operand.shape[-1]), weights, preferred_element_type=jnp.float32
    )
    return result.reshape(batch_shape + (weights.shape[-1],))


def position_bins(index_rows, index_cols, chain_rows, chain_cols):
    offset = jnp.clip(index_rows[:, None] - index_cols[None, :] + REL_MAX, 0, 2 * REL_MAX)
    return jnp.where(chain_rows[:, None] == chain_cols[None, :], offset, 2 * REL_MAX + 1)


def operand_kernel(x_ref, marks_ref, spread_ref, wl_ref, wr_ref, left_ref, right_ref, ln, side, acc):
    seqs, places, width = x_ref.shape
    groups = left_ref.shape[0] - 1
    rights = right_ref.shape[0] - 1
    lanes = left_ref.shape[2]
    per = places // groups
    for s in range(seqs):
        own = zscore_transform(x_ref[s])
        for h in range(width // 128):
            ln[h, s * places : (s + 1) * places, :] = own[:, h * 128 : (h + 1) * 128]
    marks = marks_ref[...]
    for s in range(seqs):
        own = jnp.concatenate(
            [ln[h, s * places : (s + 1) * places, :] for h in range(width // 128)], axis=1
        )
        got = lax.dot_general(
            wr_ref[...], own.astype(jnp.bfloat16), (((1,), (1,)), ((), ())),
            preferred_element_type=jnp.float32,
        )
        got = got * marks[s : s + 1, :]
        side[pl.ds(s, rights, stride=seqs), :] = jnp.concatenate(
            [got, jnp.zeros((rights, lanes - places), jnp.float32)], axis=1
        )
    right_ref[:rights] = side[...].reshape(rights, seqs, lanes).astype(jnp.bfloat16)
    for q in range(per):
        for g in range(groups):
            for h in range(width // 128):
                acc[g * seqs : (g + 1) * seqs, h * 128 : (h + 1) * 128] = ln[
                    h, pl.ds(g * per + q, seqs, stride=places), :
                ]
        part = jnp.dot(
            acc[...].astype(jnp.bfloat16), wl_ref[q], preferred_element_type=jnp.float32
        )
        total = part if q == 0 else total + part
    spread = jnp.dot(
        marks.astype(jnp.bfloat16), spread_ref[...], preferred_element_type=jnp.float32
    )
    for g in range(groups):
        left_ref[g] = (
            total[g * seqs : (g + 1) * seqs] * spread[:, g * lanes : (g + 1) * lanes]
        ).astype(jnp.bfloat16)
    block = jnp.zeros((seqs, lanes), jnp.float32)
    side[:seqs, :] = block
    side[:seqs, :places] = marks
    left_ref[groups] = side[:seqs, :].astype(jnp.bfloat16)
    right_ref[rights] = side[:seqs, :].astype(jnp.bfloat16)


def opm_operands(x, marks, mapping):
    seqs, places, width = x.shape
    opm = mapping.shape[1] // 2
    lanes = 128
    per = lanes // opm
    groups = places // per
    wl = jnp.stack(
        [
            jnp.pad(mapping[:, :opm], ((0, 0), (q * opm, lanes - (q + 1) * opm)))
            for q in range(per)
        ]
    )
    wr = mapping[:, opm:].T
    spread = jnp.repeat(jnp.eye(places, dtype=jnp.bfloat16), opm, axis=1)
    return pl.pallas_call(
        operand_kernel,
        out_shape=(
            jax.ShapeDtypeStruct((groups + 1, seqs, lanes), jnp.bfloat16),
            jax.ShapeDtypeStruct((opm + 1, seqs, lanes), jnp.bfloat16),
        ),
        scratch_shapes=[
            pltpu.VMEM((width // 128, seqs * places, 128), jnp.float32),
            pltpu.VMEM((opm * seqs, lanes), jnp.float32),
            pltpu.VMEM((groups * seqs, width), jnp.float32),
        ],
        compiler_params=pltpu.CompilerParams(vmem_limit_bytes=40 << 20),
        name="outer_operands",
    )(x, marks, spread, wl, wr)


def pair_kernel(total_rows, total_cols, *refs):
    spots = refs[0]
    rows_in = refs[1:3]
    cols_in = refs[3:5]
    pair_ref, place_ref, exit_ref, near_ref, open_ref, score_ref, live_ref = refs[5:12]
    outs = refs[12:]
    z_ref, high_ref = outs[:2]
    side_refs = outs[2 : 2 + total_cols]
    given_ref = outs[2 + total_cols]
    left, right, prod, counts, low = outs[3 + total_cols :]
    step = pl.program_id(0)
    group, places, width = pair_ref.shape
    seqs = rows_in[0].shape[1]
    lanes = 128
    chips = total_rows // 2
    opm = cols_in[0].shape[0] // chips - 1
    sent = rows_in[0].shape[0] // chips
    blocks = left.shape[0]
    bf16 = jnp.bfloat16

    @pl.when(step == 0)
    def _():
        mark_rows, mark_cols = [], []
        for k in range(total_rows):
            half, chip = k % 2, k // 2
            for g in range(blocks):
                left[g, k * seqs : (k + 1) * seqs, :] = rows_in[half][
                    chip * sent + spots[3, 0] * blocks + g
                ]
            for e in range(opm):
                right[k * seqs : (k + 1) * seqs, e * lanes : (e + 1) * lanes] = cols_in[half][
                    chip * (opm + 1) + e
                ]
            mark_rows.append(rows_in[half][chip * sent + sent - 1])
            mark_cols.append(cols_in[half][chip * (opm + 1) + opm])
        mark_rows = jnp.concatenate(mark_rows, axis=0)
        mark_cols = jnp.concatenate(mark_cols, axis=0)
        counts[...] = lax.dot_general(
            mark_rows, mark_cols, (((0,), (0,)), ((), ())), preferred_element_type=jnp.float32
        )

    grid_left = left[step]
    half = opm // 2
    for part in range(2):
        got = lax.dot_general(
            grid_left, right[:, part * half * lanes : (part + 1) * half * lanes],
            (((0,), (0,)), ((), ())), preferred_element_type=jnp.float32,
        ).astype(bf16)
        for e in range(half):
            for i in range(group):
                prod[
                    (part * half + e) * opm : (part * half + e + 1) * opm,
                    i * lanes : (i + 1) * lanes,
                ] = got[i * opm : (i + 1) * opm, e * lanes : (e + 1) * lanes]
    mixed = jnp.dot(exit_ref[...], prod[...], preferred_element_type=jnp.float32)
    pos_cols = place_ref[0:1, :]
    chain_cols = place_ref[1:2, :]
    bins, amount = [], []
    for i in range(group):
        here = step * group + i
        offset = jnp.clip(spots[0, here] - pos_cols + REL_MAX, 0, 2 * REL_MAX)
        bins.append(jnp.where(chain_cols == spots[1, here], offset, 2 * REL_MAX + 1))
        amount.append(counts[pl.ds(spots[2, 0] + here, 1), :])
    bins = jnp.concatenate(bins, axis=1)
    amount = jnp.concatenate(amount, axis=1)
    one_hot = (
        lax.broadcasted_iota(jnp.int32, (near_ref.shape[1], group * lanes), 0) == bins
    )
    one_hot = jnp.where(one_hot, 1.0, 0.0).astype(bf16)
    near = jnp.dot(near_ref[...], one_hot, preferred_element_type=jnp.float32)
    update = jnp.transpose(mixed / (count_eps + amount) + near)
    z = jnp.concatenate(
        [
            pair_ref[i].astype(jnp.float32) + update[i * lanes : i * lanes + places]
            for i in range(group)
        ],
        axis=0,
    )
    z_ref[...] = z
    ln = zscore_transform(z)
    high = ln.astype(bf16)
    start = pl.multiple_of(step * (group * places), 16)
    high_ref[pl.ds(start, group * places), :] = high
    low[pl.ds(start, group * places), :] = (ln - high.astype(jnp.float32)).astype(bf16)

    @pl.when(step == pl.num_programs(0) - 1)
    def _():
        pairs = high_ref.shape[0]
        chunk = 512
        transposed = (((1,), (1,)), ((), ()))
        half_rows = open_ref.shape[0] // 2
        each = half_rows // total_cols // 2
        for first in range(0, pairs, chunk):
            last = min(first + chunk, pairs)
            ours = high_ref[first:last, :]
            bias = lax.dot_general(
                score_ref[...], ours, transposed, preferred_element_type=jnp.float32
            ) + lax.dot_general(
                score_ref[...], low[first:last, :], transposed, preferred_element_type=jnp.float32
            )
            opened = lax.dot_general(
                open_ref[...], ours, transposed, preferred_element_type=jnp.float32
            )
            sides = (
                jax.nn.sigmoid(opened[half_rows:]) * opened[:half_rows] * live_ref[:, first:last]
            )
            for m in range(total_cols):
                at = m * each
                side_refs[m][:, first:last] = jnp.concatenate(
                    [sides[at : at + each], bias], axis=0
                ).astype(bf16)
                at = (total_cols + m) * each
                given_ref[m, :, first:last] = sides[at : at + each].astype(bf16)


def pair_stage(rows_in, cols_in, pair, spots, place, exit_t, near_t, open_t, score_t, live, total_rows, total_cols):
    tile_rows, places, width = pair.shape
    sent, seqs, lanes = rows_in[0].shape
    chips = total_rows // 2
    blocks = (sent // chips - 1) // 2
    group = tile_rows // blocks
    opm = cols_in[0].shape[0] // chips - 1
    pairs = tile_rows * places
    each = open_t.shape[0] // 4 // total_cols
    every = total_rows * seqs

    def whole(a):
        return pl.BlockSpec(a.shape, lambda g, n=a.ndim: (0,) * n)

    def whole_out(shape):
        return pl.BlockSpec(shape, lambda g, n=len(shape): (0,) * n)

    ins = list(rows_in) + list(cols_in)
    rest = [place, exit_t, near_t, open_t, score_t, live]
    bf16 = jnp.bfloat16
    outs = [
        jax.ShapeDtypeStruct((pairs, width), jnp.float32),
        jax.ShapeDtypeStruct((pairs, width), bf16),
    ] + [jax.ShapeDtypeStruct((each + score_t.shape[0], pairs), bf16)] * total_cols
    outs.append(jax.ShapeDtypeStruct((total_cols, each, pairs), bf16))
    return pl.pallas_call(
        functools.partial(pair_kernel, total_rows, total_cols),
        grid=(blocks,),
        in_specs=[pl.BlockSpec(memory_space=pltpu.SMEM)]
        + [whole(a) for a in ins]
        + [pl.BlockSpec((group, places, width), lambda g: (g, 0, 0))]
        + [whole(a) for a in rest],
        out_specs=[pl.BlockSpec((group * places, width), lambda g: (g, 0))]
        + [whole_out(o.shape) for o in outs[1:]],
        out_shape=outs,
        scratch_shapes=[
            pltpu.VMEM((blocks, every, lanes), bf16),
            pltpu.VMEM((every, opm * lanes), bf16),
            pltpu.VMEM((opm * opm, group * lanes), bf16),
            pltpu.VMEM((lanes, lanes), jnp.float32),
            pltpu.VMEM((pairs, width), bf16),
        ],
        compiler_params=pltpu.CompilerParams(
            vmem_limit_bytes=56 << 20, dimension_semantics=("arbitrary",)
        ),
        name="pair_update",
    )(spots, *ins, pair, *rest)


def spread_slots(slots, stack, base_ref, tiles, total_cols, places):
    total, high, wide = stack.shape
    pairs = slots[0].shape[1]
    count = high // total_cols
    rows = pairs // places
    residues = rows * total
    lane = lax.broadcasted_iota(jnp.int32, (count, 128), 1)
    for k in range(total):
        slot, at = k % len(slots), k // len(slots) * high
        stack[k, :, :pairs] = slots[slot][at : at + high]

    def one(k, carry):
        base = base_ref[k]
        for i in range(rows):
            first = i * places // 128 * 128
            off = i * places - first
            window = stack[k, :, first : first + 256].astype(jnp.float32)
            made = [None] * tiles.shape[0]
            for c in range(total_cols):
                to, at = divmod(c * places, 128)
                piece = window[c * count : (c + 1) * count]
                if at != off:
                    piece = pltpu.roll(piece, (at - off) % 256, 1)
                begin = piece[:, :128]
                made[to] = begin if made[to] is None else jnp.where(lane >= at, begin, made[to])
                if at + places > 128:
                    made[to + 1] = piece[:, 128:]
            kept = residues - 128 * (len(made) - 1)
            made[-1] = jnp.where(lane < kept, made[-1], 0.0)
            for t, tile in enumerate(made):
                tiles[t, pl.ds(base + i, count, stride=residues), :] = tile
        return carry

    lax.fori_loop(0, total, one, 0)


def layout_kernel(halves, total_cols, places, *refs):
    base_ref = refs[0]
    out_ref, stack, tiles = refs[1 + halves :]
    spread_slots(refs[1 : 1 + halves], stack, base_ref, tiles, total_cols, places)
    out_ref[...] = tiles[...].astype(out_ref.dtype)


def layout_bias(base, bias_slots, total_cols, places):
    total_rows = base.shape[0]
    rows, pairs = bias_slots[0].shape
    rows = rows * len(bias_slots) // total_rows
    residues = places * total_cols
    heads = rows // total_cols
    shape = (-(-residues // 128), heads * residues, 128)
    wide = -(-pairs // 128) * 128 + 128
    return pl.pallas_call(
        functools.partial(layout_kernel, len(bias_slots), total_cols, places),
        in_specs=[pl.BlockSpec(memory_space=pltpu.SMEM)]
        + [pl.BlockSpec(memory_space=pltpu.VMEM)] * len(bias_slots),
        out_specs=pl.BlockSpec(memory_space=pltpu.VMEM),
        out_shape=jax.ShapeDtypeStruct(shape, jnp.bfloat16),
        scratch_shapes=[
            pltpu.VMEM((total_rows, rows, wide), jnp.bfloat16),
            pltpu.VMEM(shape, jnp.float32),
        ],
        compiler_params=pltpu.CompilerParams(vmem_limit_bytes=48 << 20),
        name="layout_bias",
    )(base, *bias_slots)


def attention_kernel(total_cols, heads, *refs):
    bias_ref = refs[0]
    x_in = refs[1 : 1 + total_cols]
    mark_ref, project_ref, mix_ref = refs[1 + total_cols : 4 + total_cols]
    outs = refs[4 + total_cols : 4 + 2 * total_cols]
    scored, termed, summed, mixed = refs[4 + 2 * total_cols :]
    places, width = x_in[0].shape[1:]
    residues = places * total_cols
    each = width // heads
    group = 128 // each
    padded = bias_ref.shape[0] * 128
    bf16 = jnp.bfloat16
    transposed = (((1,), (1,)), ((), ()))
    chunk = 32

    x = jnp.concatenate([r[0].astype(jnp.float32) for r in x_in], axis=0)
    made = jnp.dot(
        zscore_transform(x).astype(bf16), project_ref[...], preferred_element_type=jnp.float32
    )
    present = mark_ref[0] > 0.0
    lane = lax.broadcasted_iota(jnp.int32, (1, 128), 1)
    scale = 1.0 / math.sqrt(each)
    filler = jnp.zeros((padded - residues, 128), bf16)

    def head_columns(part, h):
        at = part * width + h // group * 128
        return made[:, at : at + 128].astype(bf16)

    def only(block, h):
        inside = (lane >= h % group * each) & (lane < (h % group + 1) * each)
        return jnp.concatenate([jnp.where(inside, block, jnp.zeros_like(block)), filler], axis=0)

    def score(h):
        scored[h % 2] = lax.dot_general(
            head_columns(0, h), only(head_columns(1, h), h), transposed,
            preferred_element_type=jnp.float32,
        )

    score(0)
    for h in range(heads):
        if h + 1 < heads:
            score(h + 1)
        for first in range(0, residues, chunk):
            start = h * residues + first
            bias = jnp.concatenate(
                [bias_ref[t, start : start + chunk, :] for t in range(bias_ref.shape[0])], axis=1
            )
            scores = scored[h % 2, first : first + chunk, :] * scale + bias.astype(jnp.float32)
            scores = jnp.where(present, scores, masked_score)
            terms = jnp.exp(scores - jnp.max(scores, axis=1, keepdims=True))
            weight = jnp.sum(terms, axis=1, keepdims=True)
            termed[h % 2, first : first + chunk, :] = terms.astype(bf16)
            summed[h % 2, first : first + chunk, :] = jnp.broadcast_to(1.0 / weight, (chunk, 128))
        got = jnp.dot(
            termed[h % 2], only(head_columns(2, h), h), preferred_element_type=jnp.float32
        ) * summed[h % 2]
        total = got if h % group == 0 else total + got
        if h % group == group - 1:
            at = h // group * 128
            gate = jax.nn.sigmoid(made[:, 3 * width + at : 3 * width + at + 128])
            mixed[:, at : at + 128] = (gate * total).astype(bf16)
    after = x + jnp.dot(mixed[...], mix_ref[...], preferred_element_type=jnp.float32)
    for m in range(total_cols):
        outs[m][0] = after[m * places : (m + 1) * places].astype(bf16)


def attend(bias, heads, x_slots, marks, project, mix):
    total_cols = len(x_slots)
    seqs, places, width = x_slots[0].shape
    residues = places * total_cols
    padded = bias.shape[0] * 128

    def whole(a):
        return pl.BlockSpec(a.shape, lambda s, n=a.ndim: (0,) * n)

    per_seq = pl.BlockSpec((1, places, width), lambda s: (s, 0, 0))
    bf16 = jnp.bfloat16
    return pl.pallas_call(
        functools.partial(attention_kernel, total_cols, heads),
        grid=(seqs,),
        in_specs=[whole(bias)]
        + [per_seq] * total_cols
        + [pl.BlockSpec((1, 1, padded), lambda s: (s, 0, 0)), whole(project), whole(mix)],
        out_specs=[per_seq] * total_cols,
        out_shape=[jax.ShapeDtypeStruct((seqs, places, width), bf16)] * total_cols,
        scratch_shapes=[
            pltpu.VMEM((2, residues, padded), jnp.float32),
            pltpu.VMEM((2, residues, padded), bf16),
            pltpu.VMEM((2, residues, 128), jnp.float32),
            pltpu.VMEM((residues, width), bf16),
        ],
        compiler_params=pltpu.CompilerParams(
            vmem_limit_bytes=48 << 20, dimension_semantics=("arbitrary",)
        ),
        name="row_attention",
    )(bias, *x_slots, marks, project, mix)


def regroup_kernel(plan, total_in, *refs):
    for out, parts in zip(refs[total_in:], plan):
        rows = [
            refs[n][at] if refs[n].ndim == 3 else refs[n][at : at + count]
            for n, at, count in parts
        ]
        out[...] = jnp.concatenate([r.astype(jnp.float32) for r in rows], axis=0).astype(out.dtype)


def regroup(blocks, plan):
    pairs = blocks[0].shape[-1]
    return pl.pallas_call(
        functools.partial(regroup_kernel, plan, len(blocks)),
        in_specs=[pl.BlockSpec(memory_space=pltpu.VMEM)] * len(blocks),
        out_specs=[pl.BlockSpec(memory_space=pltpu.VMEM)] * len(plan),
        out_shape=[
            jax.ShapeDtypeStruct((sum(count for _, _, count in parts), pairs), jnp.bfloat16)
            for parts in plan
        ],
        compiler_params=pltpu.CompilerParams(vmem_limit_bytes=40 << 20),
        name="regroup",
    )(*blocks)


def stack_kernel(*refs):
    count = refs[0].shape[0]
    for n, ref in enumerate(refs[:-1]):
        refs[-1][n * count : (n + 1) * count] = ref[...]


def stack_blocks(blocks):
    shape = (len(blocks) * blocks[0].shape[0],) + blocks[0].shape[1:]
    return pl.pallas_call(
        stack_kernel,
        out_shape=jax.ShapeDtypeStruct(shape, blocks[0].dtype),
        compiler_params=pltpu.CompilerParams(vmem_limit_bytes=40 << 20),
        name="stack_blocks",
    )(*blocks)


def triangle_kernel(total_rows, total_cols, *refs):
    base_ref = refs[0]
    slots = refs[1 : 1 + total_rows]
    kept = refs[1 + total_rows : 1 + total_rows + total_cols]
    given, stack, tiles, crossed = refs[1 + total_rows + total_cols :]
    pairs = kept[0].shape[2]
    share = kept[0].shape[1]
    residues = tiles.shape[1] // (2 * share)
    rows = residues // total_rows
    places = residues // total_cols
    bf16 = jnp.bfloat16
    spread_slots(slots, stack, base_ref, tiles, total_cols, places)
    for c in range(share):
        sides = []
        for side in range(2):
            start = (side * share + c) * residues
            sides.append(
                jnp.concatenate(
                    [tiles[t, start : start + residues, :] for t in range(tiles.shape[0])], axis=1
                ).astype(bf16)
            )
        got = lax.dot_general(
            sides[0], sides[1], (((1,), (1,)), ((), ())), preferred_element_type=jnp.float32
        )
        for t in range(tiles.shape[0]):
            last = min(128, residues - t * 128)
            crossed[t, c * residues : (c + 1) * residues, :last] = got[:, t * 128 : t * 128 + last]
    lane = lax.broadcasted_iota(jnp.int32, (share, 128), 1)

    def one(j, carry):
        for h in range(2):
            outs = [given.at[m] if h else kept[m] for m in range(total_cols)]
            rows_out(j, base_ref[2 * j + h], outs)
        return carry

    def rows_out(k, base, outs):
        made = [dict() for _ in range(total_cols)]
        for i in range(rows):
            row = [
                crossed[t, pl.ds(base + i, share, stride=residues), :]
                for t in range(tiles.shape[0])
            ]
            for m in range(total_cols):
                come, off = divmod(m * places, 128)
                after = row[come + 1] if come + 1 < len(row) else row[come]
                piece = jnp.concatenate([row[come], after], axis=1)
                to, at = divmod(i * places, 128)
                if at != off:
                    piece = pltpu.roll(piece, (at - off) % 256, 1)
                begin = piece[:, :128]
                if to in made[m]:
                    begin = jnp.where(lane >= at, begin, made[m][to])
                made[m][to] = begin
                if at + places > 128:
                    made[m][to + 1] = piece[:, 128:]
                if at + places >= 128 or i == rows - 1:
                    size = min(128, pairs - to * 128)
                    outs[m][k, :, to * 128 : to * 128 + size] = made[m].pop(to)[:, :size].astype(bf16)
                    if i == rows - 1 and to + 1 in made[m]:
                        size = pairs - (to + 1) * 128
                        outs[m][k, :, (to + 1) * 128 : pairs] = made[m].pop(to + 1)[:, :size].astype(bf16)

    lax.fori_loop(0, total_rows // 2, one, 0)


def triangle(base, slots, share, total_cols, residues):
    total_rows = len(slots)
    rows, pairs = slots[1].shape
    padded = -(-residues // 128)
    wide = -(-pairs // 128) * 128 + 128
    bf16 = jnp.bfloat16
    return pl.pallas_call(
        functools.partial(triangle_kernel, total_rows, total_cols),
        in_specs=[pl.BlockSpec(memory_space=pltpu.SMEM)]
        + [pl.BlockSpec(memory_space=pltpu.VMEM)] * total_rows,
        out_specs=[pl.BlockSpec(memory_space=pltpu.VMEM)] * (total_cols + 1),
        out_shape=[jax.ShapeDtypeStruct((total_rows // 2, share, pairs), bf16)] * total_cols
        + [jax.ShapeDtypeStruct((total_cols, total_rows // 2, share, pairs), bf16)],
        scratch_shapes=[
            pltpu.VMEM((total_rows, rows, wide), bf16),
            pltpu.VMEM((padded, 2 * share * residues, 128), jnp.float32),
            pltpu.VMEM((padded, share * residues, 128), jnp.float32),
        ],
        compiler_params=pltpu.CompilerParams(vmem_limit_bytes=56 << 20),
        name="triangle",
    )(base, *slots)


def finish_kernel(total_rows, *refs):
    lead_ref = refs[0]
    chips = total_rows // 2
    high_ref, z_ref, valve_ref, exit_ref, out_ref = refs[1 + chips :]
    count = refs[1].shape[0] // 2
    slots = [refs[1 + k // 2].at[k % 2 * count : (k % 2 + 1) * count] for k in range(total_rows)]
    pairs = out_ref.shape[0]
    chunk = 512
    exits = jnp.concatenate(
        [exit_ref[lead_ref[n]].astype(jnp.float32) for n in range(exit_ref.shape[0])], axis=0
    ).astype(jnp.bfloat16)
    for first in range(0, pairs, chunk):
        last = min(first + chunk, pairs)
        crossed = jnp.concatenate(
            [s[:, first:last].astype(jnp.float32) for s in slots], axis=0
        )
        centred = crossed - jnp.mean(crossed, axis=0, keepdims=True)
        spread = jnp.mean(centred * centred, axis=0, keepdims=True)
        normed = (centred * lax.rsqrt(spread + norm_eps)).astype(jnp.bfloat16)
        projected = lax.dot_general(
            normed, exits, (((0,), (0,)), ((), ())), preferred_element_type=jnp.float32
        )
        gate = jax.nn.sigmoid(
            jnp.dot(high_ref[first:last, :], valve_ref[...], preferred_element_type=jnp.float32)
        )
        out_ref[first:last, :] = (z_ref[first:last, :] + gate * projected).astype(jnp.bfloat16)


def finish(lead, slots, high, z_one, valve, exit_w):
    return pl.pallas_call(
        functools.partial(finish_kernel, 2 * len(slots)),
        in_specs=[pl.BlockSpec(memory_space=pltpu.SMEM)]
        + [pl.BlockSpec(memory_space=pltpu.VMEM)] * (len(slots) + 4),
        out_specs=pl.BlockSpec(memory_space=pltpu.VMEM),
        out_shape=jax.ShapeDtypeStruct(high.shape, jnp.bfloat16),
        compiler_params=pltpu.CompilerParams(vmem_limit_bytes=40 << 20),
        name="pair_finish",
    )(lead, *slots, high, z_one, valve, exit_w)


def place_kernel(start_ref, *refs):
    out = refs[-1]
    for m, slot in enumerate(refs[:-1]):
        out[pl.ds(start_ref[m], slot.shape[0])] = slot[...]


def place_slots(starts, slots):
    total = len(slots)
    shape = (total * slots[0].shape[0],) + slots[0].shape[1:]
    return pl.pallas_call(
        place_kernel,
        in_specs=[pl.BlockSpec(memory_space=pltpu.SMEM)]
        + [pl.BlockSpec(memory_space=pltpu.VMEM)] * total,
        out_specs=pl.BlockSpec(memory_space=pltpu.VMEM),
        out_shape=jax.ShapeDtypeStruct(shape, slots[0].dtype),
        compiler_params=pltpu.CompilerParams(vmem_limit_bytes=40 << 20),
        name="place_sequences",
    )(starts, *slots)


def shards(
    homolog_activations,
    coupling_activations,
    homolog_existence_marks,
    observed_peptide_marks,
    peptide_ordinals,
    strand_membership,
    distance_ordinal_vectors,
    coupling_score_mapping,
    question_mapping_weights,
    address_payload_mapping,
    logistic_valve_mapping,
    mixture_exit_mapping,
    twofold_covariance_mapping,
    covariance_exit_mapping,
    triad_opening_mappings,
    triad_valve_mapping,
    triad_exit_mapping,
):
    row_total = lax.axis_size("row")
    col_total = lax.axis_size("col")
    group_ratio = row_total // col_total
    devices = row_total * col_total
    row_place = lax.axis_index("row")
    col_place = lax.axis_index("col")
    tile_rows = coupling_activations.shape[0]
    block_columns = coupling_activations.shape[1]
    number_of_homologs = homolog_activations.shape[0]
    residues = row_total * tile_rows
    heads = coupling_score_mapping.shape[1]
    breadth = question_mapping_weights.shape[1]
    head_breadth = breadth // heads
    opm = twofold_covariance_mapping.shape[1] // 2
    tri_width = triad_exit_mapping.shape[0]
    pair_width = coupling_activations.shape[2]
    own_seqs = number_of_homologs // col_total
    share = tri_width // devices
    row_first = row_place * tile_rows
    col_first = col_place * block_columns
    bf16 = jnp.bfloat16

    marks = homolog_existence_marks.astype(jnp.float32)
    left, right = opm_operands(homolog_activations, marks, twofold_covariance_mapping)
    chips = range(0, row_total, 2)

    def over_chips(pieces):
        return [pieces[0]] + [
            lax.ppermute(piece, "row", [(i, i ^ k) for i in range(row_total)])
            for k, piece in zip(chips[1:], pieces[1:])
        ]

    def other_core(block):
        return lax.ppermute(block, "row", [(i, i ^ 1) for i in range(row_total)])

    left_z = collect(left, "col")
    left_stack = jnp.stack(left_z)
    right_even = jnp.concatenate(over_chips([right] * len(chips)), axis=0)
    right_odd = other_core(right_even)
    left_even = jnp.concatenate(
        over_chips(
            [
                lax.dynamic_index_in_dim(
                    left_stack, (row_place ^ k) // group_ratio ^ col_place, 0, keepdims=False
                )
                for k in chips
            ]
        ),
        axis=0,
    )
    left_odd = other_core(left_even)
    operands = [left_even, left_odd, right_even, right_odd]

    own_marks = lax.dynamic_slice_in_dim(left_stack[:, -1], col_place * own_seqs, own_seqs, 1)
    own_marks = jnp.swapaxes(own_marks[:, :, :block_columns], 0, 1).reshape(own_seqs, 1, residues)
    padded = -(-residues // 128) * 128
    own_marks = jnp.pad(own_marks.astype(jnp.float32), ((0, 0), (0, 0), (0, padded - residues)))

    lanes = 128
    spots = jnp.stack(
        [
            lax.dynamic_slice_in_dim(peptide_ordinals, row_first, tile_rows),
            lax.dynamic_slice_in_dim(strand_membership, row_first, tile_rows),
            jnp.full((tile_rows,), row_place % group_ratio * tile_rows, jnp.int32),
            jnp.full((tile_rows,), row_place % group_ratio, jnp.int32),
        ]
    )
    place = jnp.pad(
        jnp.stack(
            [
                lax.dynamic_slice_in_dim(peptide_ordinals, col_first, block_columns),
                lax.dynamic_slice_in_dim(strand_membership, col_first, block_columns),
            ]
        ),
        ((0, 6), (0, lanes - block_columns)),
    )
    exit_t = covariance_exit_mapping.reshape(opm, opm, pair_width).transpose(2, 1, 0)
    exit_t = exit_t.reshape(pair_width, opm * opm)
    near_t = jnp.pad(
        distance_ordinal_vectors, ((0, lanes - distance_ordinal_vectors.shape[0]), (0, 0))
    ).T
    open_t = triad_opening_mappings.reshape(
        pair_width, 2, 2, row_total // 2, 2, col_total, share
    )
    open_t = open_t.transpose(2, 4, 5, 3, 1, 6, 0)
    open_t = jnp.concatenate(
        [lax.dynamic_slice_in_dim(open_t, row_place % 2 ^ h, 1, 1) for h in range(2)], axis=1
    )
    open_t = jnp.concatenate(
        [lax.dynamic_slice_in_dim(open_t, col_place ^ m, 1, 2) for m in range(col_total)], axis=2
    )
    open_t = jnp.concatenate(
        [lax.dynamic_slice_in_dim(open_t, row_place // 2 ^ j, 1, 3) for j in range(row_total // 2)],
        axis=3,
    ).reshape(4 * tri_width, pair_width)
    score_t = coupling_score_mapping.T
    live_rows = lax.dynamic_slice_in_dim(observed_peptide_marks, row_first, tile_rows)
    live_cols = lax.dynamic_slice_in_dim(observed_peptide_marks, col_first, block_columns)
    live = (live_rows[:, None] * live_cols[None, :]).astype(jnp.float32).reshape(1, -1)
    operands, x_own = lax.optimization_barrier((operands, homolog_activations))
    x_slots = exchange(x_own.reshape(col_total, own_seqs, block_columns, -1), "col")
    z_one, ln_tri, *kept, given = pair_stage(
        operands[:2], operands[2:], coupling_activations, spots, place, exit_t, near_t, open_t,
        score_t, live, row_total, col_total,
    )

    given, x_slots = lax.optimization_barrier((given, x_slots))

    row_ids = row_place ^ jnp.arange(row_total, dtype=jnp.int32)
    col_ids = col_place ^ jnp.arange(col_total, dtype=jnp.int32)
    base = (row_ids // group_ratio ^ col_place) * block_columns + row_ids % group_ratio * tile_rows
    cols, spans = range(col_total), range(row_total // 2)
    count = 2 * share
    received = other_core(given)
    received = [received[m] for m in cols]
    kept = swap(kept, "col")
    kept, received = lax.optimization_barrier((kept, received))
    received = swap(received, "col")
    kept = regroup(
        kept,
        [
            [(m, j * count, count) for m in cols]
            + [(m, count * len(spans), heads) for m in cols]
            for j in spans
        ],
    )
    kept = over_chips(kept)
    kept, received = lax.optimization_barrier((kept, received))
    received = regroup(received, [[(m, j * count, count) for m in cols] for j in spans])
    received = over_chips(received)
    kept, received = lax.optimization_barrier((kept, received))
    (bias_even,) = regroup(kept, [[(j, count * col_total, heads * col_total) for j in spans]])
    bias_odd = other_core(bias_even)

    side_slots = [slot for both in zip(kept, received) for slot in both]
    *crossed, given = triangle(base, side_slots, share, col_total, residues)
    bias_even, bias_odd, given = lax.optimization_barrier((bias_even, bias_odd, given))
    bias_all = layout_bias(base, [bias_even, bias_odd], col_total, block_columns)
    received = other_core(given)
    crossed = regroup(
        list(crossed) + [received[m] for m in cols],
        [[(h * col_total + m, j, share) for h in range(2) for j in spans] for m in cols],
    )
    crossed = swap(crossed, "col")

    project = jnp.concatenate(
        [question_mapping_weights, address_payload_mapping, logistic_valve_mapping], axis=1
    )
    own_after = attend(bias_all, heads, x_slots, own_marks, project, mixture_exit_mapping)

    crossed, own_after = lax.optimization_barrier((crossed, own_after))
    after_slots = swap(own_after, "col")
    half = share * len(spans)
    crossed = regroup(
        crossed, [[(m, h * half + j * share, share) for h in range(2) for m in cols] for j in spans]
    )
    crossed = over_chips(crossed)
    homologs_after = place_slots(col_ids * own_seqs, after_slots)
    exit_w = triad_exit_mapping.reshape(devices, share, pair_width)
    lead = (row_ids[:, None] * col_total + col_ids[None, :]).reshape(-1)
    couplings_after = finish(lead, crossed, ln_tri, z_one, triad_valve_mapping, exit_w)
    return (homologs_after, couplings_after.reshape(coupling_activations.shape))


def solution(mesh):
    placed = (
        P("row", "col", None),
        P("row", "col", None),
        P("row", "col"),
        P(),
        P(),
        P(),
        P(),
        P(),
        P(),
        P(),
        P(),
        P(),
        P(),
        P(),
        P(),
        P(),
        P(),
    )
    return jax.shard_map(
        shards,
        mesh=mesh,
        in_specs=placed,
        out_specs=(P("row", "col", None), P("row", "col", None)),
        check_vma=False,
    )
```

```python
import functools
import math

import jax
import jax.numpy as jnp
from jax import lax
from jax.experimental import pallas as pl
from jax.experimental.pallas import tpu as pltpu
from jax.sharding import PartitionSpec as P

REL_MAX = 32


norm_eps = 1e-05
count_eps = 0.001
masked_score = -1000000000.0


def swap(pieces, axis):
    total = len(pieces)
    return [pieces[0]] + [
        lax.ppermute(pieces[k], axis, [(i, i ^ k) for i in range(total)]) for k in range(1, total)
    ]


def collect(block, axis):
    return swap([block] * lax.axis_size(axis), axis)


def exchange(pieces, axis):
    me = lax.axis_index(axis)
    total = lax.axis_size(axis)
    return swap(
        [lax.dynamic_index_in_dim(pieces, me ^ k, 0, keepdims=False) for k in range(total)], axis
    )


def in_order(slots, axis):
    me = lax.axis_index(axis)
    stacked = jnp.stack(slots)
    return jnp.stack(
        [
            lax.dynamic_index_in_dim(stacked, me ^ k, 0, keepdims=False)
            for k in range(len(slots))
        ]
    )


def zscore_transform(inputs):
    inputs = inputs.astype(jnp.float32)
    centred = inputs - jnp.mean(inputs, axis=-1, keepdims=True)
    spread = jnp.mean(centred * centred, axis=-1, keepdims=True)
    return centred * lax.rsqrt(spread + norm_eps)


def regrouped_covariance(operand, weights):
    batch_shape = operand.shape[:-1]
    result = jnp.dot(
        operand.reshape(-1, operand.shape[-1]), weights, preferred_element_type=jnp.float32
    )
    return result.reshape(batch_shape + (weights.shape[-1],))


def position_bins(index_rows, index_cols, chain_rows, chain_cols):
    offset = jnp.clip(index_rows[:, None] - index_cols[None, :] + REL_MAX, 0, 2 * REL_MAX)
    return jnp.where(chain_rows[:, None] == chain_cols[None, :], offset, 2 * REL_MAX + 1)


def operand_kernel(x_ref, marks_ref, spread_ref, wl_ref, wr_ref, left_ref, right_ref, ln, side, acc):
    seqs, places, width = x_ref.shape
    groups = left_ref.shape[0] - 1
    rights = right_ref.shape[0] - 1
    lanes = left_ref.shape[2]
    per = places // groups
    for s in range(seqs):
        own = zscore_transform(x_ref[s])
        for h in range(width // 128):
            ln[h, s * places : (s + 1) * places, :] = own[:, h * 128 : (h + 1) * 128]
    marks = marks_ref[...]
    for s in range(seqs):
        own = jnp.concatenate(
            [ln[h, s * places : (s + 1) * places, :] for h in range(width // 128)], axis=1
        )
        got = lax.dot_general(
            wr_ref[...], own.astype(jnp.bfloat16), (((1,), (1,)), ((), ())),
            preferred_element_type=jnp.float32,
        )
        got = got * marks[s : s + 1, :]
        side[pl.ds(s, rights, stride=seqs), :] = jnp.concatenate(
            [got, jnp.zeros((rights, lanes - places), jnp.float32)], axis=1
        )
    right_ref[:rights] = side[...].reshape(rights, seqs, lanes).astype(jnp.bfloat16)
    for q in range(per):
        for g in range(groups):
            for h in range(width // 128):
                acc[g * seqs : (g + 1) * seqs, h * 128 : (h + 1) * 128] = ln[
                    h, pl.ds(g * per + q, seqs, stride=places), :
                ]
        part = jnp.dot(
            acc[...].astype(jnp.bfloat16), wl_ref[q], preferred_element_type=jnp.float32
        )
        total = part if q == 0 else total + part
    spread = jnp.dot(
        marks.astype(jnp.bfloat16), spread_ref[...], preferred_element_type=jnp.float32
    )
    for g in range(groups):
        left_ref[g] = (
            total[g * seqs : (g + 1) * seqs] * spread[:, g * lanes : (g + 1) * lanes]
        ).astype(jnp.bfloat16)
    block = jnp.zeros((seqs, lanes), jnp.float32)
    side[:seqs, :] = block
    side[:seqs, :places] = marks
    left_ref[groups] = side[:seqs, :].astype(jnp.bfloat16)
    right_ref[rights] = side[:seqs, :].astype(jnp.bfloat16)


def opm_operands(x, marks, mapping):
    seqs, places, width = x.shape
    opm = mapping.shape[1] // 2
    lanes = 128
    per = lanes // opm
    groups = places // per
    wl = jnp.stack(
        [
            jnp.pad(mapping[:, :opm], ((0, 0), (q * opm, lanes - (q + 1) * opm)))
            for q in range(per)
        ]
    )
    wr = mapping[:, opm:].T
    spread = jnp.repeat(jnp.eye(places, dtype=jnp.bfloat16), opm, axis=1)
    return pl.pallas_call(
        operand_kernel,
        out_shape=(
            jax.ShapeDtypeStruct((groups + 1, seqs, lanes), jnp.bfloat16),
            jax.ShapeDtypeStruct((opm + 1, seqs, lanes), jnp.bfloat16),
        ),
        scratch_shapes=[
            pltpu.VMEM((width // 128, seqs * places, 128), jnp.float32),
            pltpu.VMEM((opm * seqs, lanes), jnp.float32),
            pltpu.VMEM((groups * seqs, width), jnp.float32),
        ],
        compiler_params=pltpu.CompilerParams(vmem_limit_bytes=40 << 20),
        name="outer_operands",
    )(x, marks, spread, wl, wr)


def pair_kernel(total_rows, total_cols, *refs):
    spots = refs[0]
    rows_in = refs[1:3]
    cols_in = refs[3:5]
    pair_ref, place_ref, exit_ref, near_ref, open_ref, score_ref, live_ref = refs[5:12]
    outs = refs[12:]
    z_ref, high_ref = outs[:2]
    side_refs = outs[2 : 2 + total_cols]
    given_ref = outs[2 + total_cols]
    left, right, prod, counts, low = outs[3 + total_cols :]
    step = pl.program_id(0)
    group, places, width = pair_ref.shape
    seqs = rows_in[0].shape[1]
    lanes = 128
    chips = total_rows // 2
    opm = cols_in[0].shape[0] // chips - 1
    sent = rows_in[0].shape[0] // chips
    blocks = left.shape[0]
    bf16 = jnp.bfloat16

    @pl.when(step == 0)
    def _():
        mark_rows, mark_cols = [], []
        for k in range(total_rows):
            half, chip = k % 2, k // 2
            for g in range(blocks):
                left[g, k * seqs : (k + 1) * seqs, :] = rows_in[half][
                    chip * sent + spots[3, 0] * blocks + g
                ]
            for e in range(opm):
                right[k * seqs : (k + 1) * seqs, e * lanes : (e + 1) * lanes] = cols_in[half][
                    chip * (opm + 1) + e
                ]
            mark_rows.append(rows_in[half][chip * sent + sent - 1])
            mark_cols.append(cols_in[half][chip * (opm + 1) + opm])
        mark_rows = jnp.concatenate(mark_rows, axis=0)
        mark_cols = jnp.concatenate(mark_cols, axis=0)
        counts[...] = lax.dot_general(
            mark_rows, mark_cols, (((0,), (0,)), ((), ())), preferred_element_type=jnp.float32
        )

    grid_left = left[step]
    half = opm // 2
    for part in range(2):
        got = lax.dot_general(
            grid_left, right[:, part * half * lanes : (part + 1) * half * lanes],
            (((0,), (0,)), ((), ())), preferred_element_type=jnp.float32,
        ).astype(bf16)
        for e in range(half):
            for i in range(group):
                prod[
                    (part * half + e) * opm : (part * half + e + 1) * opm,
                    i * lanes : (i + 1) * lanes,
                ] = got[i * opm : (i + 1) * opm, e * lanes : (e + 1) * lanes]
    mixed = jnp.dot(exit_ref[...], prod[...], preferred_element_type=jnp.float32)
    pos_cols = place_ref[0:1, :]
    chain_cols = place_ref[1:2, :]
    bins, amount = [], []
    for i in range(group):
        here = step * group + i
        offset = jnp.clip(spots[0, here] - pos_cols + REL_MAX, 0, 2 * REL_MAX)
        bins.append(jnp.where(chain_cols == spots[1, here], offset, 2 * REL_MAX + 1))
        amount.append(counts[pl.ds(spots[2, 0] + here, 1), :])
    bins = jnp.concatenate(bins, axis=1)
    amount = jnp.concatenate(amount, axis=1)
    one_hot = (
        lax.broadcasted_iota(jnp.int32, (near_ref.shape[1], group * lanes), 0) == bins
    )
    one_hot = jnp.where(one_hot, 1.0, 0.0).astype(bf16)
    near = jnp.dot(near_ref[...], one_hot, preferred_element_type=jnp.float32)
    update = jnp.transpose(mixed / (count_eps + amount) + near)
    z = jnp.concatenate(
        [
            pair_ref[i].astype(jnp.float32) + update[i * lanes : i * lanes + places]
            for i in range(group)
        ],
        axis=0,
    )
    z_ref[...] = z
    ln = zscore_transform(z)
    high = ln.astype(bf16)
    start = pl.multiple_of(step * (group * places), 16)
    high_ref[pl.ds(start, group * places), :] = high
    low[pl.ds(start, group * places), :] = (ln - high.astype(jnp.float32)).astype(bf16)

    @pl.when(step == pl.num_programs(0) - 1)
    def _():
        pairs = high_ref.shape[0]
        chunk = 512
        transposed = (((1,), (1,)), ((), ()))
        half_rows = open_ref.shape[0] // 2
        each = half_rows // total_cols // 2
        for first in range(0, pairs, chunk):
            last = min(first + chunk, pairs)
            ours = high_ref[first:last, :]
            bias = lax.dot_general(
                score_ref[...], ours, transposed, preferred_element_type=jnp.float32
            ) + lax.dot_general(
                score_ref[...], low[first:last, :], transposed, preferred_element_type=jnp.float32
            )
            opened = lax.dot_general(
                open_ref[...], ours, transposed, preferred_element_type=jnp.float32
            )
            sides = (
                jax.nn.sigmoid(opened[half_rows:]) * opened[:half_rows] * live_ref[:, first:last]
            )
            for m in range(total_cols):
                at = m * each
                side_refs[m][:, first:last] = jnp.concatenate(
                    [sides[at : at + each], bias], axis=0
                ).astype(bf16)
                at = (total_cols + m) * each
                given_ref[m, :, first:last] = sides[at : at + each].astype(bf16)


def pair_stage(rows_in, cols_in, pair, spots, place, exit_t, near_t, open_t, score_t, live, total_rows, total_cols):
    tile_rows, places, width = pair.shape
    sent, seqs, lanes = rows_in[0].shape
    chips = total_rows // 2
    blocks = (sent // chips - 1) // 2
    group = tile_rows // blocks
    opm = cols_in[0].shape[0] // chips - 1
    pairs = tile_rows * places
    each = open_t.shape[0] // 4 // total_cols
    every = total_rows * seqs

    def whole(a):
        return pl.BlockSpec(a.shape, lambda g, n=a.ndim: (0,) * n)

    def whole_out(shape):
        return pl.BlockSpec(shape, lambda g, n=len(shape): (0,) * n)

    ins = list(rows_in) + list(cols_in)
    rest = [place, exit_t, near_t, open_t, score_t, live]
    bf16 = jnp.bfloat16
    outs = [
        jax.ShapeDtypeStruct((pairs, width), jnp.float32),
        jax.ShapeDtypeStruct((pairs, width), bf16),
    ] + [jax.ShapeDtypeStruct((each + score_t.shape[0], pairs), bf16)] * total_cols
    outs.append(jax.ShapeDtypeStruct((total_cols, each, pairs), bf16))
    return pl.pallas_call(
        functools.partial(pair_kernel, total_rows, total_cols),
        grid=(blocks,),
        in_specs=[pl.BlockSpec(memory_space=pltpu.SMEM)]
        + [whole(a) for a in ins]
        + [pl.BlockSpec((group, places, width), lambda g: (g, 0, 0))]
        + [whole(a) for a in rest],
        out_specs=[pl.BlockSpec((group * places, width), lambda g: (g, 0))]
        + [whole_out(o.shape) for o in outs[1:]],
        out_shape=outs,
        scratch_shapes=[
            pltpu.VMEM((blocks, every, lanes), bf16),
            pltpu.VMEM((every, opm * lanes), bf16),
            pltpu.VMEM((opm * opm, group * lanes), bf16),
            pltpu.VMEM((lanes, lanes), jnp.float32),
            pltpu.VMEM((pairs, width), bf16),
        ],
        compiler_params=pltpu.CompilerParams(
            vmem_limit_bytes=56 << 20, dimension_semantics=("arbitrary",)
        ),
        name="pair_update",
    )(spots, *ins, pair, *rest)


def spread_slots(slots, stack, base_ref, tiles, total_cols, places):
    total, high, wide = stack.shape
    pairs = slots[0].shape[1]
    count = high // total_cols
    rows = pairs // places
    residues = rows * total
    lane = lax.broadcasted_iota(jnp.int32, (count, 128), 1)
    for k in range(total):
        slot, at = k % len(slots), k // len(slots) * high
        stack[k, :, :pairs] = slots[slot][at : at + high]

    def one(k, carry):
        base = base_ref[k]
        for i in range(rows):
            first = i * places // 128 * 128
            off = i * places - first
            window = stack[k, :, first : first + 256].astype(jnp.float32)
            made = [None] * tiles.shape[0]
            for c in range(total_cols):
                to, at = divmod(c * places, 128)
                piece = window[c * count : (c + 1) * count]
                if at != off:
                    piece = pltpu.roll(piece, (at - off) % 256, 1)
                begin = piece[:, :128]
                made[to] = begin if made[to] is None else jnp.where(lane >= at, begin, made[to])
                if at + places > 128:
                    made[to + 1] = piece[:, 128:]
            kept = residues - 128 * (len(made) - 1)
            made[-1] = jnp.where(lane < kept, made[-1], 0.0)
            for t, tile in enumerate(made):
                tiles[t, pl.ds(base + i, count, stride=residues), :] = tile
        return carry

    lax.fori_loop(0, total, one, 0)


def layout_kernel(halves, total_cols, places, *refs):
    base_ref = refs[0]
    out_ref, stack, tiles = refs[1 + halves :]
    spread_slots(refs[1 : 1 + halves], stack, base_ref, tiles, total_cols, places)
    out_ref[...] = tiles[...].astype(out_ref.dtype)


def layout_bias(base, bias_slots, total_cols, places):
    total_rows = base.shape[0]
    rows, pairs = bias_slots[0].shape
    rows = rows * len(bias_slots) // total_rows
    residues = places * total_cols
    heads = rows // total_cols
    shape = (-(-residues // 128), heads * residues, 128)
    wide = -(-pairs // 128) * 128 + 128
    return pl.pallas_call(
        functools.partial(layout_kernel, len(bias_slots), total_cols, places),
        in_specs=[pl.BlockSpec(memory_space=pltpu.SMEM)]
        + [pl.BlockSpec(memory_space=pltpu.VMEM)] * len(bias_slots),
        out_specs=pl.BlockSpec(memory_space=pltpu.VMEM),
        out_shape=jax.ShapeDtypeStruct(shape, jnp.bfloat16),
        scratch_shapes=[
            pltpu.VMEM((total_rows, rows, wide), jnp.bfloat16),
            pltpu.VMEM(shape, jnp.float32),
        ],
        compiler_params=pltpu.CompilerParams(vmem_limit_bytes=48 << 20),
        name="layout_bias",
    )(base, *bias_slots)


def attention_kernel(total_cols, heads, *refs):
    bias_ref = refs[0]
    x_in = refs[1 : 1 + total_cols]
    mark_ref, project_ref, mix_ref = refs[1 + total_cols : 4 + total_cols]
    outs = refs[4 + total_cols : 4 + 2 * total_cols]
    scored, termed, summed, mixed = refs[4 + 2 * total_cols :]
    places, width = x_in[0].shape[1:]
    residues = places * total_cols
    each = width // heads
    group = 128 // each
    padded = bias_ref.shape[0] * 128
    bf16 = jnp.bfloat16
    transposed = (((1,), (1,)), ((), ()))
    chunk = 32

    x = jnp.concatenate([r[0].astype(jnp.float32) for r in x_in], axis=0)
    made = jnp.dot(
        zscore_transform(x).astype(bf16), project_ref[...], preferred_element_type=jnp.float32
    )
    present = mark_ref[0] > 0.0
    lane = lax.broadcasted_iota(jnp.int32, (1, 128), 1)
    scale = 1.0 / math.sqrt(each)
    filler = jnp.zeros((padded - residues, 128), bf16)

    def head_columns(part, h):
        at = part * width + h // group * 128
        return made[:, at : at + 128].astype(bf16)

    def only(block, h):
        inside = (lane >= h % group * each) & (lane < (h % group + 1) * each)
        return jnp.concatenate([jnp.where(inside, block, jnp.zeros_like(block)), filler], axis=0)

    def score(h):
        scored[h % 2] = lax.dot_general(
            head_columns(0, h), only(head_columns(1, h), h), transposed,
            preferred_element_type=jnp.float32,
        )

    score(0)
    for h in range(heads):
        if h + 1 < heads:
            score(h + 1)
        for first in range(0, residues, chunk):
            start = h * residues + first
            bias = jnp.concatenate(
                [bias_ref[t, start : start + chunk, :] for t in range(bias_ref.shape[0])], axis=1
            )
            scores = scored[h % 2, first : first + chunk, :] * scale + bias.astype(jnp.float32)
            scores = jnp.where(present, scores, masked_score)
            terms = jnp.exp(scores - jnp.max(scores, axis=1, keepdims=True))
            weight = jnp.sum(terms, axis=1, keepdims=True)
            termed[h % 2, first : first + chunk, :] = terms.astype(bf16)
            summed[h % 2, first : first + chunk, :] = jnp.broadcast_to(1.0 / weight, (chunk, 128))
        got = jnp.dot(
            termed[h % 2], only(head_columns(2, h), h), preferred_element_type=jnp.float32
        ) * summed[h % 2]
        total = got if h % group == 0 else total + got
        if h % group == group - 1:
            at = h // group * 128
            gate = jax.nn.sigmoid(made[:, 3 * width + at : 3 * width + at + 128])
            mixed[:, at : at + 128] = (gate * total).astype(bf16)
    after = x + jnp.dot(mixed[...], mix_ref[...], preferred_element_type=jnp.float32)
    for m in range(total_cols):
        outs[m][0] = after[m * places : (m + 1) * places].astype(bf16)


def attend(bias, heads, x_slots, marks, project, mix):
    total_cols = len(x_slots)
    seqs, places, width = x_slots[0].shape
    residues = places * total_cols
    padded = bias.shape[0] * 128

    def whole(a):
        return pl.BlockSpec(a.shape, lambda s, n=a.ndim: (0,) * n)

    per_seq = pl.BlockSpec((1, places, width), lambda s: (s, 0, 0))
    bf16 = jnp.bfloat16
    return pl.pallas_call(
        functools.partial(attention_kernel, total_cols, heads),
        grid=(seqs,),
        in_specs=[whole(bias)]
        + [per_seq] * total_cols
        + [pl.BlockSpec((1, 1, padded), lambda s: (s, 0, 0)), whole(project), whole(mix)],
        out_specs=[per_seq] * total_cols,
        out_shape=[jax.ShapeDtypeStruct((seqs, places, width), bf16)] * total_cols,
        scratch_shapes=[
            pltpu.VMEM((2, residues, padded), jnp.float32),
            pltpu.VMEM((2, residues, padded), bf16),
            pltpu.VMEM((2, residues, 128), jnp.float32),
            pltpu.VMEM((residues, width), bf16),
        ],
        compiler_params=pltpu.CompilerParams(
            vmem_limit_bytes=48 << 20, dimension_semantics=("arbitrary",)
        ),
        name="row_attention",
    )(bias, *x_slots, marks, project, mix)


def regroup_kernel(plan, total_in, *refs):
    for out, parts in zip(refs[total_in:], plan):
        rows = [
            refs[n][at] if refs[n].ndim == 3 else refs[n][at : at + count]
            for n, at, count in parts
        ]
        out[...] = jnp.concatenate([r.astype(jnp.float32) for r in rows], axis=0).astype(out.dtype)


def regroup(blocks, plan):
    pairs = blocks[0].shape[-1]
    return pl.pallas_call(
        functools.partial(regroup_kernel, plan, len(blocks)),
        in_specs=[pl.BlockSpec(memory_space=pltpu.VMEM)] * len(blocks),
        out_specs=[pl.BlockSpec(memory_space=pltpu.VMEM)] * len(plan),
        out_shape=[
            jax.ShapeDtypeStruct((sum(count for _, _, count in parts), pairs), jnp.bfloat16)
            for parts in plan
        ],
        compiler_params=pltpu.CompilerParams(vmem_limit_bytes=40 << 20),
        name="regroup",
    )(*blocks)


def stack_kernel(*refs):
    count = refs[0].shape[0]
    for n, ref in enumerate(refs[:-1]):
        refs[-1][n * count : (n + 1) * count] = ref[...]


def stack_blocks(blocks):
    shape = (len(blocks) * blocks[0].shape[0],) + blocks[0].shape[1:]
    return pl.pallas_call(
        stack_kernel,
        out_shape=jax.ShapeDtypeStruct(shape, blocks[0].dtype),
        compiler_params=pltpu.CompilerParams(vmem_limit_bytes=40 << 20),
        name="stack_blocks",
    )(*blocks)


def triangle_kernel(total_rows, total_cols, *refs):
    base_ref = refs[0]
    slots = refs[1 : 1 + total_rows]
    kept = refs[1 + total_rows : 1 + total_rows + total_cols]
    given, stack, tiles, crossed = refs[1 + total_rows + total_cols :]
    pairs = kept[0].shape[2]
    share = kept[0].shape[1]
    residues = tiles.shape[1] // (2 * share)
    rows = residues // total_rows
    places = residues // total_cols
    bf16 = jnp.bfloat16
    spread_slots(slots, stack, base_ref, tiles, total_cols, places)
    for c in range(share):
        sides = []
        for side in range(2):
            start = (side * share + c) * residues
            sides.append(
                jnp.concatenate(
                    [tiles[t, start : start + residues, :] for t in range(tiles.shape[0])], axis=1
                ).astype(bf16)
            )
        got = lax.dot_general(
            sides[0], sides[1], (((1,), (1,)), ((), ())), preferred_element_type=jnp.float32
        )
        for t in range(tiles.shape[0]):
            last = min(128, residues - t * 128)
            crossed[t, c * residues : (c + 1) * residues, :last] = got[:, t * 128 : t * 128 + last]
    lane = lax.broadcasted_iota(jnp.int32, (share, 128), 1)

    def one(j, carry):
        for h in range(2):
            outs = [given.at[m] if h else kept[m] for m in range(total_cols)]
            rows_out(j, base_ref[2 * j + h], outs)
        return carry

    def rows_out(k, base, outs):
        made = [dict() for _ in range(total_cols)]
        for i in range(rows):
            row = [
                crossed[t, pl.ds(base + i, share, stride=residues), :]
                for t in range(tiles.shape[0])
            ]
            for m in range(total_cols):
                come, off = divmod(m * places, 128)
                after = row[come + 1] if come + 1 < len(row) else row[come]
                piece = jnp.concatenate([row[come], after], axis=1)
                to, at = divmod(i * places, 128)
                if at != off:
                    piece = pltpu.roll(piece, (at - off) % 256, 1)
                begin = piece[:, :128]
                if to in made[m]:
                    begin = jnp.where(lane >= at, begin, made[m][to])
                made[m][to] = begin
                if at + places > 128:
                    made[m][to + 1] = piece[:, 128:]
                if at + places >= 128 or i == rows - 1:
                    size = min(128, pairs - to * 128)
                    outs[m][k, :, to * 128 : to * 128 + size] = made[m].pop(to)[:, :size].astype(bf16)
                    if i == rows - 1 and to + 1 in made[m]:
                        size = pairs - (to + 1) * 128
                        outs[m][k, :, (to + 1) * 128 : pairs] = made[m].pop(to + 1)[:, :size].astype(bf16)

    lax.fori_loop(0, total_rows // 2, one, 0)


def triangle(base, slots, share, total_cols, residues):
    total_rows = len(slots)
    rows, pairs = slots[1].shape
    padded = -(-residues // 128)
    wide = -(-pairs // 128) * 128 + 128
    bf16 = jnp.bfloat16
    return pl.pallas_call(
        functools.partial(triangle_kernel, total_rows, total_cols),
        in_specs=[pl.BlockSpec(memory_space=pltpu.SMEM)]
        + [pl.BlockSpec(memory_space=pltpu.VMEM)] * total_rows,
        out_specs=[pl.BlockSpec(memory_space=pltpu.VMEM)] * (total_cols + 1),
        out_shape=[jax.ShapeDtypeStruct((total_rows // 2, share, pairs), bf16)] * total_cols
        + [jax.ShapeDtypeStruct((total_cols, total_rows // 2, share, pairs), bf16)],
        scratch_shapes=[
            pltpu.VMEM((total_rows, rows, wide), bf16),
            pltpu.VMEM((padded, 2 * share * residues, 128), jnp.float32),
            pltpu.VMEM((padded, share * residues, 128), jnp.float32),
        ],
        compiler_params=pltpu.CompilerParams(vmem_limit_bytes=56 << 20),
        name="triangle",
    )(base, *slots)


def finish_kernel(total_rows, *refs):
    lead_ref = refs[0]
    chips = total_rows // 2
    high_ref, z_ref, valve_ref, exit_ref, out_ref = refs[1 + chips :]
    count = refs[1].shape[0] // 2
    slots = [refs[1 + k // 2].at[k % 2 * count : (k % 2 + 1) * count] for k in range(total_rows)]
    pairs = out_ref.shape[0]
    chunk = 512
    exits = jnp.concatenate(
        [exit_ref[lead_ref[n]].astype(jnp.float32) for n in range(exit_ref.shape[0])], axis=0
    ).astype(jnp.bfloat16)
    for first in range(0, pairs, chunk):
        last = min(first + chunk, pairs)
        crossed = jnp.concatenate(
            [s[:, first:last].astype(jnp.float32) for s in slots], axis=0
        )
        centred = crossed - jnp.mean(crossed, axis=0, keepdims=True)
        spread = jnp.mean(centred * centred, axis=0, keepdims=True)
        normed = (centred * lax.rsqrt(spread + norm_eps)).astype(jnp.bfloat16)
        projected = lax.dot_general(
            normed, exits, (((0,), (0,)), ((), ())), preferred_element_type=jnp.float32
        )
        gate = jax.nn.sigmoid(
            jnp.dot(high_ref[first:last, :], valve_ref[...], preferred_element_type=jnp.float32)
        )
        out_ref[first:last, :] = (z_ref[first:last, :] + gate * projected).astype(jnp.bfloat16)


def finish(lead, slots, high, z_one, valve, exit_w):
    return pl.pallas_call(
        functools.partial(finish_kernel, 2 * len(slots)),
        in_specs=[pl.BlockSpec(memory_space=pltpu.SMEM)]
        + [pl.BlockSpec(memory_space=pltpu.VMEM)] * (len(slots) + 4),
        out_specs=pl.BlockSpec(memory_space=pltpu.VMEM),
        out_shape=jax.ShapeDtypeStruct(high.shape, jnp.bfloat16),
        compiler_params=pltpu.CompilerParams(vmem_limit_bytes=40 << 20),
        name="pair_finish",
    )(lead, *slots, high, z_one, valve, exit_w)


def place_kernel(start_ref, *refs):
    out = refs[-1]
    for m, slot in enumerate(refs[:-1]):
        out[pl.ds(start_ref[m], slot.shape[0])] = slot[...]


def place_slots(starts, slots):
    total = len(slots)
    shape = (total * slots[0].shape[0],) + slots[0].shape[1:]
    return pl.pallas_call(
        place_kernel,
        in_specs=[pl.BlockSpec(memory_space=pltpu.SMEM)]
        + [pl.BlockSpec(memory_space=pltpu.VMEM)] * total,
        out_specs=pl.BlockSpec(memory_space=pltpu.VMEM),
        out_shape=jax.ShapeDtypeStruct(shape, slots[0].dtype),
        compiler_params=pltpu.CompilerParams(vmem_limit_bytes=40 << 20),
        name="place_sequences",
    )(starts, *slots)


def shards(
    homolog_activations,
    coupling_activations,
    homolog_existence_marks,
    observed_peptide_marks,
    peptide_ordinals,
    strand_membership,
    distance_ordinal_vectors,
    coupling_score_mapping,
    question_mapping_weights,
    address_payload_mapping,
    logistic_valve_mapping,
    mixture_exit_mapping,
    twofold_covariance_mapping,
    covariance_exit_mapping,
    triad_opening_mappings,
    triad_valve_mapping,
    triad_exit_mapping,
):
    row_total = lax.axis_size("row")
    col_total = lax.axis_size("col")
    group_ratio = row_total // col_total
    devices = row_total * col_total
    row_place = lax.axis_index("row")
    col_place = lax.axis_index("col")
    tile_rows = coupling_activations.shape[0]
    block_columns = coupling_activations.shape[1]
    number_of_homologs = homolog_activations.shape[0]
    residues = row_total * tile_rows
    heads = coupling_score_mapping.shape[1]
    breadth = question_mapping_weights.shape[1]
    head_breadth = breadth // heads
    opm = twofold_covariance_mapping.shape[1] // 2
    tri_width = triad_exit_mapping.shape[0]
    pair_width = coupling_activations.shape[2]
    own_seqs = number_of_homologs // col_total
    share = tri_width // devices
    row_first = row_place * tile_rows
    col_first = col_place * block_columns
    bf16 = jnp.bfloat16

    marks = homolog_existence_marks.astype(jnp.float32)
    left, right = opm_operands(homolog_activations, marks, twofold_covariance_mapping)
    chips = range(0, row_total, 2)

    def over_chips(pieces):
        return [pieces[0]] + [
            lax.ppermute(piece, "row", [(i, i ^ k) for i in range(row_total)])
            for k, piece in zip(chips[1:], pieces[1:])
        ]

    def other_core(block):
        return lax.ppermute(block, "row", [(i, i ^ 1) for i in range(row_total)])

    left_z = collect(left, "col")
    left_stack = jnp.stack(left_z)
    right_even = jnp.concatenate(over_chips([right] * len(chips)), axis=0)
    right_odd = other_core(right_even)
    left_even = jnp.concatenate(
        over_chips(
            [
                lax.dynamic_index_in_dim(
                    left_stack, (row_place ^ k) // group_ratio ^ col_place, 0, keepdims=False
                )
                for k in chips
            ]
        ),
        axis=0,
    )
    left_odd = other_core(left_even)
    operands = [left_even, left_odd, right_even, right_odd]

    own_marks = lax.dynamic_slice_in_dim(left_stack[:, -1], col_place * own_seqs, own_seqs, 1)
    own_marks = jnp.swapaxes(own_marks[:, :, :block_columns], 0, 1).reshape(own_seqs, 1, residues)
    padded = -(-residues // 128) * 128
    own_marks = jnp.pad(own_marks.astype(jnp.float32), ((0, 0), (0, 0), (0, padded - residues)))

    lanes = 128
    spots = jnp.stack(
        [
            lax.dynamic_slice_in_dim(peptide_ordinals, row_first, tile_rows),
            lax.dynamic_slice_in_dim(strand_membership, row_first, tile_rows),
            jnp.full((tile_rows,), row_place % group_ratio * tile_rows, jnp.int32),
            jnp.full((tile_rows,), row_place % group_ratio, jnp.int32),
        ]
    )
    place = jnp.pad(
        jnp.stack(
            [
                lax.dynamic_slice_in_dim(peptide_ordinals, col_first, block_columns),
                lax.dynamic_slice_in_dim(strand_membership, col_first, block_columns),
            ]
        ),
        ((0, 6), (0, lanes - block_columns)),
    )
    exit_t = covariance_exit_mapping.reshape(opm, opm, pair_width).transpose(2, 1, 0)
    exit_t = exit_t.reshape(pair_width, opm * opm)
    near_t = jnp.pad(
        distance_ordinal_vectors, ((0, lanes - distance_ordinal_vectors.shape[0]), (0, 0))
    ).T
    open_t = triad_opening_mappings.reshape(
        pair_width, 2, 2, row_total // 2, 2, col_total, share
    )
    open_t = open_t.transpose(2, 4, 5, 3, 1, 6, 0)
    open_t = jnp.concatenate(
        [lax.dynamic_slice_in_dim(open_t, row_place % 2 ^ h, 1, 1) for h in range(2)], axis=1
    )
    open_t = jnp.concatenate(
        [lax.dynamic_slice_in_dim(open_t, col_place ^ m, 1, 2) for m in range(col_total)], axis=2
    )
    open_t = jnp.concatenate(
        [lax.dynamic_slice_in_dim(open_t, row_place // 2 ^ j, 1, 3) for j in range(row_total // 2)],
        axis=3,
    ).reshape(4 * tri_width, pair_width)
    score_t = coupling_score_mapping.T
    live_rows = lax.dynamic_slice_in_dim(observed_peptide_marks, row_first, tile_rows)
    live_cols = lax.dynamic_slice_in_dim(observed_peptide_marks, col_first, block_columns)
    live = (live_rows[:, None] * live_cols[None, :]).astype(jnp.float32).reshape(1, -1)
    operands, x_own = lax.optimization_barrier((operands, homolog_activations))
    x_slots = exchange(x_own.reshape(col_total, own_seqs, block_columns, -1), "col")
    z_one, ln_tri, *kept, given = pair_stage(
        operands[:2], operands[2:], coupling_activations, spots, place, exit_t, near_t, open_t,
        score_t, live, row_total, col_total,
    )

    given, x_slots = lax.optimization_barrier((given, x_slots))

    row_ids = row_place ^ jnp.arange(row_total, dtype=jnp.int32)
    col_ids = col_place ^ jnp.arange(col_total, dtype=jnp.int32)
    base = (row_ids // group_ratio ^ col_place) * block_columns + row_ids % group_ratio * tile_rows
    cols, spans = range(col_total), range(row_total // 2)
    count = 2 * share
    received = other_core(given)
    received = [received[m] for m in cols]
    kept = swap(kept, "col")
    kept, received = lax.optimization_barrier((kept, received))
    received = swap(received, "col")
    kept = regroup(
        kept,
        [
            [(m, j * count, count) for m in cols]
            + [(m, count * len(spans), heads) for m in cols]
            for j in spans
        ],
    )
    kept = over_chips(kept)
    kept, received = lax.optimization_barrier((kept, received))
    received = regroup(received, [[(m, j * count, count) for m in cols] for j in spans])
    received = over_chips(received)
    kept, received = lax.optimization_barrier((kept, received))
    (bias_even,) = regroup(kept, [[(j, count * col_total, heads * col_total) for j in spans]])
    bias_odd = other_core(bias_even)

    side_slots = [slot for both in zip(kept, received) for slot in both]
    *crossed, given = triangle(base, side_slots, share, col_total, residues)
    bias_even, bias_odd, given = lax.optimization_barrier((bias_even, bias_odd, given))
    bias_all = layout_bias(base, [bias_even, bias_odd], col_total, block_columns)
    received = other_core(given)
    crossed = regroup(
        list(crossed) + [received[m] for m in cols],
        [[(h * col_total + m, j, share) for h in range(2) for j in spans] for m in cols],
    )
    crossed = swap(crossed, "col")

    project = jnp.concatenate(
        [question_mapping_weights, address_payload_mapping, logistic_valve_mapping], axis=1
    )
    own_after = attend(bias_all, heads, x_slots, own_marks, project, mixture_exit_mapping)

    after_slots = swap(own_after, "col")
    crossed, _ = lax.optimization_barrier((crossed, own_after))
    half = share * len(spans)
    crossed = regroup(
        crossed, [[(m, h * half + j * share, share) for h in range(2) for m in cols] for j in spans]
    )
    crossed = over_chips(crossed)
    homologs_after = place_slots(col_ids * own_seqs, after_slots)
    exit_w = triad_exit_mapping.reshape(devices, share, pair_width)
    lead = (row_ids[:, None] * col_total + col_ids[None, :]).reshape(-1)
    couplings_after = finish(lead, crossed, ln_tri, z_one, triad_valve_mapping, exit_w)
    return (homologs_after, couplings_after.reshape(coupling_activations.shape))


def solution(mesh):
    placed = (
        P("row", "col", None),
        P("row", "col", None),
        P("row", "col"),
        P(),
        P(),
        P(),
        P(),
        P(),
        P(),
        P(),
        P(),
        P(),
        P(),
        P(),
        P(),
        P(),
        P(),
    )
    return jax.shard_map(
        shards,
        mesh=mesh,
        in_specs=placed,
        out_specs=(P("row", "col", None), P("row", "col", None)),
        check_vma=False,
    )
```

```python
import functools
import math

import jax
import jax.numpy as jnp
from jax import lax
from jax.experimental import pallas as pl
from jax.experimental.pallas import tpu as pltpu
from jax.sharding import PartitionSpec as P

REL_MAX = 32


norm_eps = 1e-05
count_eps = 0.001
masked_score = -1000000000.0


def swap(pieces, axis):
    total = len(pieces)
    return [pieces[0]] + [
        lax.ppermute(pieces[k], axis, [(i, i ^ k) for i in range(total)]) for k in range(1, total)
    ]


def collect(block, axis):
    return swap([block] * lax.axis_size(axis), axis)


def exchange(pieces, axis):
    me = lax.axis_index(axis)
    total = lax.axis_size(axis)
    return swap(
        [lax.dynamic_index_in_dim(pieces, me ^ k, 0, keepdims=False) for k in range(total)], axis
    )


def in_order(slots, axis):
    me = lax.axis_index(axis)
    stacked = jnp.stack(slots)
    return jnp.stack(
        [
            lax.dynamic_index_in_dim(stacked, me ^ k, 0, keepdims=False)
            for k in range(len(slots))
        ]
    )


def zscore_transform(inputs):
    inputs = inputs.astype(jnp.float32)
    centred = inputs - jnp.mean(inputs, axis=-1, keepdims=True)
    spread = jnp.mean(centred * centred, axis=-1, keepdims=True)
    return centred * lax.rsqrt(spread + norm_eps)


def regrouped_covariance(operand, weights):
    batch_shape = operand.shape[:-1]
    result = jnp.dot(
        operand.reshape(-1, operand.shape[-1]), weights, preferred_element_type=jnp.float32
    )
    return result.reshape(batch_shape + (weights.shape[-1],))


def position_bins(index_rows, index_cols, chain_rows, chain_cols):
    offset = jnp.clip(index_rows[:, None] - index_cols[None, :] + REL_MAX, 0, 2 * REL_MAX)
    return jnp.where(chain_rows[:, None] == chain_cols[None, :], offset, 2 * REL_MAX + 1)


def operand_kernel(x_ref, marks_ref, spread_ref, wl_ref, wr_ref, left_ref, right_ref, ln, side, acc):
    seqs, places, width = x_ref.shape
    groups = left_ref.shape[0] - 1
    rights = right_ref.shape[0] - 1
    lanes = left_ref.shape[2]
    per = places // groups
    for s in range(seqs):
        own = zscore_transform(x_ref[s])
        for h in range(width // 128):
            ln[h, s * places : (s + 1) * places, :] = own[:, h * 128 : (h + 1) * 128]
    marks = marks_ref[...]
    for s in range(seqs):
        own = jnp.concatenate(
            [ln[h, s * places : (s + 1) * places, :] for h in range(width // 128)], axis=1
        )
        got = lax.dot_general(
            wr_ref[...], own.astype(jnp.bfloat16), (((1,), (1,)), ((), ())),
            preferred_element_type=jnp.float32,
        )
        got = got * marks[s : s + 1, :]
        side[pl.ds(s, rights, stride=seqs), :] = jnp.concatenate(
            [got, jnp.zeros((rights, lanes - places), jnp.float32)], axis=1
        )
    right_ref[:rights] = side[...].reshape(rights, seqs, lanes).astype(jnp.bfloat16)
    for q in range(per):
        for g in range(groups):
            for h in range(width // 128):
                acc[g * seqs : (g + 1) * seqs, h * 128 : (h + 1) * 128] = ln[
                    h, pl.ds(g * per + q, seqs, stride=places), :
                ]
        part = jnp.dot(
            acc[...].astype(jnp.bfloat16), wl_ref[q], preferred_element_type=jnp.float32
        )
        total = part if q == 0 else total + part
    spread = jnp.dot(
        marks.astype(jnp.bfloat16), spread_ref[...], preferred_element_type=jnp.float32
    )
    for g in range(groups):
        left_ref[g] = (
            total[g * seqs : (g + 1) * seqs] * spread[:, g * lanes : (g + 1) * lanes]
        ).astype(jnp.bfloat16)
    block = jnp.zeros((seqs, lanes), jnp.float32)
    side[:seqs, :] = block
    side[:seqs, :places] = marks
    left_ref[groups] = side[:seqs, :].astype(jnp.bfloat16)
    right_ref[rights] = side[:seqs, :].astype(jnp.bfloat16)


def opm_operands(x, marks, mapping):
    seqs, places, width = x.shape
    opm = mapping.shape[1] // 2
    lanes = 128
    per = lanes // opm
    groups = places // per
    wl = jnp.stack(
        [
            jnp.pad(mapping[:, :opm], ((0, 0), (q * opm, lanes - (q + 1) * opm)))
            for q in range(per)
        ]
    )
    wr = mapping[:, opm:].T
    spread = jnp.repeat(jnp.eye(places, dtype=jnp.bfloat16), opm, axis=1)
    return pl.pallas_call(
        operand_kernel,
        out_shape=(
            jax.ShapeDtypeStruct((groups + 1, seqs, lanes), jnp.bfloat16),
            jax.ShapeDtypeStruct((opm + 1, seqs, lanes), jnp.bfloat16),
        ),
        scratch_shapes=[
            pltpu.VMEM((width // 128, seqs * places, 128), jnp.float32),
            pltpu.VMEM((opm * seqs, lanes), jnp.float32),
            pltpu.VMEM((groups * seqs, width), jnp.float32),
        ],
        compiler_params=pltpu.CompilerParams(vmem_limit_bytes=40 << 20),
        name="outer_operands",
    )(x, marks, spread, wl, wr)


def pair_kernel(total_rows, total_cols, *refs):
    spots = refs[0]
    rows_in = refs[1:3]
    cols_in = refs[3:5]
    pair_ref, place_ref, exit_ref, near_ref, open_ref, score_ref, live_ref = refs[5:12]
    outs = refs[12:]
    z_ref, high_ref = outs[:2]
    side_refs = outs[2 : 2 + total_cols]
    given_ref = outs[2 + total_cols]
    left, right, prod, counts, low = outs[3 + total_cols :]
    step = pl.program_id(0)
    group, places, width = pair_ref.shape
    seqs = rows_in[0].shape[1]
    lanes = 128
    chips = total_rows // 2
    opm = cols_in[0].shape[0] // chips - 1
    sent = rows_in[0].shape[0] // chips
    blocks = left.shape[0]
    bf16 = jnp.bfloat16

    @pl.when(step == 0)
    def _():
        mark_rows, mark_cols = [], []
        for k in range(total_rows):
            half, chip = k % 2, k // 2
            for g in range(blocks):
                left[g, k * seqs : (k + 1) * seqs, :] = rows_in[half][
                    chip * sent + spots[3, 0] * blocks + g
                ]
            for e in range(opm):
                right[k * seqs : (k + 1) * seqs, e * lanes : (e + 1) * lanes] = cols_in[half][
                    chip * (opm + 1) + e
                ]
            mark_rows.append(rows_in[half][chip * sent + sent - 1])
            mark_cols.append(cols_in[half][chip * (opm + 1) + opm])
        mark_rows = jnp.concatenate(mark_rows, axis=0)
        mark_cols = jnp.concatenate(mark_cols, axis=0)
        counts[...] = lax.dot_general(
            mark_rows, mark_cols, (((0,), (0,)), ((), ())), preferred_element_type=jnp.float32
        )

    grid_left = left[step]
    half = opm // 2
    for part in range(2):
        got = lax.dot_general(
            grid_left, right[:, part * half * lanes : (part + 1) * half * lanes],
            (((0,), (0,)), ((), ())), preferred_element_type=jnp.float32,
        ).astype(bf16)
        for e in range(half):
            for i in range(group):
                prod[
                    (part * half + e) * opm : (part * half + e + 1) * opm,
                    i * lanes : (i + 1) * lanes,
                ] = got[i * opm : (i + 1) * opm, e * lanes : (e + 1) * lanes]
    mixed = jnp.dot(exit_ref[...], prod[...], preferred_element_type=jnp.float32)
    pos_cols = place_ref[0:1, :]
    chain_cols = place_ref[1:2, :]
    bins, amount = [], []
    for i in range(group):
        here = step * group + i
        offset = jnp.clip(spots[0, here] - pos_cols + REL_MAX, 0, 2 * REL_MAX)
        bins.append(jnp.where(chain_cols == spots[1, here], offset, 2 * REL_MAX + 1))
        amount.append(counts[pl.ds(spots[2, 0] + here, 1), :])
    bins = jnp.concatenate(bins, axis=1)
    amount = jnp.concatenate(amount, axis=1)
    one_hot = (
        lax.broadcasted_iota(jnp.int32, (near_ref.shape[1], group * lanes), 0) == bins
    )
    one_hot = jnp.where(one_hot, 1.0, 0.0).astype(bf16)
    near = jnp.dot(near_ref[...], one_hot, preferred_element_type=jnp.float32)
    update = jnp.transpose(mixed / (count_eps + amount) + near)
    z = jnp.concatenate(
        [
            pair_ref[i].astype(jnp.float32) + update[i * lanes : i * lanes + places]
            for i in range(group)
        ],
        axis=0,
    )
    z_ref[...] = z
    ln = zscore_transform(z)
    high = ln.astype(bf16)
    start = pl.multiple_of(step * (group * places), 16)
    high_ref[pl.ds(start, group * places), :] = high
    low[pl.ds(start, group * places), :] = (ln - high.astype(jnp.float32)).astype(bf16)

    @pl.when(step == pl.num_programs(0) - 1)
    def _():
        pairs = high_ref.shape[0]
        chunk = 512
        transposed = (((1,), (1,)), ((), ()))
        half_rows = open_ref.shape[0] // 2
        each = half_rows // total_cols // 2
        for first in range(0, pairs, chunk):
            last = min(first + chunk, pairs)
            ours = high_ref[first:last, :]
            bias = lax.dot_general(
                score_ref[...], ours, transposed, preferred_element_type=jnp.float32
            ) + lax.dot_general(
                score_ref[...], low[first:last, :], transposed, preferred_element_type=jnp.float32
            )
            opened = lax.dot_general(
                open_ref[...], ours, transposed, preferred_element_type=jnp.float32
            )
            sides = (
                jax.nn.sigmoid(opened[half_rows:]) * opened[:half_rows] * live_ref[:, first:last]
            )
            for m in range(total_cols):
                at = m * each
                side_refs[m][:, first:last] = jnp.concatenate(
                    [sides[at : at + each], bias], axis=0
                ).astype(bf16)
                at = (total_cols + m) * each
                given_ref[m, :, first:last] = sides[at : at + each].astype(bf16)


def pair_stage(rows_in, cols_in, pair, spots, place, exit_t, near_t, open_t, score_t, live, total_rows, total_cols):
    tile_rows, places, width = pair.shape
    sent, seqs, lanes = rows_in[0].shape
    chips = total_rows // 2
    blocks = (sent // chips - 1) // 2
    group = tile_rows // blocks
    opm = cols_in[0].shape[0] // chips - 1
    pairs = tile_rows * places
    each = open_t.shape[0] // 4 // total_cols
    every = total_rows * seqs

    def whole(a):
        return pl.BlockSpec(a.shape, lambda g, n=a.ndim: (0,) * n)

    def whole_out(shape):
        return pl.BlockSpec(shape, lambda g, n=len(shape): (0,) * n)

    ins = list(rows_in) + list(cols_in)
    rest = [place, exit_t, near_t, open_t, score_t, live]
    bf16 = jnp.bfloat16
    outs = [
        jax.ShapeDtypeStruct((pairs, width), jnp.float32),
        jax.ShapeDtypeStruct((pairs, width), bf16),
    ] + [jax.ShapeDtypeStruct((each + score_t.shape[0], pairs), bf16)] * total_cols
    outs.append(jax.ShapeDtypeStruct((total_cols, each, pairs), bf16))
    return pl.pallas_call(
        functools.partial(pair_kernel, total_rows, total_cols),
        grid=(blocks,),
        in_specs=[pl.BlockSpec(memory_space=pltpu.SMEM)]
        + [whole(a) for a in ins]
        + [pl.BlockSpec((group, places, width), lambda g: (g, 0, 0))]
        + [whole(a) for a in rest],
        out_specs=[pl.BlockSpec((group * places, width), lambda g: (g, 0))]
        + [whole_out(o.shape) for o in outs[1:]],
        out_shape=outs,
        scratch_shapes=[
            pltpu.VMEM((blocks, every, lanes), bf16),
            pltpu.VMEM((every, opm * lanes), bf16),
            pltpu.VMEM((opm * opm, group * lanes), bf16),
            pltpu.VMEM((lanes, lanes), jnp.float32),
            pltpu.VMEM((pairs, width), bf16),
        ],
        compiler_params=pltpu.CompilerParams(
            vmem_limit_bytes=56 << 20, dimension_semantics=("arbitrary",)
        ),
        name="pair_update",
    )(spots, *ins, pair, *rest)


def spread_slots(slots, stack, base_ref, tiles, total_cols, places):
    total, high, wide = stack.shape
    pairs = slots[0].shape[1]
    count = high // total_cols
    rows = pairs // places
    residues = rows * total
    pitch = tiles.shape[1] // count
    lane = lax.broadcasted_iota(jnp.int32, (count, 128), 1)
    for k in range(total):
        slot, at = k % len(slots), k // len(slots) * high
        stack[k, :, :pairs] = slots[slot][at : at + high]

    def one(k, carry):
        base = base_ref[k]
        for i in range(rows):
            first = i * places // 128 * 128
            off = i * places - first
            window = stack[k, :, first : first + 256].astype(jnp.float32)
            made = [None] * tiles.shape[0]
            for c in range(total_cols):
                to, at = divmod(c * places, 128)
                piece = window[c * count : (c + 1) * count]
                if at != off:
                    piece = pltpu.roll(piece, (at - off) % 256, 1)
                begin = piece[:, :128]
                made[to] = begin if made[to] is None else jnp.where(lane >= at, begin, made[to])
                if at + places > 128:
                    made[to + 1] = piece[:, 128:]
            kept = residues - 128 * (len(made) - 1)
            made[-1] = jnp.where(lane < kept, made[-1], 0.0)
            for t, tile in enumerate(made):
                tiles[t, pl.ds(base + i, count, stride=pitch), :] = tile
        return carry

    lax.fori_loop(0, total, one, 0)


def layout_kernel(halves, total_cols, places, *refs):
    base_ref = refs[0]
    out_ref, stack, tiles = refs[1 + halves :]
    spread_slots(refs[1 : 1 + halves], stack, base_ref, tiles, total_cols, places)
    residues = places * total_cols
    heads = out_ref.shape[1] // residues
    pitch = tiles.shape[1] // heads
    for h in range(heads):
        out_ref[:, h * residues : (h + 1) * residues, :] = tiles[
            :, h * pitch : h * pitch + residues, :
        ].astype(out_ref.dtype)


def layout_bias(base, bias_slots, total_cols, places):
    total_rows = base.shape[0]
    rows, pairs = bias_slots[0].shape
    rows = rows * len(bias_slots) // total_rows
    residues = places * total_cols
    heads = rows // total_cols
    shape = (-(-residues // 128), heads * residues, 128)
    wide = -(-pairs // 128) * 128 + 128
    return pl.pallas_call(
        functools.partial(layout_kernel, len(bias_slots), total_cols, places),
        in_specs=[pl.BlockSpec(memory_space=pltpu.SMEM)]
        + [pl.BlockSpec(memory_space=pltpu.VMEM)] * len(bias_slots),
        out_specs=pl.BlockSpec(memory_space=pltpu.VMEM),
        out_shape=jax.ShapeDtypeStruct(shape, jnp.bfloat16),
        scratch_shapes=[
            pltpu.VMEM((total_rows, rows, wide), jnp.bfloat16),
            pltpu.VMEM((shape[0], heads * (residues + 8), 128), jnp.float32),
        ],
        compiler_params=pltpu.CompilerParams(vmem_limit_bytes=48 << 20),
        name="layout_bias",
    )(base, *bias_slots)


def attention_kernel(total_cols, heads, *refs):
    bias_ref = refs[0]
    x_in = refs[1 : 1 + total_cols]
    mark_ref, project_ref, mix_ref = refs[1 + total_cols : 4 + total_cols]
    outs = refs[4 + total_cols : 4 + 2 * total_cols]
    scored, termed, summed, mixed = refs[4 + 2 * total_cols :]
    places, width = x_in[0].shape[1:]
    residues = places * total_cols
    each = width // heads
    group = 128 // each
    padded = bias_ref.shape[0] * 128
    bf16 = jnp.bfloat16
    transposed = (((1,), (1,)), ((), ()))
    chunk = 32

    x = jnp.concatenate([r[0].astype(jnp.float32) for r in x_in], axis=0)
    made = jnp.dot(
        zscore_transform(x).astype(bf16), project_ref[...], preferred_element_type=jnp.float32
    )
    present = mark_ref[0] > 0.0
    lane = lax.broadcasted_iota(jnp.int32, (1, 128), 1)
    scale = 1.0 / math.sqrt(each)
    filler = jnp.zeros((padded - residues, 128), bf16)

    def head_columns(part, h):
        at = part * width + h // group * 128
        return made[:, at : at + 128].astype(bf16)

    def only(block, h):
        inside = (lane >= h % group * each) & (lane < (h % group + 1) * each)
        return jnp.concatenate([jnp.where(inside, block, jnp.zeros_like(block)), filler], axis=0)

    def score(h):
        scored[h % 2] = lax.dot_general(
            head_columns(0, h), only(head_columns(1, h), h), transposed,
            preferred_element_type=jnp.float32,
        )

    score(0)
    for h in range(heads):
        if h + 1 < heads:
            score(h + 1)
        for first in range(0, residues, chunk):
            start = h * residues + first
            bias = jnp.concatenate(
                [bias_ref[t, start : start + chunk, :] for t in range(bias_ref.shape[0])], axis=1
            )
            scores = scored[h % 2, first : first + chunk, :] * scale + bias.astype(jnp.float32)
            scores = jnp.where(present, scores, masked_score)
            terms = jnp.exp(scores - jnp.max(scores, axis=1, keepdims=True))
            weight = jnp.sum(terms, axis=1, keepdims=True)
            termed[h % 2, first : first + chunk, :] = terms.astype(bf16)
            summed[h % 2, first : first + chunk, :] = jnp.broadcast_to(1.0 / weight, (chunk, 128))
        got = jnp.dot(
            termed[h % 2], only(head_columns(2, h), h), preferred_element_type=jnp.float32
        ) * summed[h % 2]
        total = got if h % group == 0 else total + got
        if h % group == group - 1:
            at = h // group * 128
            gate = jax.nn.sigmoid(made[:, 3 * width + at : 3 * width + at + 128])
            mixed[:, at : at + 128] = (gate * total).astype(bf16)
    after = x + jnp.dot(mixed[...], mix_ref[...], preferred_element_type=jnp.float32)
    for m in range(total_cols):
        outs[m][0] = after[m * places : (m + 1) * places].astype(bf16)


def attend(bias, heads, x_slots, marks, project, mix):
    total_cols = len(x_slots)
    seqs, places, width = x_slots[0].shape
    residues = places * total_cols
    padded = bias.shape[0] * 128

    def whole(a):
        return pl.BlockSpec(a.shape, lambda s, n=a.ndim: (0,) * n)

    per_seq = pl.BlockSpec((1, places, width), lambda s: (s, 0, 0))
    bf16 = jnp.bfloat16
    return pl.pallas_call(
        functools.partial(attention_kernel, total_cols, heads),
        grid=(seqs,),
        in_specs=[whole(bias)]
        + [per_seq] * total_cols
        + [pl.BlockSpec((1, 1, padded), lambda s: (s, 0, 0)), whole(project), whole(mix)],
        out_specs=[per_seq] * total_cols,
        out_shape=[jax.ShapeDtypeStruct((seqs, places, width), bf16)] * total_cols,
        scratch_shapes=[
            pltpu.VMEM((2, residues, padded), jnp.float32),
            pltpu.VMEM((2, residues, padded), bf16),
            pltpu.VMEM((2, residues, 128), jnp.float32),
            pltpu.VMEM((residues, width), bf16),
        ],
        compiler_params=pltpu.CompilerParams(
            vmem_limit_bytes=48 << 20, dimension_semantics=("arbitrary",)
        ),
        name="row_attention",
    )(bias, *x_slots, marks, project, mix)


def regroup_kernel(plan, total_in, *refs):
    for out, parts in zip(refs[total_in:], plan):
        rows = [
            refs[n][at] if refs[n].ndim == 3 else refs[n][at : at + count]
            for n, at, count in parts
        ]
        out[...] = jnp.concatenate([r.astype(jnp.float32) for r in rows], axis=0).astype(out.dtype)


def regroup(blocks, plan):
    pairs = blocks[0].shape[-1]
    return pl.pallas_call(
        functools.partial(regroup_kernel, plan, len(blocks)),
        in_specs=[pl.BlockSpec(memory_space=pltpu.VMEM)] * len(blocks),
        out_specs=[pl.BlockSpec(memory_space=pltpu.VMEM)] * len(plan),
        out_shape=[
            jax.ShapeDtypeStruct((sum(count for _, _, count in parts), pairs), jnp.bfloat16)
            for parts in plan
        ],
        compiler_params=pltpu.CompilerParams(vmem_limit_bytes=40 << 20),
        name="regroup",
    )(*blocks)


def stack_kernel(*refs):
    count = refs[0].shape[0]
    for n, ref in enumerate(refs[:-1]):
        refs[-1][n * count : (n + 1) * count] = ref[...]


def stack_blocks(blocks):
    shape = (len(blocks) * blocks[0].shape[0],) + blocks[0].shape[1:]
    return pl.pallas_call(
        stack_kernel,
        out_shape=jax.ShapeDtypeStruct(shape, blocks[0].dtype),
        compiler_params=pltpu.CompilerParams(vmem_limit_bytes=40 << 20),
        name="stack_blocks",
    )(*blocks)


def triangle_kernel(total_rows, total_cols, residues, *refs):
    base_ref = refs[0]
    slots = refs[1 : 1 + total_rows]
    kept = refs[1 + total_rows : 1 + total_rows + total_cols]
    given, stack, tiles, crossed = refs[1 + total_rows + total_cols :]
    pairs = kept[0].shape[2]
    share = kept[0].shape[1]
    pitch = tiles.shape[1] // (2 * share)
    rows = residues // total_rows
    places = residues // total_cols
    bf16 = jnp.bfloat16
    spread_slots(slots, stack, base_ref, tiles, total_cols, places)
    for c in range(share):
        sides = []
        for side in range(2):
            start = (side * share + c) * pitch
            sides.append(
                jnp.concatenate(
                    [tiles[t, start : start + residues, :] for t in range(tiles.shape[0])], axis=1
                ).astype(bf16)
            )
        got = lax.dot_general(
            sides[0], sides[1], (((1,), (1,)), ((), ())), preferred_element_type=jnp.float32
        )
        for t in range(tiles.shape[0]):
            last = min(128, residues - t * 128)
            crossed[t, c * pitch : c * pitch + residues, :last] = got[:, t * 128 : t * 128 + last]
    lane = lax.broadcasted_iota(jnp.int32, (share, 128), 1)

    def one(j, carry):
        for h in range(2):
            outs = [given.at[m] if h else kept[m] for m in range(total_cols)]
            rows_out(j, base_ref[2 * j + h], outs)
        return carry

    def rows_out(k, base, outs):
        made = [dict() for _ in range(total_cols)]
        for i in range(rows):
            row = [
                crossed[t, pl.ds(base + i, share, stride=pitch), :]
                for t in range(tiles.shape[0])
            ]
            for m in range(total_cols):
                come, off = divmod(m * places, 128)
                after = row[come + 1] if come + 1 < len(row) else row[come]
                piece = jnp.concatenate([row[come], after], axis=1)
                to, at = divmod(i * places, 128)
                if at != off:
                    piece = pltpu.roll(piece, (at - off) % 256, 1)
                begin = piece[:, :128]
                if to in made[m]:
                    begin = jnp.where(lane >= at, begin, made[m][to])
                made[m][to] = begin
                if at + places > 128:
                    made[m][to + 1] = piece[:, 128:]
                if at + places >= 128 or i == rows - 1:
                    size = min(128, pairs - to * 128)
                    outs[m][k, :, to * 128 : to * 128 + size] = made[m].pop(to)[:, :size].astype(bf16)
                    if i == rows - 1 and to + 1 in made[m]:
                        size = pairs - (to + 1) * 128
                        outs[m][k, :, (to + 1) * 128 : pairs] = made[m].pop(to + 1)[:, :size].astype(bf16)

    lax.fori_loop(0, total_rows // 2, one, 0)


def triangle(base, slots, share, total_cols, residues):
    total_rows = len(slots)
    rows, pairs = slots[1].shape
    padded = -(-residues // 128)
    wide = -(-pairs // 128) * 128 + 128
    bf16 = jnp.bfloat16
    return pl.pallas_call(
        functools.partial(triangle_kernel, total_rows, total_cols, residues),
        in_specs=[pl.BlockSpec(memory_space=pltpu.SMEM)]
        + [pl.BlockSpec(memory_space=pltpu.VMEM)] * total_rows,
        out_specs=[pl.BlockSpec(memory_space=pltpu.VMEM)] * (total_cols + 1),
        out_shape=[jax.ShapeDtypeStruct((total_rows // 2, share, pairs), bf16)] * total_cols
        + [jax.ShapeDtypeStruct((total_cols, total_rows // 2, share, pairs), bf16)],
        scratch_shapes=[
            pltpu.VMEM((total_rows, rows, wide), bf16),
            pltpu.VMEM((padded, 2 * share * (residues + 8), 128), jnp.float32),
            pltpu.VMEM((padded, max(share, 8) * (residues + 8), 128), jnp.float32),
        ],
        compiler_params=pltpu.CompilerParams(vmem_limit_bytes=56 << 20),
        name="triangle",
    )(base, *slots)


def finish_kernel(total_rows, *refs):
    lead_ref = refs[0]
    chips = total_rows // 2
    high_ref, z_ref, valve_ref, exit_ref, out_ref = refs[1 + chips :]
    count = refs[1].shape[0] // 2
    slots = [refs[1 + k // 2].at[k % 2 * count : (k % 2 + 1) * count] for k in range(total_rows)]
    pairs = out_ref.shape[0]
    chunk = 512
    exits = jnp.concatenate(
        [exit_ref[lead_ref[n]].astype(jnp.float32) for n in range(exit_ref.shape[0])], axis=0
    ).astype(jnp.bfloat16)
    for first in range(0, pairs, chunk):
        last = min(first + chunk, pairs)
        crossed = jnp.concatenate(
            [s[:, first:last].astype(jnp.float32) for s in slots], axis=0
        )
        centred = crossed - jnp.mean(crossed, axis=0, keepdims=True)
        spread = jnp.mean(centred * centred, axis=0, keepdims=True)
        normed = (centred * lax.rsqrt(spread + norm_eps)).astype(jnp.bfloat16)
        projected = lax.dot_general(
            normed, exits, (((0,), (0,)), ((), ())), preferred_element_type=jnp.float32
        )
        gate = jax.nn.sigmoid(
            jnp.dot(high_ref[first:last, :], valve_ref[...], preferred_element_type=jnp.float32)
        )
        out_ref[first:last, :] = (z_ref[first:last, :] + gate * projected).astype(jnp.bfloat16)


def finish(lead, slots, high, z_one, valve, exit_w):
    return pl.pallas_call(
        functools.partial(finish_kernel, 2 * len(slots)),
        in_specs=[pl.BlockSpec(memory_space=pltpu.SMEM)]
        + [pl.BlockSpec(memory_space=pltpu.VMEM)] * (len(slots) + 4),
        out_specs=pl.BlockSpec(memory_space=pltpu.VMEM),
        out_shape=jax.ShapeDtypeStruct(high.shape, jnp.bfloat16),
        compiler_params=pltpu.CompilerParams(vmem_limit_bytes=40 << 20),
        name="pair_finish",
    )(lead, *slots, high, z_one, valve, exit_w)


def place_kernel(start_ref, *refs):
    out = refs[-1]
    for m, slot in enumerate(refs[:-1]):
        out[pl.ds(start_ref[m], slot.shape[0])] = slot[...]


def place_slots(starts, slots):
    total = len(slots)
    shape = (total * slots[0].shape[0],) + slots[0].shape[1:]
    return pl.pallas_call(
        place_kernel,
        in_specs=[pl.BlockSpec(memory_space=pltpu.SMEM)]
        + [pl.BlockSpec(memory_space=pltpu.VMEM)] * total,
        out_specs=pl.BlockSpec(memory_space=pltpu.VMEM),
        out_shape=jax.ShapeDtypeStruct(shape, slots[0].dtype),
        compiler_params=pltpu.CompilerParams(vmem_limit_bytes=40 << 20),
        name="place_sequences",
    )(starts, *slots)


def shards(
    homolog_activations,
    coupling_activations,
    homolog_existence_marks,
    observed_peptide_marks,
    peptide_ordinals,
    strand_membership,
    distance_ordinal_vectors,
    coupling_score_mapping,
    question_mapping_weights,
    address_payload_mapping,
    logistic_valve_mapping,
    mixture_exit_mapping,
    twofold_covariance_mapping,
    covariance_exit_mapping,
    triad_opening_mappings,
    triad_valve_mapping,
    triad_exit_mapping,
):
    row_total = lax.axis_size("row")
    col_total = lax.axis_size("col")
    group_ratio = row_total // col_total
    devices = row_total * col_total
    row_place = lax.axis_index("row")
    col_place = lax.axis_index("col")
    tile_rows = coupling_activations.shape[0]
    block_columns = coupling_activations.shape[1]
    number_of_homologs = homolog_activations.shape[0]
    residues = row_total * tile_rows
    heads = coupling_score_mapping.shape[1]
    breadth = question_mapping_weights.shape[1]
    head_breadth = breadth // heads
    opm = twofold_covariance_mapping.shape[1] // 2
    tri_width = triad_exit_mapping.shape[0]
    pair_width = coupling_activations.shape[2]
    own_seqs = number_of_homologs // col_total
    share = tri_width // devices
    row_first = row_place * tile_rows
    col_first = col_place * block_columns
    bf16 = jnp.bfloat16

    marks = homolog_existence_marks.astype(jnp.float32)
    left, right = opm_operands(homolog_activations, marks, twofold_covariance_mapping)
    chips = range(0, row_total, 2)

    def over_chips(pieces):
        return [pieces[0]] + [
            lax.ppermute(piece, "row", [(i, i ^ k) for i in range(row_total)])
            for k, piece in zip(chips[1:], pieces[1:])
        ]

    def other_core(block):
        return lax.ppermute(block, "row", [(i, i ^ 1) for i in range(row_total)])

    left_z = collect(left, "col")
    left_stack = jnp.stack(left_z)
    right_even = jnp.concatenate(over_chips([right] * len(chips)), axis=0)
    right_odd = other_core(right_even)
    left_even = jnp.concatenate(
        over_chips(
            [
                lax.dynamic_index_in_dim(
                    left_stack, (row_place ^ k) // group_ratio ^ col_place, 0, keepdims=False
                )
                for k in chips
            ]
        ),
        axis=0,
    )
    left_odd = other_core(left_even)
    operands = [left_even, left_odd, right_even, right_odd]

    own_marks = lax.dynamic_slice_in_dim(left_stack[:, -1], col_place * own_seqs, own_seqs, 1)
    own_marks = jnp.swapaxes(own_marks[:, :, :block_columns], 0, 1).reshape(own_seqs, 1, residues)
    padded = -(-residues // 128) * 128
    own_marks = jnp.pad(own_marks.astype(jnp.float32), ((0, 0), (0, 0), (0, padded - residues)))

    lanes = 128
    spots = jnp.stack(
        [
            lax.dynamic_slice_in_dim(peptide_ordinals, row_first, tile_rows),
            lax.dynamic_slice_in_dim(strand_membership, row_first, tile_rows),
            jnp.full((tile_rows,), row_place % group_ratio * tile_rows, jnp.int32),
            jnp.full((tile_rows,), row_place % group_ratio, jnp.int32),
        ]
    )
    place = jnp.pad(
        jnp.stack(
            [
                lax.dynamic_slice_in_dim(peptide_ordinals, col_first, block_columns),
                lax.dynamic_slice_in_dim(strand_membership, col_first, block_columns),
            ]
        ),
        ((0, 6), (0, lanes - block_columns)),
    )
    exit_t = covariance_exit_mapping.reshape(opm, opm, pair_width).transpose(2, 1, 0)
    exit_t = exit_t.reshape(pair_width, opm * opm)
    near_t = jnp.pad(
        distance_ordinal_vectors, ((0, lanes - distance_ordinal_vectors.shape[0]), (0, 0))
    ).T
    open_t = triad_opening_mappings.reshape(
        pair_width, 2, 2, row_total // 2, 2, col_total, share
    )
    open_t = open_t.transpose(2, 4, 5, 3, 1, 6, 0)
    open_t = jnp.concatenate(
        [lax.dynamic_slice_in_dim(open_t, row_place % 2 ^ h, 1, 1) for h in range(2)], axis=1
    )
    open_t = jnp.concatenate(
        [lax.dynamic_slice_in_dim(open_t, col_place ^ m, 1, 2) for m in range(col_total)], axis=2
    )
    open_t = jnp.concatenate(
        [lax.dynamic_slice_in_dim(open_t, row_place // 2 ^ j, 1, 3) for j in range(row_total // 2)],
        axis=3,
    ).reshape(4 * tri_width, pair_width)
    score_t = coupling_score_mapping.T
    live_rows = lax.dynamic_slice_in_dim(observed_peptide_marks, row_first, tile_rows)
    live_cols = lax.dynamic_slice_in_dim(observed_peptide_marks, col_first, block_columns)
    live = (live_rows[:, None] * live_cols[None, :]).astype(jnp.float32).reshape(1, -1)
    operands, x_own = lax.optimization_barrier((operands, homolog_activations))
    x_slots = exchange(x_own.reshape(col_total, own_seqs, block_columns, -1), "col")
    z_one, ln_tri, *kept, given = pair_stage(
        operands[:2], operands[2:], coupling_activations, spots, place, exit_t, near_t, open_t,
        score_t, live, row_total, col_total,
    )

    given, x_slots = lax.optimization_barrier((given, x_slots))

    row_ids = row_place ^ jnp.arange(row_total, dtype=jnp.int32)
    col_ids = col_place ^ jnp.arange(col_total, dtype=jnp.int32)
    base = (row_ids // group_ratio ^ col_place) * block_columns + row_ids % group_ratio * tile_rows
    cols, spans = range(col_total), range(row_total // 2)
    count = 2 * share
    received = other_core(given)
    received = [received[m] for m in cols]
    kept = swap(kept, "col")
    kept, received = lax.optimization_barrier((kept, received))
    received = swap(received, "col")
    kept = regroup(
        kept,
        [
            [(m, j * count, count) for m in cols]
            + [(m, count * len(spans), heads) for m in cols]
            for j in spans
        ],
    )
    kept = over_chips(kept)
    kept, received = lax.optimization_barrier((kept, received))
    received = regroup(received, [[(m, j * count, count) for m in cols] for j in spans])
    received = over_chips(received)
    kept, received = lax.optimization_barrier((kept, received))
    (bias_even,) = regroup(kept, [[(j, count * col_total, heads * col_total) for j in spans]])
    bias_odd = other_core(bias_even)

    side_slots = [slot for both in zip(kept, received) for slot in both]
    *crossed, given = triangle(base, side_slots, share, col_total, residues)
    bias_even, bias_odd, given = lax.optimization_barrier((bias_even, bias_odd, given))
    bias_all = layout_bias(base, [bias_even, bias_odd], col_total, block_columns)
    received = other_core(given)
    crossed = regroup(
        list(crossed) + [received[m] for m in cols],
        [[(h * col_total + m, j, share) for h in range(2) for j in spans] for m in cols],
    )
    crossed = swap(crossed, "col")

    project = jnp.concatenate(
        [question_mapping_weights, address_payload_mapping, logistic_valve_mapping], axis=1
    )
    own_after = attend(bias_all, heads, x_slots, own_marks, project, mixture_exit_mapping)

    after_slots = swap(own_after, "col")
    crossed, _ = lax.optimization_barrier((crossed, own_after))
    half = share * len(spans)
    crossed = regroup(
        crossed, [[(m, h * half + j * share, share) for h in range(2) for m in cols] for j in spans]
    )
    crossed = over_chips(crossed)
    homologs_after = place_slots(col_ids * own_seqs, after_slots)
    exit_w = triad_exit_mapping.reshape(devices, share, pair_width)
    lead = (row_ids[:, None] * col_total + col_ids[None, :]).reshape(-1)
    couplings_after = finish(lead, crossed, ln_tri, z_one, triad_valve_mapping, exit_w)
    return (homologs_after, couplings_after.reshape(coupling_activations.shape))


def solution(mesh):
    placed = (
        P("row", "col", None),
        P("row", "col", None),
        P("row", "col"),
        P(),
        P(),
        P(),
        P(),
        P(),
        P(),
        P(),
        P(),
        P(),
        P(),
        P(),
        P(),
        P(),
        P(),
    )
    return jax.shard_map(
        shards,
        mesh=mesh,
        in_specs=placed,
        out_specs=(P("row", "col", None), P("row", "col", None)),
        check_vma=False,
    )
```
